32 devices in a mesh: frames: 16 (over z, y, core), patch: 2 (over x).
Axes of the slice: x: 2, y: 2, z: 4, core: 2. Of those that a mesh axis runs over, the one named last changes fastest.
Arguments:
- tokens: bfloat16 [16, 1024, 1152], P('frames', 'patch'), may hold values from -6 to 6
- cotangent: bfloat16 [16, 1024, 1152], P('frames', 'patch'), may hold values from -6 to 6
- clip_embed: float32 [2, 1152], replicated, may hold values from -6 to 6
- timesteps: int32 [2], replicated, may hold values from 0 to 999
- frame_clip: int32 [16], P('frames'), may hold values from 0 to 1, never falling along the last dimension, each value on 1 to 15 neighbouring positions
- ada_weight: bfloat16 [1152, 6912], P(('frames', 'patch')), may hold values from -0.1875 to 0.1875
- ada_bias: bfloat16 [6912], P(('frames', 'patch')), may hold values from -3 to 3
- qkv_weight: bfloat16 [1152, 3456], P(('frames', 'patch')), may hold values from -0.1875 to 0.1875
- query_bias: bfloat16 [1152], P(('frames', 'patch')), may hold values from -2.5 to 2.5
- value_bias: bfloat16 [1152], P(('frames', 'patch')), may hold values from -2.5 to 2.5
- out_weight: bfloat16 [1152, 1152], P(('frames', 'patch')), may hold values from -3 to 3
- out_bias: bfloat16 [1152], P(('frames', 'patch')), may hold values from -5 to 5
- up_weight: bfloat16 [1152, 4608], P(('frames', 'patch')), may hold values from -0.1875 to 0.1875
- up_bias: bfloat16 [4608], P(('frames', 'patch')), may hold values from -2.5 to 2.5
- down_weight: bfloat16 [4608, 1152], P(('frames', 'patch')), may hold values from -0.125 to 0.125
- down_bias: bfloat16 [1152], P(('frames', 'patch')), may hold values from -5 to 5
Outputs:
- output: bfloat16 [16, 1024, 1152], P('frames', 'patch')
- tokens_grad: bfloat16 [16, 1024, 1152], P('frames', 'patch')
- clip_grad: float32 [2, 1152], replicated
- ada_weight_grad: float32 [1152, 6912], P(('frames', 'patch'))
- ada_bias_grad: float32 [6912], P(('frames', 'patch'))
- qkv_weight_grad: float32 [1152, 3456], P(('frames', 'patch'))
- query_bias_grad: float32 [1152], P(('frames', 'patch'))
- value_bias_grad: float32 [1152], P(('frames', 'patch'))
- out_weight_grad: float32 [1152, 1152], P(('frames', 'patch'))
- out_bias_grad: float32 [1152], P(('frames', 'patch'))
- up_weight_grad: float32 [1152, 4608], P(('frames', 'patch'))
- up_bias_grad: float32 [4608], P(('frames', 'patch'))
- down_weight_grad: float32 [4608, 1152], P(('frames', 'patch'))
- down_bias_grad: float32 [1152], P(('frames', 'patch'))
The draws below stay inside these ranges and needn't reach their ends.
Inputs may be any that keep to these rules, and one draw needn't show every extreme that they name: `frame_clip`: never falls along the frames; every clip has at least one frame.
All inputs are finite; a program needn't handle non-finite values.
Results may differ from the reference program's by a relative error of at most 0.018.
Values may be sent and summed in bfloat16 or wider, within the bound.
A program may use at most 320 MiB of HBM per device.

```python
import math
import jax
import jax.numpy as jnp
import numpy as np
from jax import lax

D = 1152
HEADS = 16
HEAD_DIM = 72
FF = 4608
PATCHES = 1024
FRAMES = 16
CLIPS = 2


def shard_levels(key, dims, pieces, least, top_value):
    loudness = 1.0
    for axis_at, blocks in pieces:
        draws = jax.random.uniform(jax.random.fold_in(jax.random.fold_in(key, 6), axis_at), (blocks,), jnp.float32, least / len(pieces), top_value / len(pieces))
        loudness = loudness * jnp.repeat(jnp.exp(draws), dims[axis_at] // blocks).reshape((-1,) + (1,) * (len(dims) - 1 - axis_at))
    return loudness


def profile(number_of, total, limit, slope):
    weights = [(1 << 20) // math.isqrt(standing ** slope) + 1 for standing in range(2, number_of + 1)]
    spare, counts = total - limit - (number_of - 1), [1] * (number_of - 1)
    while spare > 0:
        movable = [i for i in range(number_of - 1) if counts[i] < limit]
        whole, remaining = sum([weights[i] for i in movable]), spare
        for i in movable:
            extra = min(limit - counts[i], max(1, remaining * weights[i] // whole), spare)
            counts[i] = counts[i] + extra
            spare = spare - extra
    return np.array([limit] + counts)


def ragged(key, number_of, total, limit, slope):
    if number_of == 2:
        one = jax.random.randint(key, (), max(1, total - limit), min(limit, total - 1) + 1)
        return jnp.stack([one, total - one])
    sizes = jnp.asarray(profile(number_of, total, limit, slope), jnp.int32)
    twos = (number_of - 1) // 2
    giver, sink = sizes[1:1 + 2 * twos:2], sizes[2:2 + 2 * twos:2]
    room = jnp.minimum(giver - 1, limit - sink)
    passed = jax.random.randint(jax.random.fold_in(key, 1), (twos,), 0, 1 << 20) % (room + 1)
    sizes = sizes.at[1:1 + 2 * twos:2].set(giver - passed).at[2:2 + 2 * twos:2].set(sink + passed)
    return sizes[jax.random.permutation(jax.random.fold_in(key, 2), number_of)]


def centred(key, extent, scale, most, split=(), kind=jnp.bfloat16):
    level = shard_levels(key, extent, split, -0.22, 0.18) if split else 1.0
    values = jax.random.normal(key, extent, jnp.float32) * scale * level
    return jnp.minimum(jnp.maximum(values, -most), most).astype(kind)


def setup_inputs(seed: int = 0) -> dict:
    streams_of = jax.random.split(jax.random.key(seed), 17)
    return {
        "tokens": centred(streams_of[0], (FRAMES, PATCHES, D), 1.0, 6.0, ((0, 16), (1, 2))),
        "cotangent": centred(streams_of[1], (FRAMES, PATCHES, D), 1.0, 6.0, ((0, 16), (1, 2))),
        "clip_embed": centred(streams_of[2], (CLIPS, D), 1.0, 6.0, (), jnp.float32),
        "timesteps": jax.random.randint(streams_of[3], (CLIPS,), 0, 1000).astype(jnp.int32),
        "frame_clip": jnp.searchsorted(jnp.cumsum(ragged(streams_of[4], CLIPS, FRAMES, min(17, FRAMES - CLIPS + 1), 0)), jnp.arange(FRAMES), side="right").astype(jnp.int32),
        "ada_weight": centred(streams_of[5], (D, 6 * D), D ** -0.5, 0.1875, ((0, 32),)),
        "ada_bias": centred(streams_of[6], (6 * D,), 0.5, 3.0, ((0, 32),)),
        "qkv_weight": centred(streams_of[7], (D, 3 * D), D ** -0.5, 0.1875, ((0, 32),)),
        "query_bias": centred(streams_of[8], (D,), 0.4, 2.5, ((0, 32),)),
        "value_bias": centred(streams_of[9], (D,), 0.4, 2.5, ((0, 32),)),
        "out_weight": centred(streams_of[10], (D, D), (max(1, D // 256)) ** -0.5, 3.0, ((0, 32),)),
        "out_bias": centred(streams_of[11], (D,), 1.0, 5.0, ((0, 32),)),
        "up_weight": centred(streams_of[12], (D, FF), D ** -0.5, 0.1875, ((0, 32),)),
        "up_bias": centred(streams_of[13], (FF,), 0.4, 2.5, ((0, 32),)),
        "down_weight": centred(streams_of[14], (FF, D), (FF // 2) ** -0.5, 0.125, ((0, 32),)),
        "down_bias": centred(streams_of[15], (D,), 1.0, 5.0, ((0, 32),)),
    }


@jax.custom_vjp
def low(v):
    return lax.optimization_barrier(v.astype(jnp.bfloat16)).astype(jnp.float32)

@jax.custom_vjp
def low_back(v):
    return v

def low_keep(v):
    return (low(v), None)

def low_pass(kept, grad):
    return (grad,)

def back_keep(v):
    return (v, None)

def back_low(kept, grad):
    return (low(grad),)
low.defvjp(low_keep, low_pass)
low_back.defvjp(back_keep, back_low)

def matmul_hi(left, right):
    return jnp.dot(left, right, precision=lax.Precision.HIGHEST, preferred_element_type=jnp.float32)

def layer_norm(values_in):
    centre = values_in - lax.optimization_barrier(jnp.mean(values_in, axis=-1, keepdims=True))
    spread = lax.optimization_barrier(jnp.mean(centre * centre, axis=-1, keepdims=True))
    return centre * lax.rsqrt(spread + 1e-06)

def gelu_tanh(values_in):
    inner = 0.7978845608028654 * (values_in + 0.044715 * values_in * values_in * values_in)
    return 0.5 * values_in * (1.0 + jnp.tanh(inner))

def sinusoid(steps_in, width_in):
    half_width = width_in // 2
    freqs = jnp.exp(-math.log(10000.0) * jnp.arange(half_width, dtype=jnp.float32) / half_width)
    angles = steps_in.astype(jnp.float32)[:, None] * freqs[None, :]
    return jnp.concatenate([jnp.cos(angles), jnp.sin(angles)], axis=1)

def forward(params, token_in, clip_in, timesteps, frame_clip):
    ada_w, ada_b, qkv_w, query_b, value_b, out_w, out_b, up_w, up_b, down_w, down_b = params
    condition = clip_in + sinusoid(timesteps, D)
    modulation = low_back(matmul_hi(low(jax.nn.silu(condition)), ada_w) + ada_b)
    frame_mod = modulation[frame_clip]
    qkv_bias = jnp.concatenate([query_b, jnp.zeros((D,), jnp.float32), value_b])
    score_scale = 1.0 / math.sqrt(HEAD_DIM)
    group_frames = 4

    def frame_block(inputs):
        block_tokens, block_mod = inputs
        parts = [block_mod[:, None, column * D:(column + 1) * D] for column in range(6)]
        shift_one, scale_one, gate_one, shift_two, scale_two, gate_two = parts
        hidden_one = low(layer_norm(block_tokens) * (1.0 + scale_one) + shift_one)
        projected = matmul_hi(hidden_one.reshape(-1, D), qkv_w) + qkv_bias
        shape_heads = (group_frames, PATCHES, HEADS, HEAD_DIM)
        queries = low_back(low(projected[:, :D])).reshape(shape_heads)
        keys_all = low_back(low(projected[:, D:2 * D])).reshape(shape_heads)
        values_all = low_back(low(projected[:, 2 * D:])).reshape(shape_heads)
        scores = low_back(jnp.einsum('fqhd,fkhd->fhqk', queries, keys_all, precision=lax.Precision.HIGHEST) * score_scale)
        row_max = lax.optimization_barrier(jnp.max(scores, axis=-1, keepdims=True))
        exp_scores = jnp.exp(scores - row_max)
        attn_prob = low(exp_scores / lax.optimization_barrier(jnp.sum(exp_scores, axis=-1, keepdims=True)))
        attended = jnp.einsum('fhqk,fkhd->fqhd', attn_prob, values_all, precision=lax.Precision.HIGHEST)
        attended = low_back(low(attended.reshape(-1, D)))
        branch_one = low_back(matmul_hi(attended, out_w) + out_b).reshape(block_tokens.shape)
        midway = block_tokens + gate_one * branch_one
        hidden_two = low(layer_norm(midway) * (1.0 + scale_two) + shift_two)
        pre_act = low_back(matmul_hi(hidden_two.reshape(-1, D), up_w) + up_b)
        activation = low(gelu_tanh(pre_act))
        branch_two = low_back(matmul_hi(activation, down_w) + down_b).reshape(block_tokens.shape)
        return midway + gate_two * branch_two
    group_count = FRAMES // group_frames
    stacked = lax.map(jax.checkpoint(frame_block), (token_in.reshape(group_count, group_frames, PATCHES, D), frame_mod.reshape(group_count, group_frames, 6 * D)))
    return stacked.reshape(FRAMES, PATCHES, D)

def reference(tokens, cotangent, clip_embed, timesteps, frame_clip, ada_weight, ada_bias, qkv_weight, query_bias, value_bias, out_weight, out_bias, up_weight, up_bias, down_weight, down_bias):
    params = (ada_weight.astype(jnp.float32), ada_bias.astype(jnp.float32), qkv_weight.astype(jnp.float32), query_bias.astype(jnp.float32), value_bias.astype(jnp.float32), out_weight.astype(jnp.float32), out_bias.astype(jnp.float32), up_weight.astype(jnp.float32), up_bias.astype(jnp.float32), down_weight.astype(jnp.float32), down_bias.astype(jnp.float32))

    def wrapped(param_set, token_in, clip_in):
        return forward(param_set, token_in, clip_in, timesteps, frame_clip)
    result, pullback = jax.vjp(wrapped, params, tokens.astype(jnp.float32), clip_embed.astype(jnp.float32))
    param_grads, token_grad, clip_grad = pullback(cotangent.astype(jnp.float32))
    g_ada_w, g_ada_b, g_qkv_w, g_query_b, g_value_b, g_out_w, g_out_b, g_up_w, g_up_b, g_down_w, g_down_b = param_grads
    return (result.astype(jnp.bfloat16), token_grad.astype(jnp.bfloat16), clip_grad, g_ada_w, g_ada_b, g_qkv_w, g_query_b, g_value_b, g_out_w, g_out_b, g_up_w, g_up_b, g_down_w, g_down_b)
```

```python
import functools
import math

import jax
import jax.numpy as jnp
from jax import lax
from jax.experimental import pallas as pl
from jax.experimental.pallas import tpu as pltpu
from jax.sharding import Mesh
from jax.sharding import PartitionSpec as P

HEADS = 16
HEAD_DIM = 72
BF16 = jnp.bfloat16
F32 = jnp.float32
LOG2E = 1.4426950408889634
MESH_ID = pl.DeviceIdType.MESH
MIB = 2**20


def layer_norm(values_in):
    centre = values_in - jnp.mean(values_in, axis=-1, keepdims=True)
    spread = jnp.mean(centre * centre, axis=-1, keepdims=True)
    inv_std = lax.rsqrt(spread + 1e-06)
    return (centre * inv_std, inv_std)


def norm_back(grad_normed, normed, inv_std):
    mean_grad = jnp.mean(grad_normed, axis=-1, keepdims=True)
    mean_prod = jnp.mean(grad_normed * normed, axis=-1, keepdims=True)
    return (grad_normed - mean_grad - normed * mean_prod) * inv_std


def gelu_tanh(values_in):
    inner = 0.7978845608028654 * (values_in + 0.044715 * values_in * values_in * values_in)
    return 0.5 * values_in * (1.0 + jnp.tanh(inner))


def sinusoid(steps_in, width_in):
    half_width = width_in // 2
    freqs = jnp.exp(-math.log(10000.0) * jnp.arange(half_width, dtype=jnp.float32) / half_width)
    angles = steps_in.astype(jnp.float32)[:, None] * freqs[None, :]
    return jnp.concatenate([jnp.cos(angles), jnp.sin(angles)], axis=1)


def ring_place(index, size):
    along, across = index // 2, index % 2
    return (1 - across) * along + across * (size - 1 - along)


def ring_index(place, size):
    place = (place + 2 * size) % size
    back = place // (size // 2)
    return (1 - back) * 2 * place + back * (2 * (size - 1 - place) + 1)


def ring_peers(size):
    ring, core, patch = (lax.axis_index(name) for name in ("ring", "core", "patch"))
    place = ring_place(ring, size)
    right = (ring_index(place + 1, size), core, patch)
    left = (ring_index(place - 1, size), core, patch)
    return ring, place, right, left


def greet(peers):
    barrier = pltpu.get_barrier_semaphore()
    for peer in peers:
        pl.semaphore_signal(barrier, inc=1, device_id=peer, device_id_type=MESH_ID)
    pl.semaphore_wait(barrier, len(peers))


def halves(rows, columns):
    if rows % 16 == 0:
        cut = -(-rows // 32) * 16
        return (pl.ds(0, cut), slice(None)), (pl.ds(cut, rows - cut), slice(None))
    cut = -(-columns // 256) * 128
    return (slice(None), pl.ds(0, cut)), (slice(None), pl.ds(cut, columns - cut))


def ring_gather_kernel(size, count, *refs):
    ins, outs = refs[:count], refs[count : 2 * count]
    send_sem, recv_sem, local_sem = refs[2 * count :]
    ring, place, right, left = ring_peers(size)
    greet([right, left])
    local = [
        pltpu.make_async_copy(ins[at], outs[at].at[ring], local_sem.at[at]) for at in range(count)
    ]
    for copy in local:
        copy.start()
    copies = {}
    for step in range(size - 1):
        for at in range(count):
            parts = halves(*ins[at].shape)
            for way, (part, peer, sign) in enumerate(zip(parts, (right, left), (-1, 1))):
                slot = ring_index(place + sign * step, size)
                if step:
                    copies[at, way, step - 1].wait_recv()
                    source = outs[at].at[(slot,) + part]
                else:
                    source = ins[at].at[part]
                copy = pltpu.make_async_remote_copy(
                    src_ref=source,
                    dst_ref=outs[at].at[(slot,) + part],
                    send_sem=send_sem.at[at, way, step],
                    recv_sem=recv_sem.at[at, way, step],
                    device_id=peer,
                    device_id_type=MESH_ID,
                )
                copy.start()
                copies[at, way, step] = copy
    for (at, way, step), copy in copies.items():
        if step == size - 2:
            copy.wait_recv()
        copy.wait_send()
    for copy in local:
        copy.wait()


def ring_gather(blocks, size, call_id):
    count = len(blocks)
    space = pl.BlockSpec(memory_space=pl.ANY)
    moved = sum(block.size * 2 * size for block in blocks)
    return pl.pallas_call(
        functools.partial(ring_gather_kernel, size, count),
        out_shape=[jax.ShapeDtypeStruct((size,) + block.shape, block.dtype) for block in blocks],
        in_specs=[space] * count,
        out_specs=[space] * count,
        scratch_shapes=[
            pltpu.SemaphoreType.DMA((count, 2, size - 1)),
            pltpu.SemaphoreType.DMA((count, 2, size - 1)),
            pltpu.SemaphoreType.DMA((count,)),
        ],
        compiler_params=pltpu.CompilerParams(collective_id=call_id, has_side_effects=True),
        cost_estimate=pl.CostEstimate(flops=0, bytes_accessed=moved * 12, transcendentals=0),
        name=f"ring_gather_{call_id}",
    )(*blocks)


def ring_sum_kernel(size, count, *refs):
    ins, outs = refs[:count], refs[count : 2 * count]
    held, landed = refs[2 * count : 3 * count], refs[3 * count : 4 * count]
    send_sem, recv_sem = refs[4 * count :]
    ring, place, right, left = ring_peers(size)
    greet([right, left])
    copies = {}
    for step in range(size):
        for at in range(count):
            parts = halves(*ins[at].shape[1:])
            for way, (part, peer, sign) in enumerate(zip(parts, (right, left), (-1, 1))):
                slot = ring_index(place + sign * (step + 1), size)
                total = ins[at][(slot,) + part]
                if step:
                    copies[at, way, step - 1].wait_recv()
                    total = total.astype(F32) + landed[at][(step - 1,) + part].astype(F32)
                if step == size - 1:
                    outs[at][part] = total.astype(outs[at].dtype)
                    continue
                held[at][(step,) + part] = total.astype(BF16)
                copy = pltpu.make_async_remote_copy(
                    src_ref=held[at].at[(step,) + part],
                    dst_ref=landed[at].at[(step,) + part],
                    send_sem=send_sem.at[at, way, step],
                    recv_sem=recv_sem.at[at, way, step],
                    device_id=peer,
                    device_id_type=MESH_ID,
                )
                copy.start()
                copies[at, way, step] = copy
    for copy in copies.values():
        copy.wait_send()


def ring_sum(blocks, dtypes, size, call_id):
    count = len(blocks)
    space = pl.BlockSpec(memory_space=pltpu.VMEM)
    moved = sum(block.size * 2 for block in blocks)
    slots = [pltpu.VMEM((size - 1,) + block.shape[1:], BF16) for block in blocks]
    return pl.pallas_call(
        functools.partial(ring_sum_kernel, size, count),
        out_shape=[
            jax.ShapeDtypeStruct(block.shape[1:], dtype)
            for block, dtype in zip(blocks, dtypes)
        ],
        in_specs=[space] * count,
        out_specs=[space] * count,
        scratch_shapes=slots
        + slots
        + [
            pltpu.SemaphoreType.DMA((count, 2, size - 1)),
            pltpu.SemaphoreType.DMA((count, 2, size - 1)),
        ],
        compiler_params=pltpu.CompilerParams(
            collective_id=call_id, has_side_effects=True, vmem_limit_bytes=40 * MIB
        ),
        cost_estimate=pl.CostEstimate(flops=0, bytes_accessed=moved * 12, transcendentals=0),
        name=f"ring_sum_{call_id}",
    )(*blocks)


def sum_bits(sizes):
    bits = []
    for axis, size in enumerate(sizes):
        bit = 1
        while bit < size:
            bits.append((axis, bit))
            bit *= 2
    return bits


def all_sum_kernel(bits, in_ref, out_ref, held, landed, send_sem, recv_sem):
    here = [lax.axis_index(name) for name in ("ring", "core", "patch")]
    peers = []
    for axis, bit in bits:
        peer = list(here)
        peer[axis] = here[axis] + (1 - 2 * ((here[axis] // bit) % 2)) * bit
        peers.append(tuple(peer))
    greet(peers)
    held[0] = in_ref[...]
    for step, peer in enumerate(peers):
        copy = pltpu.make_async_remote_copy(
            src_ref=held.at[step],
            dst_ref=landed.at[step],
            send_sem=send_sem.at[step],
            recv_sem=recv_sem.at[step],
            device_id=peer,
            device_id_type=MESH_ID,
        )
        copy.start()
        copy.wait()
        total = held[step] + landed[step]
        if step == len(peers) - 1:
            out_ref[...] = total
        else:
            held[step + 1] = total


def all_sum(vector, sizes, call_id):
    length = vector.shape[0]
    rows = -(-length // 1024) * 8
    block = jnp.pad(vector, (0, rows * 128 - length)).reshape(rows, 128)
    bits = sum_bits(sizes)
    space = pl.BlockSpec(memory_space=pltpu.VMEM)
    total = pl.pallas_call(
        functools.partial(all_sum_kernel, bits),
        out_shape=jax.ShapeDtypeStruct(block.shape, F32),
        in_specs=[space],
        out_specs=space,
        scratch_shapes=[
            pltpu.VMEM((len(bits), rows, 128), F32),
            pltpu.VMEM((len(bits), rows, 128), F32),
            pltpu.SemaphoreType.DMA((len(bits),)),
            pltpu.SemaphoreType.DMA((len(bits),)),
        ],
        compiler_params=pltpu.CompilerParams(collective_id=call_id, has_side_effects=True),
        name=f"all_sum_{call_id}",
    )(block)
    return total.reshape(rows * 128)[:length]


def attention_kernel(factor, chunk, q_ref, k_ref, v_ref, out_ref, lse_ref):
    keys = k_ref[0].T
    values_t = v_ref[0]
    for start in range(0, q_ref.shape[2], chunk):
        span = slice(start, start + chunk)
        scores = jnp.dot(keys, q_ref[0, :, span], preferred_element_type=F32) * factor
        top = jnp.max(scores, axis=0, keepdims=True)
        probs = jnp.exp2(scores - top)
        total = jnp.sum(probs, axis=0, keepdims=True)
        mixed = jnp.dot(values_t, probs.astype(BF16), preferred_element_type=F32)
        out_ref[0, :, span] = (mixed / total).astype(BF16)
        lse_ref[0, :, span] = top + jnp.log2(total)


def attention(qkv, patches):
    triple, dim, tokens = qkv.shape
    heads = triple // 3
    frames = tokens // patches
    block = (1, dim, patches)
    factor = LOG2E / math.sqrt(HEAD_DIM)
    return pl.pallas_call(
        functools.partial(attention_kernel, factor, min(256, patches)),
        out_shape=[
            jax.ShapeDtypeStruct((heads, dim, tokens), BF16),
            jax.ShapeDtypeStruct((heads, 1, tokens), F32),
        ],
        grid=(frames, heads),
        in_specs=[
            pl.BlockSpec(block, lambda f, h: (h, 0, f)),
            pl.BlockSpec(block, lambda f, h: (heads + h, 0, f)),
            pl.BlockSpec(block, lambda f, h: (2 * heads + h, 0, f)),
        ],
        out_specs=[
            pl.BlockSpec(block, lambda f, h: (h, 0, f)),
            pl.BlockSpec((1, 1, patches), lambda f, h: (h, 0, f)),
        ],
        compiler_params=pltpu.CompilerParams(vmem_limit_bytes=32 * MIB),
        cost_estimate=pl.CostEstimate(
            flops=4 * heads * patches * tokens * 256,
            bytes_accessed=4 * heads * dim * tokens * 2,
            transcendentals=heads * patches * tokens,
        ),
        name="attention",
    )(qkv, qkv, qkv)


def attention_back_kernel(
    factor, chunk, q_ref, k_ref, v_ref, g_ref, lse_ref, dq_ref, dk_ref, dv_ref, dk_sum, dv_sum
):
    keys_t = k_ref[0]
    keys = keys_t.T
    values = v_ref[0].T
    scale = factor / LOG2E
    patches = q_ref.shape[2]
    for start in range(0, patches, chunk):
        span = slice(start, start + chunk)
        queries_t = q_ref[0, :, span]
        grad_t = g_ref[0, :, span]
        scores = jnp.dot(keys, queries_t, preferred_element_type=F32) * factor
        probs = jnp.exp2(scores - lse_ref[0, :, span])
        grad_probs = jnp.dot(values, grad_t, preferred_element_type=F32)
        row_dot = jnp.sum(probs * grad_probs, axis=0, keepdims=True)
        grad_scores = (probs * (grad_probs - row_dot)).astype(BF16)
        probs_low = probs.astype(BF16)
        dq = jnp.dot(keys_t, grad_scores, preferred_element_type=F32)
        dq_ref[0, :, span] = (dq * scale).astype(BF16)
        dims = (((1,), (1,)), ((), ()))
        dk = lax.dot_general(queries_t, grad_scores, dims, preferred_element_type=F32)
        dv = lax.dot_general(grad_t, probs_low, dims, preferred_element_type=F32)
        if start == 0:
            dk_sum[...] = dk
            dv_sum[...] = dv
        else:
            dk_sum[...] += dk
            dv_sum[...] += dv
    dk_ref[0] = (dk_sum[...] * scale).astype(BF16)
    dv_ref[0] = dv_sum[...].astype(BF16)


def attention_back(qkv, grad, lse, patches):
    triple, dim, tokens = qkv.shape
    heads = triple // 3
    frames = tokens // patches
    block = (1, dim, patches)
    factor = LOG2E / math.sqrt(HEAD_DIM)
    spec = pl.BlockSpec(block, lambda f, h: (h, 0, f))
    shape = jax.ShapeDtypeStruct((heads, dim, tokens), BF16)
    parts = pl.pallas_call(
        functools.partial(attention_back_kernel, factor, min(256, patches)),
        out_shape=[shape] * 3,
        grid=(frames, heads),
        in_specs=[
            spec,
            pl.BlockSpec(block, lambda f, h: (heads + h, 0, f)),
            pl.BlockSpec(block, lambda f, h: (2 * heads + h, 0, f)),
            spec,
            pl.BlockSpec((1, 1, patches), lambda f, h: (h, 0, f)),
        ],
        out_specs=[spec] * 3,
        scratch_shapes=[pltpu.VMEM((dim, patches), F32)] * 2,
        compiler_params=pltpu.CompilerParams(vmem_limit_bytes=40 * MIB),
        cost_estimate=pl.CostEstimate(
            flops=10 * heads * patches * tokens * 256,
            bytes_accessed=8 * heads * dim * tokens * 2,
            transcendentals=heads * patches * tokens,
        ),
        name="attention_back",
    )(qkv, qkv, qkv, grad, lse)
    return jnp.concatenate(parts, axis=0)


def from_patch(array, hops, size):
    if hops == 0:
        return array
    return lax.ppermute(array, "patch", [((to + hops) % size, to) for to in range(size)])


def from_core(array):
    return lax.ppermute(array, "core", [(0, 1), (1, 0)])


def group_gather(block, size):
    mine = jnp.concatenate([from_patch(block, hops, size) for hops in range(size)], axis=0)
    return jnp.concatenate([mine, from_core(mine)], axis=0)


def group_sum(terms, size):
    half = terms.shape[0] // 2
    mine = terms[:half].astype(F32) + from_core(terms[half:].astype(BF16)).astype(F32)
    rows = half // size
    total = mine[:rows]
    for hops in range(1, size):
        send = mine[hops * rows : (hops + 1) * rows].astype(BF16)
        total = total + from_patch(send, size - hops, size).astype(F32)
    return total


def group_swap(pieces, size):
    out = []
    for dc in range(2):
        row = []
        for dx in range(size):
            piece = pieces[dc][(size - dx) % size]
            piece = from_patch(piece, dx, size)
            row.append(from_core(piece) if dc else piece)
        out.append(row)
    return out


def natural(pieces, size):
    core, patch = lax.axis_index("core"), lax.axis_index("patch")
    if size == 2:
        swapped = [
            [jnp.where(patch == 0, row[0], row[1]), jnp.where(patch == 0, row[1], row[0])]
            for row in pieces
        ]
    else:
        swapped = []
        for row in pieces:
            stack = jnp.stack(row)
            swapped.append(
                [
                    lax.dynamic_index_in_dim(stack, (to - patch + size) % size, 0, False)
                    for to in range(size)
                ]
            )
    first = [jnp.where(core == 0, a, b) for a, b in zip(swapped[0], swapped[1])]
    second = [jnp.where(core == 0, b, a) for a, b in zip(swapped[0], swapped[1])]
    return first + second


def relative(blocks, size):
    core, patch = lax.axis_index("core"), lax.axis_index("patch")
    return [
        [
            lax.dynamic_index_in_dim(
                blocks, (core + dc) % 2 * size + (patch + dx) % size, 0, False
            )
            for dx in range(size)
        ]
        for dc in range(2)
    ]


def per_device(
    tokens,
    cotangent,
    clip_embed,
    timesteps,
    frame_clip,
    ada_weight,
    ada_bias,
    qkv_weight,
    query_bias,
    value_bias,
    out_weight,
    out_bias,
    up_weight,
    up_bias,
    down_weight,
    down_bias,
):
    ring_size, patch_size = lax.axis_size("ring"), lax.axis_size("patch")
    sizes = (ring_size, 2, patch_size)
    group = 2 * patch_size
    device_count = ring_size * group
    ring, core, patch = (lax.axis_index(name) for name in ("ring", "core", "patch"))
    member = core * patch_size + patch
    device = ring * group + member
    rows, width = tokens.shape[1:]
    tokens, cotangent = tokens[0], cotangent[0]
    patches = patch_size * rows
    clips = clip_embed.shape[0]
    hidden = up_weight.shape[1]
    share = width // device_count
    heads = HEADS // group
    head_width = heads * HEAD_DIM
    units = hidden // group
    mine = jnp.arange(group) == member
    mine_of_all = jnp.arange(device_count) == device

    tokens_all = group_gather(tokens, patch_size)

    qkv_cols = jnp.transpose(qkv_weight.reshape(share, 3, group, head_width), (2, 0, 1, 3)).reshape(
        group, share, 3 * head_width
    )
    up_cols = jnp.transpose(
        up_weight.reshape(share, ring_size, group, hidden // device_count), (2, 0, 1, 3)
    ).reshape(group, share, units)
    packed = jnp.concatenate(
        [qkv_cols, up_cols, jnp.broadcast_to(out_weight, (group,) + out_weight.shape)], axis=2
    )
    received = jnp.concatenate(
        natural(group_swap(relative(packed, patch_size), patch_size), patch_size), axis=0
    )
    qkv_block = received[:, : 3 * head_width]
    up_block = received[:, 3 * head_width : 3 * head_width + units]
    out_block = received[:, 3 * head_width + units :]
    (w_qkv,) = ring_gather([qkv_block], ring_size, 1)
    w_out, w_up, w_down = ring_gather([out_block, up_block, down_weight], ring_size, 2)
    w_qkv = w_qkv.reshape(width, 3 * head_width)
    w_out = w_out.reshape(width, width)
    w_up = w_up.reshape(width, units)
    w_down = w_down.reshape(units, width)

    condition = clip_embed + sinusoid(timesteps, width)
    silu_cond, silu_back = jax.vjp(jax.nn.silu, condition)
    silu_low = silu_cond.astype(BF16)
    silu_part = lax.dynamic_slice_in_dim(silu_low, device * share, share, 1)
    mod_part = jnp.dot(silu_part, ada_weight, preferred_element_type=F32)

    def placed(shard):
        return jnp.where(mine_of_all[:, None], shard.astype(F32)[None, :], 0.0).reshape(-1)

    mod_part = mod_part + placed(ada_bias)[None, :]
    frame_count = 2 * ring_size
    own_frame = 2 * ring + core
    clip_part = jnp.where(
        (jnp.arange(frame_count) == own_frame) & (patch == 0), frame_clip[0].astype(F32), 0.0
    )
    sent = [
        mod_part.reshape(-1),
        placed(query_bias),
        placed(value_bias),
        placed(out_bias),
        placed(down_bias),
        placed(up_bias),
        clip_part,
    ]
    summed = all_sum(jnp.concatenate(sent), sizes, 3)
    got, at = [], 0
    for item in sent:
        got.append(summed[at : at + item.shape[0]])
        at += item.shape[0]
    modulation = got[0].reshape(clips, 6 * width)
    b_query = lax.dynamic_slice_in_dim(got[1], member * head_width, head_width, 0)
    b_value = lax.dynamic_slice_in_dim(got[2], member * head_width, head_width, 0)
    b_out, b_down = got[3], got[4]
    b_up = lax.dynamic_index_in_dim(
        got[5].reshape(ring_size, group, hidden // device_count), member, 1, False
    ).reshape(units)
    own_clip = frame_clip[0]
    other_clip = lax.dynamic_index_in_dim(got[6], 2 * ring + 1 - core, 0, False).astype(jnp.int32)
    own_mod = lax.dynamic_index_in_dim(modulation, own_clip, 0, False)
    other_mod = lax.dynamic_index_in_dim(modulation, other_clip, 0, False)
    shift_one, scale_one, gate_one, shift_two, scale_two, gate_two = (
        own_mod[at * width : (at + 1) * width] for at in range(6)
    )
    both = jnp.stack([own_mod[: 2 * width], other_mod[: 2 * width]])[:, None, :]

    normed_all, _ = layer_norm(tokens_all.astype(F32).reshape(2, patches, width))
    hidden_one = (
        (normed_all * (1.0 + both[:, :, width:]) + both[:, :, :width])
        .astype(BF16)
        .reshape(2 * patches, width)
    )
    qkv_bias = jnp.concatenate([b_query, jnp.zeros_like(b_query), b_value])
    projected = (
        lax.dot_general(w_qkv, hidden_one, (((0,), (1,)), ((), ())), preferred_element_type=F32)
        + qkv_bias[:, None]
    ).astype(BF16)
    qkv = projected.reshape(3 * heads, HEAD_DIM, 2 * patches)
    attended_t, lse = attention(qkv, patches)
    attended_t = attended_t.reshape(head_width, 2 * patches)

    def token_pieces(array):
        return [
            [
                array[:, (dc * patch_size + dx) * rows : (dc * patch_size + dx + 1) * rows]
                for dx in range(patch_size)
            ]
            for dc in range(2)
        ]

    attended = jnp.concatenate(
        natural(group_swap(token_pieces(attended_t), patch_size), patch_size), axis=0
    )

    input_rows = tokens.astype(F32)
    branch_one = (
        lax.dot_general(attended, w_out, (((0,), (0,)), ((), ())), preferred_element_type=F32)
        + b_out
    )
    midway = input_rows + gate_one * branch_one
    normed_two, inv_two = layer_norm(midway)
    hidden_two = (normed_two * (1.0 + scale_two) + shift_two).astype(BF16)
    grad_out = cotangent.astype(F32)
    grad_branch_two = (gate_two * grad_out).astype(BF16)

    gb_two_all = group_gather(grad_branch_two, patch_size)
    hidden_two_all = group_gather(hidden_two, patch_size)
    pre_act = jnp.dot(hidden_two_all, w_up, preferred_element_type=F32) + b_up
    act_full, gelu_back = jax.vjp(gelu_tanh, pre_act)
    act_low = act_full.astype(BF16)
    branch_two = group_sum(jnp.dot(act_low, w_down, preferred_element_type=F32), patch_size) + b_down
    output = (midway + gate_two * branch_two).astype(BF16)

    grad_act = lax.dot_general(
        gb_two_all, w_down, (((1,), (1,)), ((), ())), preferred_element_type=F32
    )
    grad_pre = gelu_back(grad_act)[0].astype(BF16)
    grad_hidden_two = group_sum(
        lax.dot_general(grad_pre, w_up, (((1,), (1,)), ((), ())), preferred_element_type=F32),
        patch_size,
    )
    over_tokens = (((0,), (0,)), ((), ()))
    g_down = lax.dot_general(act_low, gb_two_all, over_tokens, preferred_element_type=F32).astype(
        BF16
    )
    g_up = lax.dot_general(
        hidden_two_all, grad_pre, over_tokens, preferred_element_type=F32
    ).astype(BF16)
    g_up_b = jnp.sum(grad_pre.astype(F32), axis=0)
    g_down_b = jnp.sum(grad_branch_two.astype(F32), axis=0)
    block_rows = width // ring_size
    share_down, sum_up = ring_sum(
        [
            g_down.reshape(ring_size, units // ring_size, width),
            g_up.reshape(ring_size, block_rows, units),
        ],
        [F32, BF16],
        ring_size,
        4,
    )

    grad_gate_two = jnp.sum(grad_out * branch_two, axis=0)
    grad_shift_two = jnp.sum(grad_hidden_two, axis=0)
    grad_scale_two = jnp.sum(grad_hidden_two * normed_two, axis=0)
    grad_midway = grad_out + norm_back(grad_hidden_two * (1.0 + scale_two), normed_two, inv_two)
    grad_gate_one = jnp.sum(grad_midway * branch_one, axis=0)
    grad_branch_one = (gate_one * grad_midway).astype(BF16)
    g_out_b = jnp.sum(grad_branch_one.astype(F32), axis=0)
    grad_attended = lax.dot_general(
        w_out, grad_branch_one, (((1,), (1,)), ((), ())), preferred_element_type=F32
    ).astype(BF16)
    g_out = jnp.dot(attended, grad_branch_one, preferred_element_type=F32).astype(BF16)
    swapped = group_swap(
        relative(grad_attended.reshape(group, head_width, rows), patch_size), patch_size
    )
    grad_mix = jnp.concatenate([piece for row in swapped for piece in row], axis=1)
    grad_projected = attention_back(
        qkv, grad_mix.reshape(heads, HEAD_DIM, 2 * patches), lse, patches
    ).reshape(3 * head_width, 2 * patches)

    g_qkv = lax.dot_general(
        hidden_one, grad_projected, (((0,), (1,)), ((), ())), preferred_element_type=F32
    ).astype(BF16)
    g_query_b = jnp.sum(grad_projected[:head_width].astype(F32), axis=1)
    g_value_b = jnp.sum(grad_projected[2 * head_width :].astype(F32), axis=1)
    grad_hidden_one = group_sum(
        lax.dot_general(
            grad_projected, w_qkv, (((0,), (1,)), ((), ())), preferred_element_type=F32
        ),
        patch_size,
    )
    sum_out, sum_qkv = ring_sum(
        [g_out.reshape(ring_size, block_rows, width), g_qkv.reshape(ring_size, block_rows, -1)],
        [BF16, BF16],
        ring_size,
        5,
    )

    normed_one, inv_one = layer_norm(input_rows)
    grad_shift_one = jnp.sum(grad_hidden_one, axis=0)
    grad_scale_one = jnp.sum(grad_hidden_one * normed_one, axis=0)
    tokens_grad = (
        grad_midway + norm_back(grad_hidden_one * (1.0 + scale_one), normed_one, inv_one)
    ).astype(BF16)

    pieces = jnp.concatenate([sum_qkv, sum_up, sum_out], axis=1).reshape(group, share, -1)
    got_w = natural(group_swap(relative(pieces, patch_size), patch_size), patch_size)
    stacked = jnp.stack(got_w).astype(F32)
    share_qkv = jnp.transpose(
        stacked[:, :, : 3 * head_width].reshape(group, share, 3, head_width), (1, 2, 0, 3)
    ).reshape(share, 3 * width)
    share_up = jnp.transpose(
        stacked[:, :, 3 * head_width : 3 * head_width + units].reshape(
            group, share, ring_size, hidden // device_count
        ),
        (1, 2, 0, 3),
    ).reshape(share, hidden)
    share_out = jnp.sum(stacked[:, :, 3 * head_width + units :], axis=0)

    frame_grads = jnp.concatenate(
        [
            grad_shift_one,
            grad_scale_one,
            grad_gate_one,
            grad_shift_two,
            grad_scale_two,
            grad_gate_two,
        ]
    )
    clip_terms = jnp.where(
        (jnp.arange(clips) == own_clip)[:, None], frame_grads[None, :], 0.0
    ).reshape(-1)
    terms = [
        clip_terms,
        jnp.where(mine[:, None], g_query_b[None, :], 0.0).reshape(-1),
        jnp.where(mine[:, None], g_value_b[None, :], 0.0).reshape(-1),
        g_out_b,
        g_down_b,
        jnp.where(mine[None, :, None], g_up_b.reshape(ring_size, 1, -1), 0.0).reshape(-1),
    ]
    summed = all_sum(jnp.concatenate(terms), sizes, 6)
    got, at = [], 0
    for item in terms:
        got.append(summed[at : at + item.shape[0]])
        at += item.shape[0]
    mod_low = got[0].reshape(clips, 6 * width).astype(BF16)

    def own(vector):
        length = vector.shape[0] // device_count
        return lax.dynamic_slice_in_dim(vector, device * length, length, 0)

    ada_bias_grad = own(jnp.sum(mod_low.astype(F32), axis=0))
    ada_weight_grad = lax.dot_general(
        silu_part, mod_low, (((0,), (0,)), ((), ())), preferred_element_type=F32
    )
    grad_silu_part = lax.dot_general(
        mod_low, ada_weight, (((1,), (1,)), ((), ())), preferred_element_type=F32
    )
    grad_silu = all_sum(
        jnp.where(mine_of_all[None, :, None], grad_silu_part[:, None, :], 0.0).reshape(-1),
        sizes,
        7,
    ).reshape(clips, width)
    clip_grad = silu_back(grad_silu)[0]
    return (
        output[None],
        tokens_grad[None],
        clip_grad,
        ada_weight_grad,
        ada_bias_grad,
        share_qkv,
        own(got[1]),
        own(got[2]),
        share_out,
        own(got[3]),
        share_up,
        own(got[5]),
        share_down,
        own(got[4]),
    )


def solution(mesh):
    frames, patch = mesh.shape["frames"], mesh.shape["patch"]
    inner = Mesh(mesh.devices.reshape(frames // 2, 2, patch), ("ring", "core", "patch"))
    every = ("ring", "core", "patch")
    tokens = P(("ring", "core"), "patch", None)
    matrix = P(every, None)
    vector = P(every)
    return jax.shard_map(
        per_device,
        mesh=inner,
        in_specs=(
            tokens,
            tokens,
            P(),
            P(),
            P(("ring", "core")),
            matrix,
            vector,
            matrix,
            vector,
            vector,
            matrix,
            vector,
            matrix,
            vector,
            matrix,
            vector,
        ),
        out_specs=(
            tokens,
            tokens,
            P(),
            matrix,
            vector,
            matrix,
            vector,
            vector,
            matrix,
            vector,
            matrix,
            vector,
            matrix,
            vector,
        ),
        check_vma=False,
    )
```

```python
import functools
import math

import jax
import jax.numpy as jnp
from jax import lax
from jax.experimental import pallas as pl
from jax.experimental.pallas import tpu as pltpu
from jax.sharding import Mesh
from jax.sharding import PartitionSpec as P

HEADS = 16
HEAD_DIM = 72
BF16 = jnp.bfloat16
F32 = jnp.float32
LOG2E = 1.4426950408889634
MESH_ID = pl.DeviceIdType.MESH
MIB = 2**20


def layer_norm(values_in):
    centre = values_in - jnp.mean(values_in, axis=-1, keepdims=True)
    spread = jnp.mean(centre * centre, axis=-1, keepdims=True)
    inv_std = lax.rsqrt(spread + 1e-06)
    return (centre * inv_std, inv_std)


def norm_back(grad_normed, normed, inv_std):
    mean_grad = jnp.mean(grad_normed, axis=-1, keepdims=True)
    mean_prod = jnp.mean(grad_normed * normed, axis=-1, keepdims=True)
    return (grad_normed - mean_grad - normed * mean_prod) * inv_std


def gelu_tanh(values_in):
    inner = 0.7978845608028654 * (values_in + 0.044715 * values_in * values_in * values_in)
    return 0.5 * values_in * (1.0 + jnp.tanh(inner))


def sinusoid(steps_in, width_in):
    half_width = width_in // 2
    freqs = jnp.exp(-math.log(10000.0) * jnp.arange(half_width, dtype=jnp.float32) / half_width)
    angles = steps_in.astype(jnp.float32)[:, None] * freqs[None, :]
    return jnp.concatenate([jnp.cos(angles), jnp.sin(angles)], axis=1)


class Where:
    def __init__(self, sizes):
        self.size, _, self.span = sizes
        self.ring, self.core, self.patch = (
            lax.axis_index(name) for name in ("ring", "core", "patch")
        )
        along, across = self.ring // 2, self.ring % 2
        self.place = (1 - across) * along + across * (self.size - 1 - along)
        self.member = self.core * self.span + self.patch

    def at_place(self, place):
        place = (place + 2 * self.size) % self.size
        back = place // (self.size // 2)
        return (1 - back) * 2 * place + back * (2 * (self.size - 1 - place) + 1)

    def neighbour(self, step):
        return (self.at_place(self.place + step), self.core, self.patch)

    def peer(self, dc, dx):
        core = 1 - self.core if dc else self.core
        return (self.ring, core, (self.patch + dx) % self.span)

    def peer_member(self, dc, dx):
        _, core, patch = self.peer(dc, dx)
        return core * self.span + patch

    def ring_peers(self):
        return [self.neighbour(1), self.neighbour(-1)]

    def group_peers(self):
        return [
            self.peer(dc, dx) for dc in range(2) for dx in range(self.span) if dc or dx
        ]


def greet(peers):
    barrier = pltpu.get_barrier_semaphore()
    for peer in peers:
        pl.semaphore_signal(barrier, inc=1, device_id=peer, device_id_type=MESH_ID)
    pl.semaphore_wait(barrier, len(peers))


def remote(source, target, send_sem, recv_sem, peer):
    return pltpu.make_async_remote_copy(
        src_ref=source,
        dst_ref=target,
        send_sem=send_sem,
        recv_sem=recv_sem,
        device_id=peer,
        device_id_type=MESH_ID,
    )


def halves(rows, columns):
    if rows % 16 == 0:
        cut = -(-rows // 32) * 16
        return (pl.ds(0, cut), slice(None)), (pl.ds(cut, rows - cut), slice(None))
    cut = -(-columns // 256) * 128
    return (slice(None), pl.ds(0, cut)), (slice(None), pl.ds(cut, columns - cut))


class RingGather:
    @staticmethod
    def scratch(size):
        dma = pltpu.SemaphoreType.DMA
        return [dma((2, size - 1)), dma((2, size - 1)), dma((1,))]

    def __init__(self, where, block, out, sems):
        self.where, self.block, self.out = where, block, out
        self.send, self.recv, self.own = sems
        self.steps = where.size

    def keep(self):
        return pltpu.make_async_copy(self.block, self.out.at[self.where.ring], self.own.at[0])

    def copy(self, way, step):
        where, sign = self.where, (-1, 1)[way]
        part = halves(*self.block.shape)[way]
        slot = where.at_place(where.place + sign * step)
        target = self.out.at[(slot,) + part]
        source = target if step else self.block.at[part]
        return remote(
            source, target, self.send.at[way, step], self.recv.at[way, step], where.neighbour(-sign)
        )

    def run(self, step):
        last = self.where.size - 2
        if step == 0:
            self.keep().start()
        for way in range(2):
            if step:
                self.copy(way, step - 1).wait_recv()
            if step <= last:
                self.copy(way, step).start()
        if step > last:
            for way in range(2):
                for past in range(last + 1):
                    self.copy(way, past).wait_send()
            self.keep().wait()


class RingGatherSplit:
    @staticmethod
    def scratch(size):
        dma, half = pltpu.SemaphoreType.DMA, size // 2
        return [dma((half,)), dma((half,)), dma((half,)), dma((half,)), dma((1,))]

    def __init__(self, where, block, out, sems):
        self.where, self.block, self.out = where, block, out
        self.send, self.recv, self.send_core, self.recv_core, self.own = sems
        self.half = where.size // 2
        self.steps = self.half + 2

    def keep(self):
        return pltpu.make_async_copy(self.block, self.out.at[self.where.ring], self.own.at[0])

    def slot(self, step):
        where = self.where
        return self.out.at[where.at_place(where.place + (2 * where.core - 1) * step)]

    def copy(self, step):
        where = self.where
        target = self.slot(step)
        source = target if step else self.block
        peer = where.neighbour(1 - 2 * where.core)
        return remote(source, target, self.send.at[step], self.recv.at[step], peer)

    def hand(self, step):
        target = self.slot(step + 1)
        return remote(
            target, target, self.send_core.at[step], self.recv_core.at[step], self.where.peer(1, 0)
        )

    def run(self, step):
        half = self.half
        if step == 0:
            self.keep().start()
        if 0 < step <= half:
            self.copy(step - 1).wait_recv()
        if step < half:
            self.copy(step).start()
        if 0 < step < half:
            self.hand(step - 1).start()
        if step == half + 1:
            for past in range(half):
                self.copy(past).wait_send()
            for past in range(half - 1):
                self.hand(past).wait()
            self.keep().wait()


class RingSum:
    @staticmethod
    def scratch(size, rows, columns):
        dma = pltpu.SemaphoreType.DMA
        slots = pltpu.VMEM((size - 1, rows, columns), BF16)
        return [slots, slots, dma((2, size - 1)), dma((2, size - 1))]

    def __init__(self, where, terms, out, scratch):
        self.where, self.terms, self.out = where, terms, out
        self.held, self.landed, self.send, self.recv = scratch
        self.steps = where.size

    def copy(self, way, step):
        part = (step,) + halves(*self.terms.shape[1:])[way]
        return remote(
            self.held.at[part],
            self.landed.at[part],
            self.send.at[way, step],
            self.recv.at[way, step],
            self.where.neighbour((1, -1)[way]),
        )

    def run(self, step):
        where, last = self.where, self.where.size - 2
        for way, part in enumerate(halves(*self.terms.shape[1:])):
            slot = where.at_place(where.place + (-1, 1)[way] * (step + 1))
            total = self.terms[(slot,) + part]
            if step:
                self.copy(way, step - 1).wait_recv()
                total = total.astype(F32) + self.landed[(step - 1,) + part].astype(F32)
            if step <= last:
                self.held[(step,) + part] = total.astype(BF16)
                self.copy(way, step).start()
            else:
                self.out[part] = total.astype(self.out.dtype)
        if step > last:
            for way in range(2):
                for past in range(last + 1):
                    self.copy(way, past).wait_send()


class GroupGather:
    @staticmethod
    def scratch(span, parts=1):
        dma = pltpu.SemaphoreType.DMA
        return [dma((2, span, parts)), dma((2, span, parts)), dma((1,))]

    def __init__(self, where, block, out, sems, parts=1):
        self.where, self.block, self.out, self.parts = where, block, out, parts
        self.send, self.recv, self.own = sems
        self.steps = 3

    def rows(self, part):
        size = self.block.shape[0] // self.parts
        return pl.ds(part * size, size)

    def hop(self, dx, part):
        where, rows = self.where, self.rows(part)
        at = (0, dx, part)
        return remote(
            self.block.at[rows],
            self.out.at[0, dx, rows],
            self.send.at[at],
            self.recv.at[at],
            where.peer(0, where.span - dx),
        )

    def cross(self, dx, part):
        rows = self.rows(part)
        source = self.out.at[0, dx, rows] if dx else self.block.at[rows]
        at = (1, dx, part)
        return remote(
            source,
            self.out.at[1, dx, rows],
            self.send.at[at],
            self.recv.at[at],
            self.where.peer(1, 0),
        )

    def start(self, part):
        for dx in range(1, self.where.span):
            self.hop(dx, part).start()
        self.cross(0, part).start()

    def pass_on(self, part):
        for dx in range(1, self.where.span):
            self.hop(dx, part).wait_recv()
            self.cross(dx, part).start()

    def finish(self):
        for part in range(self.parts):
            for dx in range(self.where.span):
                if dx:
                    self.hop(dx, part).wait_send()
                self.cross(dx, part).wait()

    def keep(self):
        return pltpu.make_async_copy(self.block, self.out.at[0, 0], self.own.at[0])

    def run(self, step):
        if step == 0:
            self.keep().start()
            for part in range(self.parts):
                self.start(part)
        elif step == 1:
            for part in range(self.parts):
                self.pass_on(part)
        else:
            self.finish()
            self.keep().wait()


class GroupSwap:
    @staticmethod
    def scratch(span):
        dma = pltpu.SemaphoreType.DMA
        return [dma((2, span)), dma((2, span)), dma((1,))]

    def __init__(self, where, source, target, sems):
        self.where, self.source, self.target = where, source, target
        self.send, self.recv, self.own = sems
        self.steps = 2

    def run(self, step):
        where = self.where
        keep = pltpu.make_async_copy(self.source(0, 0), self.target(0, 0), self.own.at[0])
        copies = [
            remote(
                self.source(dc, dx),
                self.target(dc, dx),
                self.send.at[dc, dx],
                self.recv.at[dc, dx],
                where.peer(dc, dx),
            )
            for dx in reversed(range(where.span))
            for dc in range(2)
            if dc or dx
        ]
        if step == 0:
            for copy in copies:
                copy.start()
            keep.start()
        else:
            for copy in copies:
                copy.wait()
            keep.wait()


class GroupSum:
    @staticmethod
    def scratch(span, rows, columns):
        dma = pltpu.SemaphoreType.DMA
        slots = pltpu.VMEM((span, rows, columns), BF16)
        return [slots, slots, dma((span,)), dma((span,)), dma((span,)), dma((span,))]

    def __init__(self, where, terms, out, scratch):
        self.where, self.terms, self.out = where, terms, out
        self.crossed, self.landed, *sems = scratch
        self.send_core, self.recv_core, self.send, self.recv = sems
        self.steps = 3

    def cross(self, dx):
        return remote(
            self.terms.at[1, dx],
            self.crossed.at[dx],
            self.send_core.at[dx],
            self.recv_core.at[dx],
            self.where.peer(1, 0),
        )

    def hop(self, dx):
        return remote(
            self.crossed.at[dx],
            self.landed.at[dx],
            self.send.at[dx],
            self.recv.at[dx],
            self.where.peer(0, dx),
        )

    def fold(self, dx):
        self.cross(dx).wait_recv()
        total = self.terms[0, dx].astype(F32) + self.crossed[dx].astype(F32)
        self.crossed[dx] = total.astype(BF16)
        self.hop(dx).start()

    def finish(self):
        self.cross(0).wait_recv()
        total = self.terms[0, 0].astype(F32) + self.crossed[0].astype(F32)
        for dx in range(1, self.where.span):
            self.hop(dx).wait_recv()
            total = total + self.landed[dx].astype(F32)
        self.out[...] = total.astype(self.out.dtype)
        for dx in range(self.where.span):
            self.cross(dx).wait_send()
            if dx:
                self.hop(dx).wait_send()

    def run(self, step):
        later = list(reversed(range(self.where.span)))
        if step == 0:
            for dx in later:
                self.cross(dx).start()
        elif step == 1:
            for dx in later[:-1]:
                self.fold(dx)
        else:
            self.finish()


class CoreSum:
    @staticmethod
    def scratch(span, rows, columns):
        dma = pltpu.SemaphoreType.DMA
        return [pltpu.VMEM((span, rows, columns), BF16), dma((span,)), dma((span,))]

    def __init__(self, where, terms, out, scratch):
        self.where, self.terms, self.out = where, terms, out
        self.crossed, self.send_core, self.recv_core = scratch

    cross = GroupSum.cross

    def fold(self, dx):
        self.cross(dx).wait_recv()
        total = self.terms[0, dx].astype(F32) + self.crossed[dx].astype(F32)
        self.out[dx] = total.astype(BF16)

    def finish(self):
        for dx in range(self.where.span):
            self.cross(dx).wait_send()


class PatchSum:
    @staticmethod
    def scratch(span, rows, columns):
        dma = pltpu.SemaphoreType.DMA
        return [pltpu.VMEM((span, rows, columns), BF16), dma((span,)), dma((span,))]

    def __init__(self, where, terms, out, scratch):
        self.where, self.crossed, self.out = where, terms, out
        self.landed, self.send, self.recv = scratch
        self.steps = 2

    hop = GroupSum.hop

    def run(self, step):
        span = self.where.span
        if step == 0:
            for dx in range(1, span):
                self.hop(dx).start()
        else:
            total = self.crossed[0].astype(F32)
            for dx in range(1, span):
                self.hop(dx).wait_recv()
                total = total + self.landed[dx].astype(F32)
            self.out[...] = total
            for dx in range(1, span):
                self.hop(dx).wait_send()


class AllSum:
    @staticmethod
    def bits(sizes):
        found = []
        for axis in (2, 0, 1):
            bit = 1
            while bit < sizes[axis]:
                found.append((axis, bit))
                bit *= 2
        return found

    @staticmethod
    def scratch(sizes, rows):
        count = len(AllSum.bits(sizes))
        dma = pltpu.SemaphoreType.DMA
        slots = pltpu.VMEM((count, rows, 128), F32)
        return [slots, slots, dma((count,)), dma((count,))]

    def __init__(self, where, sizes, block, out, scratch):
        self.block, self.out = block, out
        self.held, self.landed, self.send, self.recv = scratch
        here = (where.ring, where.core, where.patch)
        self.peers = []
        for axis, bit in AllSum.bits(sizes):
            peer = list(here)
            peer[axis] = here[axis] + (1 - 2 * ((here[axis] // bit) % 2)) * bit
            self.peers.append(tuple(peer))
        self.steps = len(self.peers) + 1

    def copy(self, step):
        return remote(
            self.held.at[step],
            self.landed.at[step],
            self.send.at[step],
            self.recv.at[step],
            self.peers[step],
        )

    def run(self, step):
        if step == 0:
            total = self.block[...]
        else:
            self.copy(step - 1).wait()
            total = self.held[step - 1] + self.landed[step - 1]
        if step < len(self.peers):
            self.held[step] = total
            self.copy(step).start()
        else:
            self.out[...] = total


HBM = pl.BlockSpec(memory_space=pl.ANY)
CORE = pl.BlockSpec(memory_space=pltpu.VMEM)


def take(refs, counts):
    found, at = [], 0
    for count in counts:
        found.append(list(refs[at : at + count]))
        at += count
    return found


def flat_block(vector):
    rows = -(-vector.shape[0] // 1024) * 8
    return jnp.pad(vector, (0, rows * 128 - vector.shape[0])).reshape(rows, 128)


def entry_kernel(sizes, share, *refs):
    where = Where(sizes)
    size, group = where.size, 2 * where.span
    ins, outs, scratch = take(refs, (5, 5, len(refs) - 10))
    tokens, qkv_cols, up_cols, out_rows, vector = ins
    tokens_all, w_qkv, w_out, up_block, summed = outs
    lands, rest = scratch[:3], scratch[3:]
    wide, blocks = rest[:3], rest[3:5]
    sems = take(rest[5:], (3, 3, 3, 3, 3, 5, 4))
    greet(
        where.ring_peers() + where.group_peers() + AllSum(where, sizes, None, None, [0] * 4).peers
    )
    member = where.member

    def swap(source, land, job_sems):
        return GroupSwap(where, source, lambda dc, dx: land.at[member], job_sems)

    swaps = [
        swap(lambda dc, dx: qkv_cols.at[where.peer_member(dc, dx)], lands[0], sems[0]),
        swap(lambda dc, dx: out_rows, lands[1], sems[1]),
        swap(lambda dc, dx: up_cols.at[where.peer_member(dc, dx)], lands[2], sems[2]),
    ]
    gather = GroupGather(where, tokens, tokens_all, sems[3])
    ring_qkv = RingGather(where, blocks[0], w_qkv, sems[4])
    ring_out = RingGatherSplit(where, blocks[1], w_out, sems[5])
    sums = AllSum(where, sizes, vector, summed, sems[6])

    def join(at, block):
        for piece in range(group):
            wide[at][piece * share : (piece + 1) * share, :] = lands[at][piece].astype(F32)
        block[...] = wide[at][...].astype(BF16)

    swaps[0].run(0)
    sums.run(0)
    swaps[1].run(0)
    swaps[2].run(0)
    gather.run(0)
    swaps[0].run(1)
    join(0, blocks[0])
    ring_qkv.run(0)
    sums.run(1)
    swaps[1].run(1)
    join(1, blocks[1])
    ring_out.run(0)
    swaps[2].run(1)
    join(2, up_block)
    steps = max(ring_qkv.steps, ring_out.steps, sums.steps - 1)
    for step in range(1, steps):
        for job, at in ((ring_qkv, step), (ring_out, step), (sums, step + 1)):
            if at < job.steps:
                job.run(at)
        if step == steps - 2:
            gather.run(1)
    gather.run(2)


def entry(tokens, qkv_cols, up_cols, out_rows, vector, sizes, call_id):
    size, _, span = sizes
    group = 2 * span
    share = out_rows.shape[0]
    rows, width = tokens.shape
    block_rows = group * share
    columns = [qkv_cols.shape[2], width, up_cols.shape[2]]
    shape = jax.ShapeDtypeStruct
    scratch = [pltpu.VMEM((group, share, n), BF16) for n in columns]
    scratch += [pltpu.VMEM((block_rows, n), F32) for n in columns]
    scratch += [pltpu.VMEM((block_rows, n), BF16) for n in columns[:2]]
    scratch += GroupSwap.scratch(span) * 3
    scratch += GroupGather.scratch(span)
    scratch += RingGather.scratch(size)
    scratch += RingGatherSplit.scratch(size)
    scratch += AllSum.scratch(sizes, vector.shape[0])
    return pl.pallas_call(
        functools.partial(entry_kernel, sizes, share),
        out_shape=[
            shape((2, span, rows, width), BF16),
            shape((size, block_rows, columns[0]), BF16),
            shape((size, block_rows, width), BF16),
            shape((block_rows, columns[2]), BF16),
            shape(vector.shape, F32),
        ],
        in_specs=[HBM, HBM, HBM, HBM, CORE],
        out_specs=[HBM, HBM, HBM, CORE, CORE],
        scratch_shapes=scratch,
        compiler_params=pltpu.CompilerParams(
            collective_id=call_id, has_side_effects=True, vmem_limit_bytes=32 * MIB
        ),
        name="entry",
    )(tokens, qkv_cols, up_cols, out_rows, vector)


def exchange_kernel(sizes, kinds, counts, order, *refs):
    where = Where(sizes)
    ins, outs, scratch = take(refs, (len(kinds), len(kinds), len(refs) - 2 * len(kinds)))
    scratch = take(scratch, counts)
    jobs, peers = [], []
    for kind, source, out, own in zip(kinds, ins, outs, scratch):
        if kind is AllSum:
            jobs.append(AllSum(where, sizes, source, out, own))
            peers += jobs[-1].peers
        else:
            jobs.append(kind(where, source, out, own))
    if any(kind in (RingGather, RingSum, RingGatherSplit) for kind in kinds):
        peers += where.ring_peers()
    if any(kind in (GroupGather, GroupSum, RingGatherSplit) for kind in kinds):
        peers += where.group_peers()
    greet(peers)
    for step in range(max(job.steps for job in jobs)):
        for job in jobs:
            if step < job.steps:
                job.run(step)


def exchange(jobs, sizes, call_id):
    size, _, span = sizes
    kinds, arrays, outs, scratch, counts, spaces = [], [], [], [], [], []
    shape = jax.ShapeDtypeStruct
    for kind, array, *dtype in jobs:
        kinds.append(kind)
        arrays.append(array)
        inside = True
        if kind is RingSum:
            outs.append(shape(array.shape[1:], dtype[0]))
            own = RingSum.scratch(size, *array.shape[1:])
        elif kind is GroupSum:
            outs.append(shape(array.shape[2:], dtype[0]))
            own = GroupSum.scratch(span, *array.shape[2:])
        elif kind is AllSum:
            outs.append(shape(array.shape, F32))
            own = AllSum.scratch(sizes, array.shape[0])
        elif kind is GroupGather:
            outs.append(shape((2, span) + array.shape, array.dtype))
            own, inside = GroupGather.scratch(span), False
        else:
            outs.append(shape((size,) + array.shape, array.dtype))
            own, inside = kind.scratch(size), False
        scratch += own
        counts.append(len(own))
        spaces.append(CORE if inside else HBM)
    return pl.pallas_call(
        functools.partial(exchange_kernel, sizes, tuple(kinds), tuple(counts), None),
        out_shape=outs,
        in_specs=spaces,
        out_specs=spaces,
        scratch_shapes=scratch,
        compiler_params=pltpu.CompilerParams(
            collective_id=call_id, has_side_effects=True, vmem_limit_bytes=48 * MIB
        ),
        name=f"exchange_{call_id}",
    )(*arrays)


def along_grid(jobs, total, before):
    at = pl.program_id(0) * pl.num_programs(1) + pl.program_id(1)
    if before:
        for grid in range(total):
            todo = [(job, grid) for job in jobs if grid < job.steps - 1]
            if todo:

                @pl.when(at == grid)
                def _():
                    for job, step in todo:
                        job.run(step)

    else:

        @pl.when(at == total - 1)
        def _():
            for job in jobs:
                for step in range(min(total, job.steps - 1), job.steps):
                    job.run(step)


def attention_kernel(sizes, factor, chunk, total, *refs):
    where = Where(sizes)
    ins, outs, scratch = take(refs, (5, 4, len(refs) - 9))
    q_ref, k_ref, v_ref, up_block, grad_block = ins
    out_ref, lse_ref, w_up, grad_all = outs
    sems = take(scratch, (3, 3))
    jobs = [
        RingGather(where, up_block, w_up, sems[0]),
        GroupGather(where, grad_block, grad_all, sems[1]),
    ]
    at = pl.program_id(0) * pl.num_programs(1) + pl.program_id(1)

    @pl.when(at == 0)
    def _():
        greet(where.ring_peers() + where.group_peers())

    along_grid(jobs[:1], total, True)

    @pl.when(at == 0)
    def _():
        jobs[1].run(0)

    keys = k_ref[0].T
    values_t = v_ref[0]
    for start in range(0, q_ref.shape[2], chunk):
        span = slice(start, start + chunk)
        scores = jnp.dot(keys, q_ref[0, :, span], preferred_element_type=F32) * factor
        top = jnp.max(scores, axis=0, keepdims=True)
        probs = jnp.exp2(scores - top)
        row_sum = jnp.sum(probs, axis=0, keepdims=True)
        mixed = jnp.dot(values_t, probs.astype(BF16), preferred_element_type=F32)
        out_ref[0, :, span] = (mixed / row_sum).astype(BF16)
        lse_ref[0, :, span] = top + jnp.log2(row_sum)

    along_grid(jobs[:1], total, False)

    @pl.when(at == total - 1)
    def _():
        jobs[1].run(1)
        jobs[1].run(2)


def attention(qkv, up_block, grad_block, patches, sizes, call_id):
    size, _, span = sizes
    triple, dim, tokens = qkv.shape
    heads = triple // 3
    frames = tokens // patches
    block = (1, dim, patches)
    factor = LOG2E / math.sqrt(HEAD_DIM)
    shape = jax.ShapeDtypeStruct
    return pl.pallas_call(
        functools.partial(attention_kernel, sizes, factor, min(256, patches), frames * heads),
        out_shape=[
            shape((heads, dim, tokens), BF16),
            shape((heads, 1, tokens), F32),
            shape((size,) + up_block.shape, BF16),
            shape((2, span) + grad_block.shape, BF16),
        ],
        grid=(frames, heads),
        in_specs=[
            pl.BlockSpec(block, lambda f, h: (h, 0, f)),
            pl.BlockSpec(block, lambda f, h: (heads + h, 0, f)),
            pl.BlockSpec(block, lambda f, h: (2 * heads + h, 0, f)),
            HBM,
            HBM,
        ],
        out_specs=[
            pl.BlockSpec(block, lambda f, h: (h, 0, f)),
            pl.BlockSpec((1, 1, patches), lambda f, h: (h, 0, f)),
            HBM,
            HBM,
        ],
        scratch_shapes=RingGather.scratch(size) + GroupGather.scratch(span),
        compiler_params=pltpu.CompilerParams(
            collective_id=call_id, has_side_effects=True, vmem_limit_bytes=32 * MIB
        ),
        cost_estimate=pl.CostEstimate(
            flops=4 * heads * patches * tokens * 256,
            bytes_accessed=4 * heads * dim * tokens * 2,
            transcendentals=heads * patches * tokens,
        ),
        name="attention",
    )(qkv, qkv, qkv, up_block, grad_block)


def attention_back_kernel(sizes, factor, chunk, total, *refs):
    where = Where(sizes)
    ins, outs, scratch = take(refs, (7, 5, len(refs) - 12))
    q_ref, k_ref, v_ref, g_ref, lse_ref, up_terms, half_terms = ins
    dq_ref, dk_ref, dv_ref, up_sum, half_sum = outs
    dk_sum, dv_sum = scratch[:2]
    own = take(scratch[2:], (4, 3))
    ring_up = RingSum(where, up_terms, up_sum, own[0])
    half = PatchSum(where, half_terms, half_sum, own[1])
    at = pl.program_id(0) * pl.num_programs(1) + pl.program_id(1)

    @pl.when(at == 0)
    def _():
        greet(where.ring_peers() + where.group_peers())
        half.run(0)

    along_grid([ring_up], total, True)

    keys_t = k_ref[0]
    keys = keys_t.T
    values = v_ref[0].T
    scale = factor / LOG2E
    patches = q_ref.shape[2]
    for start in range(0, patches, chunk):
        span = slice(start, start + chunk)
        queries_t = q_ref[0, :, span]
        grad_t = g_ref[0, :, span]
        scores = jnp.dot(keys, queries_t, preferred_element_type=F32) * factor
        probs = jnp.exp2(scores - lse_ref[0, :, span])
        grad_probs = jnp.dot(values, grad_t, preferred_element_type=F32)
        row_dot = jnp.sum(probs * grad_probs, axis=0, keepdims=True)
        grad_scores = (probs * (grad_probs - row_dot)).astype(BF16)
        probs_low = probs.astype(BF16)
        dq = jnp.dot(keys_t, grad_scores, preferred_element_type=F32)
        dq_ref[0, :, span] = (dq * scale).astype(BF16)
        dims = (((1,), (1,)), ((), ()))
        dk = lax.dot_general(queries_t, grad_scores, dims, preferred_element_type=F32)
        dv = lax.dot_general(grad_t, probs_low, dims, preferred_element_type=F32)
        if start == 0:
            dk_sum[...] = dk
            dv_sum[...] = dv
        else:
            dk_sum[...] += dk
            dv_sum[...] += dv
    dk_ref[0] = (dk_sum[...] * scale).astype(BF16)
    dv_ref[0] = dv_sum[...].astype(BF16)

    along_grid([ring_up], total, False)

    @pl.when(at == total - 1)
    def _():
        half.run(1)


def attention_back(qkv, grad, lse, up_terms, half_terms, patches, sizes, call_id):
    size, _, span = sizes
    triple, dim, tokens = qkv.shape
    heads = triple // 3
    frames = tokens // patches
    block = (1, dim, patches)
    factor = LOG2E / math.sqrt(HEAD_DIM)
    spec = pl.BlockSpec(block, lambda f, h: (h, 0, f))
    shape = jax.ShapeDtypeStruct
    grads = shape((heads, dim, tokens), BF16)
    *parts, up_sum, half_sum = pl.pallas_call(
        functools.partial(attention_back_kernel, sizes, factor, min(256, patches), frames * heads),
        out_shape=[grads] * 3
        + [shape(up_terms.shape[1:], BF16), shape(half_terms.shape[1:], F32)],
        grid=(frames, heads),
        in_specs=[
            spec,
            pl.BlockSpec(block, lambda f, h: (heads + h, 0, f)),
            pl.BlockSpec(block, lambda f, h: (2 * heads + h, 0, f)),
            spec,
            pl.BlockSpec((1, 1, patches), lambda f, h: (h, 0, f)),
            CORE,
            CORE,
        ],
        out_specs=[spec] * 3 + [CORE, CORE],
        scratch_shapes=[pltpu.VMEM((dim, patches), F32)] * 2
        + RingSum.scratch(size, *up_terms.shape[1:])
        + PatchSum.scratch(span, *half_terms.shape[1:]),
        compiler_params=pltpu.CompilerParams(
            collective_id=call_id, has_side_effects=True, vmem_limit_bytes=48 * MIB
        ),
        cost_estimate=pl.CostEstimate(
            flops=10 * heads * patches * tokens * 256,
            bytes_accessed=8 * heads * dim * tokens * 2,
            transcendentals=heads * patches * tokens,
        ),
        name="attention_back",
    )(qkv, qkv, qkv, grad, lse, up_terms, half_terms)
    return jnp.concatenate(parts, axis=0), up_sum, half_sum


def joined(array):
    group, features, count = array.shape
    if features % 16:
        return array.astype(F32).reshape(group * features, count).astype(BF16)
    return array.reshape(group * features, count)


def middle_kernel(sizes, parts, *refs):
    where = Where(sizes)
    ins, outs, scratch = take(refs, (5, 5, len(refs) - 10))
    heads_t, w_out, tokens, vectors, down_block = ins
    attended, branch, midway, hidden_all, w_down = outs
    hidden = scratch[0]
    sems = take(scratch[1:], (3, 3, 3))
    greet(where.ring_peers() + where.group_peers())
    rows, width = tokens.shape
    span = where.span

    swap = GroupSwap(
        where,
        lambda dc, dx: heads_t.at[:, pl.ds((dc * span + dx) * rows, rows)],
        lambda dc, dx: attended.at[where.member],
        sems[0],
    )
    ring = RingGather(where, down_block, w_down, sems[1])
    gather = GroupGather(where, hidden, hidden_all, sems[2], parts)
    swap.run(0)
    for step in range(4):
        ring.run(step)
    swap.run(1)
    size = rows // parts
    for part in range(parts):
        span_rows = slice(part * size, (part + 1) * size)
        mixed = joined(attended[:, :, span_rows])
        one = lax.dot_general(
            mixed, w_out[...], (((0,), (0,)), ((), ())), preferred_element_type=F32
        )
        one = one + vectors[0:1, :]
        branch[span_rows, :] = one
        mid = tokens[span_rows, :].astype(F32) + vectors[1:2, :] * one
        midway[span_rows, :] = mid
        normed, _ = layer_norm(mid)
        hidden[span_rows, :] = (normed * (1.0 + vectors[2:3, :]) + vectors[3:4, :]).astype(BF16)
        gather.start(part)
    for step in range(4, ring.steps):
        ring.run(step)
    for part in range(parts):
        gather.pass_on(part)
    gather.finish()
    gather.keep().start()
    gather.keep().wait()


def middle(heads_t, w_out, tokens, vectors, down_block, sizes, call_id):
    size, _, span = sizes
    rows, width = tokens.shape
    parts = rows // 128
    shape = jax.ShapeDtypeStruct
    return pl.pallas_call(
        functools.partial(middle_kernel, sizes, parts),
        out_shape=[
            shape((2 * span, heads_t.shape[0], rows), BF16),
            shape((rows, width), F32),
            shape((rows, width), F32),
            shape((2, span, rows, width), BF16),
            shape((size,) + down_block.shape, BF16),
        ],
        in_specs=[CORE, CORE, CORE, CORE, HBM],
        out_specs=[CORE, CORE, CORE, HBM, HBM],
        scratch_shapes=[pltpu.VMEM((rows, width), BF16)]
        + GroupSwap.scratch(span)
        + RingGather.scratch(size)
        + GroupGather.scratch(span, parts),
        compiler_params=pltpu.CompilerParams(
            collective_id=call_id, has_side_effects=True, vmem_limit_bytes=40 * MIB
        ),
        name="middle",
    )(heads_t, w_out, tokens, vectors, down_block)


def gelu_both(values_in):
    square = values_in * values_in
    inner = 0.7978845608028654 * values_in * (1.0 + 0.044715 * square)
    bent = jnp.tanh(inner)
    outer = 0.5 * (1.0 + bent)
    slope = 0.7978845608028654 * (1.0 + 3.0 * 0.044715 * square)
    return values_in * outer, outer + 0.5 * values_in * (1.0 - bent * bent) * slope


def feed_kernel(sizes, chunk, tile, *refs):
    where = Where(sizes)
    ins, outs, scratch = take(refs, (5, 5, len(refs) - 10))
    hidden, grad, w_up, w_down, bias = ins
    half, grad_hidden, g_up, g_down, g_bias = outs
    act, grad_pre, branch, back = scratch[:4]
    own = take(scratch[4:], (3, 6))
    span = where.span
    rows, width = grad_hidden.shape
    units = bias.shape[1]
    sum_half = CoreSum(where, branch, half, own[0])
    sum_back = GroupSum(where, back, grad_hidden, own[1])
    greet(where.group_peers())
    each = rows // chunk
    across = (((1,), (1,)), ((), ()))

    def body(step, total):
        at = step // each
        dx, dc = span - 1 - at // 2, 1 - at % 2
        inside = pl.ds(pl.multiple_of(step % each * chunk, chunk), chunk)
        first = pl.multiple_of((dc * span + dx) * rows + step % each * chunk, chunk)
        here = pl.ds(first, chunk)
        pre = jnp.dot(hidden[here, :], w_up[...], preferred_element_type=F32) + bias[...]
        value, slope = gelu_both(pre)
        value = value.astype(BF16)
        act[here, :] = value
        grad_act = lax.dot_general(grad[here, :], w_down[...], across, preferred_element_type=F32)
        low = (grad_act * slope).astype(BF16)
        grad_pre[here, :] = low
        back[dc, dx, inside, :] = lax.dot_general(
            low, w_up[...], across, preferred_element_type=F32
        ).astype(BF16)
        branch[dc, dx, inside, :] = jnp.dot(
            value, w_down[...], preferred_element_type=F32
        ).astype(BF16)
        for place in range(2 * span):
            done_dx, done_dc = span - 1 - place // 2, 1 - place % 2

            @pl.when(step == (place + 1) * each - 1)
            def _():
                if done_dc:
                    sum_back.cross(done_dx).start()
                    sum_half.cross(done_dx).start()
                elif done_dx:
                    sum_back.fold(done_dx)
                    sum_half.fold(done_dx)

        return total + jnp.sum(low.astype(F32), axis=0, keepdims=True)

    zero = jnp.zeros((1, units), F32)
    g_bias[...] = lax.fori_loop(0, 2 * span * each, body, zero)
    sum_half.fold(0)
    over = (((0,), (0,)), ((), ()))
    for low in range(0, units, tile):
        cut = slice(low, low + tile)
        g_down[cut, :] = lax.dot_general(
            act[:, cut], grad[...], over, preferred_element_type=F32
        ).astype(BF16)
        g_up[:, cut] = lax.dot_general(
            hidden[...], grad_pre[:, cut], over, preferred_element_type=F32
        ).astype(BF16)
    sum_half.finish()
    sum_back.finish()


def feed(hidden, grad, w_up, w_down, bias, sizes, call_id):
    _, _, span = sizes
    tokens, width = hidden.shape
    units = w_up.shape[1]
    rows = tokens // (2 * span)
    shape = jax.ShapeDtypeStruct
    terms = pltpu.VMEM((2, span, rows, width), BF16)
    return pl.pallas_call(
        functools.partial(feed_kernel, sizes, min(256, rows), 384 if units % 384 == 0 else units),
        out_shape=[
            shape((span, rows, width), BF16),
            shape((rows, width), F32),
            shape((width, units), BF16),
            shape((units, width), BF16),
            shape((1, units), F32),
        ],
        in_specs=[CORE] * 5,
        out_specs=[CORE] * 5,
        scratch_shapes=[pltpu.VMEM((tokens, units), BF16)] * 2
        + [terms] * 2
        + CoreSum.scratch(span, rows, width)
        + GroupSum.scratch(span, rows, width),
        compiler_params=pltpu.CompilerParams(
            collective_id=call_id, has_side_effects=True, vmem_limit_bytes=60 * MIB
        ),
        name="feed",
    )(hidden, grad, w_up, w_down, bias)


def from_patch(array, hops, size):
    if hops == 0:
        return array
    return lax.ppermute(array, "patch", [((to + hops) % size, to) for to in range(size)])


def from_core(array):
    return lax.ppermute(array, "core", [(0, 1), (1, 0)])


def group_swap(pieces, size):
    out = []
    for dc in range(2):
        row = []
        for dx in range(size):
            piece = pieces[dc][(size - dx) % size]
            piece = from_patch(piece, dx, size)
            row.append(from_core(piece) if dc else piece)
        out.append(row)
    return out


def natural(pieces, size):
    core, patch = lax.axis_index("core"), lax.axis_index("patch")
    if size == 2:
        swapped = [
            [jnp.where(patch == 0, row[0], row[1]), jnp.where(patch == 0, row[1], row[0])]
            for row in pieces
        ]
    else:
        swapped = []
        for row in pieces:
            stack = jnp.stack(row)
            swapped.append(
                [
                    lax.dynamic_index_in_dim(stack, (to - patch + size) % size, 0, False)
                    for to in range(size)
                ]
            )
    first = [jnp.where(core == 0, a, b) for a, b in zip(swapped[0], swapped[1])]
    second = [jnp.where(core == 0, b, a) for a, b in zip(swapped[0], swapped[1])]
    return first + second


def relative(blocks, size):
    core, patch = lax.axis_index("core"), lax.axis_index("patch")
    return [
        [
            lax.dynamic_index_in_dim(
                blocks, (core + dc) % 2 * size + (patch + dx) % size, 0, False
            )
            for dx in range(size)
        ]
        for dc in range(2)
    ]


def per_device(
    tokens,
    cotangent,
    clip_embed,
    timesteps,
    frame_clip,
    ada_weight,
    ada_bias,
    qkv_weight,
    query_bias,
    value_bias,
    out_weight,
    out_bias,
    up_weight,
    up_bias,
    down_weight,
    down_bias,
):
    ring_size, patch_size = lax.axis_size("ring"), lax.axis_size("patch")
    sizes = (ring_size, 2, patch_size)
    group = 2 * patch_size
    device_count = ring_size * group
    ring, core, patch = (lax.axis_index(name) for name in ("ring", "core", "patch"))
    member = core * patch_size + patch
    device = ring * group + member
    rows, width = tokens.shape[1:]
    tokens, cotangent = tokens[0], cotangent[0]
    patches = patch_size * rows
    clips = clip_embed.shape[0]
    hidden = up_weight.shape[1]
    share = width // device_count
    heads = HEADS // group
    head_width = heads * HEAD_DIM
    units = hidden // group
    mine = jnp.arange(group) == member
    mine_of_all = jnp.arange(device_count) == device

    qkv_cols = jnp.transpose(qkv_weight.reshape(share, 3, group, head_width), (2, 0, 1, 3)).reshape(
        group, share, 3 * head_width
    )
    up_cols = jnp.transpose(
        up_weight.reshape(share, ring_size, group, hidden // device_count), (2, 0, 1, 3)
    ).reshape(group, share, units)

    condition = clip_embed + sinusoid(timesteps, width)
    silu_cond, silu_back = jax.vjp(jax.nn.silu, condition)
    silu_low = silu_cond.astype(BF16)
    silu_part = lax.dynamic_slice_in_dim(silu_low, device * share, share, 1)
    mod_part = jnp.dot(silu_part, ada_weight, preferred_element_type=F32)
    shards = [ada_bias, query_bias, value_bias, out_bias, down_bias, up_bias]
    lengths = [shard.shape[0] for shard in shards]
    shards = jnp.concatenate(shards).astype(F32)
    placed = jnp.where(mine_of_all[:, None], shards[None, :], 0.0).reshape(-1)
    frame_count = 2 * ring_size
    own_frame = 2 * ring + core
    clip_part = jnp.where(
        (jnp.arange(frame_count) == own_frame) & (patch == 0), frame_clip[0].astype(F32), 0.0
    )
    vector = jnp.concatenate([mod_part.reshape(-1), placed, clip_part])

    tokens_all, w_qkv, w_out, up_block, summed = entry(
        tokens, qkv_cols, up_cols, out_weight, flat_block(vector), sizes, 1
    )
    w_qkv = w_qkv.reshape(width, 3 * head_width)
    w_out = w_out.reshape(width, width)
    summed = summed.reshape(-1)
    split = clips * 6 * width
    full = summed[split : split + placed.shape[0]].reshape(device_count, -1)
    found, at = [], 0
    for length in lengths:
        found.append(full[:, at : at + length].reshape(-1))
        at += length
    ada_full, query_full, value_full, b_out, b_down, up_full = found
    modulation = summed[:split].reshape(clips, 6 * width) + ada_full[None, :]
    clips_of = summed[split + placed.shape[0] :][:frame_count]
    b_query = lax.dynamic_slice_in_dim(query_full, member * head_width, head_width, 0)
    b_value = lax.dynamic_slice_in_dim(value_full, member * head_width, head_width, 0)
    b_up = lax.dynamic_index_in_dim(
        up_full.reshape(ring_size, group, hidden // device_count), member, 1, False
    ).reshape(units)
    own_clip = frame_clip[0]
    other_clip = lax.dynamic_index_in_dim(clips_of, 2 * ring + 1 - core, 0, False).astype(jnp.int32)
    own_mod = lax.dynamic_index_in_dim(modulation, own_clip, 0, False)
    other_mod = lax.dynamic_index_in_dim(modulation, other_clip, 0, False)
    shift_one, scale_one, gate_one, shift_two, scale_two, gate_two = (
        own_mod[at * width : (at + 1) * width] for at in range(6)
    )
    both = jnp.stack([own_mod[: 2 * width], other_mod[: 2 * width]])[:, None, :]

    normed_all, _ = layer_norm(tokens_all.astype(F32).reshape(2, patches, width))
    hidden_one = (
        (normed_all * (1.0 + both[:, :, width:]) + both[:, :, :width])
        .astype(BF16)
        .reshape(2 * patches, width)
    )
    qkv_bias = jnp.concatenate([b_query, jnp.zeros_like(b_query), b_value])
    projected = (
        lax.dot_general(w_qkv, hidden_one, (((0,), (1,)), ((), ())), preferred_element_type=F32)
        + qkv_bias[:, None]
    ).astype(BF16)
    qkv = projected.reshape(3 * heads, HEAD_DIM, 2 * patches)
    grad_out = cotangent.astype(F32)
    grad_branch_two = (gate_two * grad_out).astype(BF16)
    attended_t, lse, w_up, gb_two_all = attention(
        qkv, up_block, grad_branch_two, patches, sizes, 2
    )
    w_up = w_up.reshape(width, units)

    vectors = jnp.stack([b_out, gate_one, scale_two, shift_two] + [b_out] * 4)
    attended, branch_one, midway, hidden_two_all, w_down = middle(
        attended_t.reshape(head_width, 2 * patches), w_out, tokens, vectors, down_weight, sizes, 3
    )
    attended = attended.reshape(width, rows)
    w_down = w_down.reshape(units, width)

    branch_half, grad_hidden_two, g_up, g_down, g_up_b = feed(
        hidden_two_all.reshape(2 * patches, width),
        gb_two_all.reshape(2 * patches, width),
        w_up,
        w_down,
        b_up[None, :],
        sizes,
        4,
    )
    g_up_b = g_up_b[0]
    g_down_b = jnp.sum(grad_branch_two.astype(F32), axis=0)
    block_rows = width // ring_size
    (share_down,) = exchange(
        [(RingSum, g_down.reshape(ring_size, units // ring_size, width), F32)], sizes, 5
    )

    input_rows = tokens.astype(F32)
    normed_two, inv_two = layer_norm(midway)
    grad_shift_two = jnp.sum(grad_hidden_two, axis=0)
    grad_scale_two = jnp.sum(grad_hidden_two * normed_two, axis=0)
    grad_midway = grad_out + norm_back(grad_hidden_two * (1.0 + scale_two), normed_two, inv_two)
    grad_gate_one = jnp.sum(grad_midway * branch_one, axis=0)
    grad_branch_one = (gate_one * grad_midway).astype(BF16)
    g_out_b = jnp.sum(grad_branch_one.astype(F32), axis=0)
    grad_attended = lax.dot_general(
        w_out, grad_branch_one, (((1,), (1,)), ((), ())), preferred_element_type=F32
    ).astype(BF16)
    g_out = jnp.dot(attended, grad_branch_one, preferred_element_type=F32).astype(BF16)
    swapped = group_swap(
        relative(grad_attended.reshape(group, head_width, rows), patch_size), patch_size
    )
    grad_mix = jnp.concatenate([piece for row in swapped for piece in row], axis=1)
    grad_projected, sum_up, branch_two = attention_back(
        qkv,
        grad_mix.reshape(heads, HEAD_DIM, 2 * patches),
        lse,
        g_up.reshape(ring_size, block_rows, units),
        branch_half,
        patches,
        sizes,
        6,
    )
    grad_projected = grad_projected.reshape(3 * head_width, 2 * patches)
    branch_two = branch_two + b_down
    output = (midway + gate_two * branch_two).astype(BF16)
    grad_gate_two = jnp.sum(grad_out * branch_two, axis=0)

    g_qkv = lax.dot_general(
        hidden_one, grad_projected, (((0,), (1,)), ((), ())), preferred_element_type=F32
    ).astype(BF16)
    g_query_b = jnp.sum(grad_projected[:head_width].astype(F32), axis=1)
    g_value_b = jnp.sum(grad_projected[2 * head_width :].astype(F32), axis=1)
    grad_hidden_terms = lax.dot_general(
        grad_projected, w_qkv, (((0,), (1,)), ((), ())), preferred_element_type=F32
    ).astype(BF16)
    grad_hidden_one, sum_qkv, sum_out = exchange(
        [
            (GroupSum, grad_hidden_terms.reshape(2, patch_size, rows, width), F32),
            (RingSum, g_qkv.reshape(ring_size, block_rows, -1), BF16),
            (RingSum, g_out.reshape(ring_size, block_rows, width), BF16),
        ],
        sizes,
        7,
    )

    normed_one, inv_one = layer_norm(input_rows)
    grad_shift_one = jnp.sum(grad_hidden_one, axis=0)
    grad_scale_one = jnp.sum(grad_hidden_one * normed_one, axis=0)
    tokens_grad = (
        grad_midway + norm_back(grad_hidden_one * (1.0 + scale_one), normed_one, inv_one)
    ).astype(BF16)

    pieces = jnp.concatenate([sum_qkv, sum_up, sum_out], axis=1).reshape(group, share, -1)
    got_w = natural(group_swap(relative(pieces, patch_size), patch_size), patch_size)
    stacked = jnp.stack(got_w).astype(F32)
    share_qkv = jnp.transpose(
        stacked[:, :, : 3 * head_width].reshape(group, share, 3, head_width), (1, 2, 0, 3)
    ).reshape(share, 3 * width)
    share_up = jnp.transpose(
        stacked[:, :, 3 * head_width : 3 * head_width + units].reshape(
            group, share, ring_size, hidden // device_count
        ),
        (1, 2, 0, 3),
    ).reshape(share, hidden)
    share_out = jnp.sum(stacked[:, :, 3 * head_width + units :], axis=0)

    frame_grads = jnp.concatenate(
        [
            grad_shift_one,
            grad_scale_one,
            grad_gate_one,
            grad_shift_two,
            grad_scale_two,
            grad_gate_two,
        ]
    )
    clip_terms = jnp.where(
        (jnp.arange(clips) == own_clip)[:, None], frame_grads[None, :], 0.0
    ).reshape(-1)
    terms = [
        clip_terms,
        jnp.where(mine[:, None], g_query_b[None, :], 0.0).reshape(-1),
        jnp.where(mine[:, None], g_value_b[None, :], 0.0).reshape(-1),
        g_out_b,
        g_down_b,
        jnp.where(mine[None, :, None], g_up_b.reshape(ring_size, 1, -1), 0.0).reshape(-1),
    ]
    (summed,) = exchange([(AllSum, flat_block(jnp.concatenate(terms)))], sizes, 8)
    summed = summed.reshape(-1)
    got, at = [], 0
    for item in terms:
        got.append(summed[at : at + item.shape[0]])
        at += item.shape[0]
    mod_low = got[0].reshape(clips, 6 * width).astype(BF16)

    def own(vector):
        length = vector.shape[0] // device_count
        return lax.dynamic_slice_in_dim(vector, device * length, length, 0)

    ada_bias_grad = own(jnp.sum(mod_low.astype(F32), axis=0))
    ada_weight_grad = lax.dot_general(
        silu_part, mod_low, (((0,), (0,)), ((), ())), preferred_element_type=F32
    )
    grad_silu_part = lax.dot_general(
        mod_low, ada_weight, (((1,), (1,)), ((), ())), preferred_element_type=F32
    )
    spread = jnp.where(mine_of_all[None, :, None], grad_silu_part[:, None, :], 0.0).reshape(-1)
    (grad_silu,) = exchange([(AllSum, flat_block(spread))], sizes, 9)
    grad_silu = grad_silu.reshape(-1)[: clips * width].reshape(clips, width)
    clip_grad = silu_back(grad_silu)[0]
    return (
        output[None],
        tokens_grad[None],
        clip_grad,
        ada_weight_grad,
        ada_bias_grad,
        share_qkv,
        own(got[1]),
        own(got[2]),
        share_out,
        own(got[3]),
        share_up,
        own(got[5]),
        share_down,
        own(got[4]),
    )


def solution(mesh):
    frames, patch = mesh.shape["frames"], mesh.shape["patch"]
    inner = Mesh(mesh.devices.reshape(frames // 2, 2, patch), ("ring", "core", "patch"))
    every = ("ring", "core", "patch")
    tokens = P(("ring", "core"), "patch", None)
    matrix = P(every, None)
    vector = P(every)
    return jax.shard_map(
        per_device,
        mesh=inner,
        in_specs=(
            tokens,
            tokens,
            P(),
            P(),
            P(("ring", "core")),
            matrix,
            vector,
            matrix,
            vector,
            vector,
            matrix,
            vector,
            matrix,
            vector,
            matrix,
            vector,
        ),
        out_specs=(
            tokens,
            tokens,
            P(),
            matrix,
            vector,
            matrix,
            vector,
            vector,
            matrix,
            vector,
            matrix,
            vector,
            matrix,
            vector,
        ),
        check_vma=False,
    )
```

```python
import functools
import math

import jax
import jax.numpy as jnp
from jax import lax
from jax.experimental import pallas as pl
from jax.experimental.pallas import tpu as pltpu
from jax.sharding import Mesh
from jax.sharding import PartitionSpec as P

HEADS = 16
HEAD_DIM = 72
BF16 = jnp.bfloat16
F32 = jnp.float32
LOG2E = 1.4426950408889634
MESH_ID = pl.DeviceIdType.MESH
MIB = 2**20


def layer_norm(values_in):
    centre = values_in - jnp.mean(values_in, axis=-1, keepdims=True)
    spread = jnp.mean(centre * centre, axis=-1, keepdims=True)
    inv_std = lax.rsqrt(spread + 1e-06)
    return (centre * inv_std, inv_std)


def norm_back(grad_normed, normed, inv_std):
    mean_grad = jnp.mean(grad_normed, axis=-1, keepdims=True)
    mean_prod = jnp.mean(grad_normed * normed, axis=-1, keepdims=True)
    return (grad_normed - mean_grad - normed * mean_prod) * inv_std


def gelu_tanh(values_in):
    inner = 0.7978845608028654 * (values_in + 0.044715 * values_in * values_in * values_in)
    return 0.5 * values_in * (1.0 + jnp.tanh(inner))


def sinusoid(steps_in, width_in):
    half_width = width_in // 2
    freqs = jnp.exp(-math.log(10000.0) * jnp.arange(half_width, dtype=jnp.float32) / half_width)
    angles = steps_in.astype(jnp.float32)[:, None] * freqs[None, :]
    return jnp.concatenate([jnp.cos(angles), jnp.sin(angles)], axis=1)


class Where:
    def __init__(self, sizes):
        self.size, _, self.span = sizes
        self.ring, self.core, self.patch = (
            lax.axis_index(name) for name in ("ring", "core", "patch")
        )
        along, across = self.ring // 2, self.ring % 2
        self.place = (1 - across) * along + across * (self.size - 1 - along)
        self.member = self.core * self.span + self.patch

    def at_place(self, place):
        place = (place + 2 * self.size) % self.size
        back = place // (self.size // 2)
        return (1 - back) * 2 * place + back * (2 * (self.size - 1 - place) + 1)

    def neighbour(self, step):
        return (self.at_place(self.place + step), self.core, self.patch)

    def peer(self, dc, dx):
        core = 1 - self.core if dc else self.core
        return (self.ring, core, (self.patch + dx) % self.span)

    def peer_member(self, dc, dx):
        _, core, patch = self.peer(dc, dx)
        return core * self.span + patch

    def ring_peers(self):
        return [self.neighbour(1), self.neighbour(-1)]

    def group_peers(self):
        return [
            self.peer(dc, dx) for dc in range(2) for dx in range(self.span) if dc or dx
        ]


def greet(peers):
    barrier = pltpu.get_barrier_semaphore()
    for peer in peers:
        pl.semaphore_signal(barrier, inc=1, device_id=peer, device_id_type=MESH_ID)
    pl.semaphore_wait(barrier, len(peers))


def remote(source, target, send_sem, recv_sem, peer):
    return pltpu.make_async_remote_copy(
        src_ref=source,
        dst_ref=target,
        send_sem=send_sem,
        recv_sem=recv_sem,
        device_id=peer,
        device_id_type=MESH_ID,
    )


def strands(rows, columns):
    by_rows = rows % 16 == 0
    tile = 16 if by_rows else 128
    tiles = (rows if by_rows else columns) // tile
    sizes = [tiles // 4 + (at < tiles % 4) for at in range(4)]
    found, low = [], 0
    for at, count in enumerate(sizes):
        cut = pl.ds(low * tile, count * tile)
        found.append((at // 2, (cut, slice(None)) if by_rows else (slice(None), cut)))
        low += count
    return found


class RingGather:
    @staticmethod
    def scratch(size):
        dma = pltpu.SemaphoreType.DMA
        return [dma((4, size - 1)), dma((4, size - 1)), dma((1,))]

    def __init__(self, where, block, out, sems):
        self.where, self.block, self.out = where, block, out
        self.send, self.recv, self.own = sems
        self.parts = strands(*block.shape)
        self.events = 2 * (where.size - 1) + 1

    def keep(self):
        return pltpu.make_async_copy(self.block, self.out.at[self.where.ring], self.own.at[0])

    def copy(self, at, step):
        where = self.where
        way, part = self.parts[at]
        sign = (-1, 1)[way]
        slot = where.at_place(where.place + sign * step)
        target = self.out.at[(slot,) + part]
        source = target if step else self.block.at[part]
        return remote(
            source, target, self.send.at[at, step], self.recv.at[at, step], where.neighbour(-sign)
        )

    def run(self, event):
        step, piece = event // 2, event % 2
        if event == 0:
            self.keep().start()
        if event < self.events - 1:
            for at in (piece, piece + 2):
                if step:
                    self.copy(at, step - 1).wait_recv()
                self.copy(at, step).start()
        else:
            for at in range(4):
                self.copy(at, step - 1).wait_recv()
                for past in range(step):
                    self.copy(at, past).wait_send()
            self.keep().wait()


class RingGatherSplit:
    @staticmethod
    def scratch(size):
        dma, half = pltpu.SemaphoreType.DMA, size // 2
        return [dma((2, half))] * 4 + [dma((1,))]

    def __init__(self, where, block, out, sems):
        self.where, self.block, self.out = where, block, out
        self.send, self.recv, self.send_core, self.recv_core, self.own = sems
        self.half = where.size // 2
        self.events = self.half + 2
        cut = -(-block.shape[0] // 32) * 16
        self.parts = (pl.ds(0, cut), pl.ds(cut, block.shape[0] - cut))

    def keep(self):
        return pltpu.make_async_copy(self.block, self.out.at[self.where.ring], self.own.at[0])

    def slot(self, step, at):
        where = self.where
        place = where.at_place(where.place + (2 * where.core - 1) * step)
        return self.out.at[place, self.parts[at]]

    def copy(self, step, at):
        where = self.where
        target = self.slot(step, at)
        source = target if step else self.block.at[self.parts[at]]
        peer = where.neighbour(1 - 2 * where.core)
        return remote(source, target, self.send.at[at, step], self.recv.at[at, step], peer)

    def hand(self, step, at):
        target = self.slot(step + 1, at)
        return remote(
            target,
            target,
            self.send_core.at[at, step],
            self.recv_core.at[at, step],
            self.where.peer(1, 0),
        )

    def run(self, step):
        half = self.half
        if step == 0:
            self.keep().start()
        for at in range(2):
            if 0 < step <= half:
                self.copy(step - 1, at).wait_recv()
            if step < half:
                self.copy(step, at).start()
            if 0 < step < half:
                self.hand(step - 1, at).start()
            if step == half + 1:
                for past in range(half):
                    self.copy(past, at).wait_send()
                for past in range(half - 1):
                    self.hand(past, at).wait()
        if step == half + 1:
            self.keep().wait()


class RingSum:
    @staticmethod
    def scratch(size, rows, columns):
        dma = pltpu.SemaphoreType.DMA
        slots = pltpu.VMEM((size - 1, rows, columns), BF16)
        return [slots, slots, dma((4, size - 1)), dma((4, size - 1))]

    def __init__(self, where, terms, out, scratch):
        self.where, self.terms, self.out = where, terms, out
        self.held, self.landed, self.send, self.recv = scratch
        self.parts = strands(*out.shape)
        self.events = 2 * where.size

    def copy(self, at, step):
        way, part = self.parts[at]
        part = (step,) + part
        return remote(
            self.held.at[part],
            self.landed.at[part],
            self.send.at[at, step],
            self.recv.at[at, step],
            self.where.neighbour((1, -1)[way]),
        )

    def term(self, slot, part):
        if len(self.terms.shape) == 3:
            return self.terms[(slot,) + part]
        rows = self.out.shape[0]
        first = pl.multiple_of(slot * rows + part[0].start, 16)
        return self.terms[(pl.ds(first, part[0].size), part[1])]

    def run(self, event):
        step, piece = event // 2, event % 2
        where, last = self.where, self.where.size - 2
        for at in (piece, piece + 2):
            way, part = self.parts[at]
            slot = where.at_place(where.place + (-1, 1)[way] * (step + 1))
            total = self.term(slot, part)
            if step:
                self.copy(at, step - 1).wait_recv()
                total = total.astype(F32) + self.landed[(step - 1,) + part].astype(F32)
            if step <= last:
                self.held[(step,) + part] = total.astype(BF16)
                self.copy(at, step).start()
            else:
                self.out[part] = total.astype(self.out.dtype)
        if event == self.events - 1:
            for at in range(4):
                for past in range(last + 1):
                    self.copy(at, past).wait_send()


class RingSumSplit:
    @staticmethod
    def scratch(size, rows, columns):
        dma, half = pltpu.SemaphoreType.DMA, size // 2
        slots = pltpu.VMEM((half, rows, columns), BF16)
        return [slots] * 3 + [dma((half,)), dma((half,)), dma((2, half)), dma((2, half))]

    def __init__(self, where, terms, out, scratch):
        self.where, self.terms, self.out = where, terms, out
        self.given, self.held, self.landed, *sems = scratch
        self.send_core, self.recv_core, self.send, self.recv = sems
        self.half = where.size // 2
        self.events = self.half + 1
        rows = out.shape[0]
        cut = -(-rows // 32) * 16
        self.parts = (pl.ds(0, cut), pl.ds(cut, rows - cut))

    def slot(self, step, side):
        return self.where.at_place(self.where.place + side * (self.half - step))

    def give(self, step):
        side = 2 * self.where.core - 1
        return remote(
            self.terms.at[self.slot(step, side)],
            self.given.at[step],
            self.send_core.at[step],
            self.recv_core.at[step],
            self.where.peer(1, 0),
        )

    def copy(self, step, at):
        return remote(
            self.held.at[step, self.parts[at]],
            self.landed.at[step, self.parts[at]],
            self.send.at[at, step],
            self.recv.at[at, step],
            self.where.neighbour(1 - 2 * self.where.core),
        )

    def run(self, step):
        half, core = self.half, self.where.core
        if step == 0:
            for at in range(half):
                self.give(at).start()
        if step < half:
            self.give(step).wait_recv()
            slot = self.slot(step, 1 - 2 * core)
        for at, rows in enumerate(self.parts):
            if step < half:
                total = self.terms[slot, rows].astype(F32) + self.given[step, rows].astype(F32)
                if step == 0:
                    total = total * (1 - core).astype(F32)
            else:
                total = self.terms[self.where.ring, rows].astype(F32)
            if step:
                self.copy(step - 1, at).wait_recv()
                total = total + self.landed[step - 1, rows].astype(F32)
            if step < half:
                self.held[step, rows] = total.astype(BF16)
                self.copy(step, at).start()
            else:
                self.out[rows] = total.astype(self.out.dtype)
        if step == half:
            for past in range(half):
                self.give(past).wait_send()
                for at in range(2):
                    self.copy(past, at).wait_send()


class GroupGather:
    @staticmethod
    def scratch(span, parts=1):
        dma = pltpu.SemaphoreType.DMA
        return [dma((2, span, parts)), dma((2, span, parts)), dma((1,))]

    def __init__(self, where, block, out, sems, parts=1):
        self.where, self.block, self.out, self.parts = where, block, out, parts
        self.send, self.recv, self.own = sems

    def rows(self, part):
        size = self.block.shape[0] // self.parts
        return pl.ds(part * size, size)

    def hop(self, dx, part):
        where, rows = self.where, self.rows(part)
        at = (0, dx, part)
        return remote(
            self.block.at[rows],
            self.out.at[0, dx, rows],
            self.send.at[at],
            self.recv.at[at],
            where.peer(0, where.span - dx),
        )

    def cross(self, dx, part):
        rows = self.rows(part)
        source = self.out.at[0, dx, rows] if dx else self.block.at[rows]
        at = (1, dx, part)
        return remote(
            source,
            self.out.at[1, dx, rows],
            self.send.at[at],
            self.recv.at[at],
            self.where.peer(1, 0),
        )

    def start(self, part):
        for dx in range(1, self.where.span):
            self.hop(dx, part).start()
        self.cross(0, part).start()

    def pass_on(self, part):
        for dx in range(1, self.where.span):
            self.hop(dx, part).wait_recv()
            self.cross(dx, part).start()

    def arrived(self, dx):
        for part in range(self.parts):
            self.cross(dx, part).wait_recv()

    def sent(self):
        for part in range(self.parts):
            for dx in range(self.where.span):
                if dx:
                    self.hop(dx, part).wait_send()
                self.cross(dx, part).wait_send()

    def finish(self):
        for dx in range(self.where.span):
            self.arrived(dx)
        self.sent()

    def keep(self):
        return pltpu.make_async_copy(self.block, self.out.at[0, 0], self.own.at[0])

    def run(self, step):
        if step == 0:
            self.keep().start()
            for part in range(self.parts):
                self.start(part)
        elif step == 1:
            for part in range(self.parts):
                self.pass_on(part)
        else:
            self.finish()
            self.keep().wait()


class GroupSwap:
    @staticmethod
    def scratch(span):
        dma = pltpu.SemaphoreType.DMA
        return [dma((2, span)), dma((2, span)), dma((1,))]

    def __init__(self, where, source, target, sems):
        self.where, self.source, self.target = where, source, target
        self.send, self.recv, self.own = sems

    def run(self, step):
        where = self.where
        keep = pltpu.make_async_copy(self.source(0, 0), self.target(0, 0), self.own.at[0])
        copies = [
            remote(
                self.source(dc, dx),
                self.target(dc, dx),
                self.send.at[dc, dx],
                self.recv.at[dc, dx],
                where.peer(dc, dx),
            )
            for dx in reversed(range(where.span))
            for dc in range(2)
            if dc or dx
        ]
        if step == 0:
            for copy in copies:
                copy.start()
            keep.start()
        else:
            for copy in copies:
                copy.wait()
            keep.wait()


class GroupSum:
    @staticmethod
    def scratch(span, rows, columns):
        dma = pltpu.SemaphoreType.DMA
        slots = pltpu.VMEM((span, rows, columns), BF16)
        return [slots, slots, dma((span,)), dma((span,)), dma((span,)), dma((span,))]

    def __init__(self, where, terms, out, scratch):
        self.where, self.terms, self.out = where, terms, out
        self.crossed, self.landed, *sems = scratch
        self.send_core, self.recv_core, self.send, self.recv = sems

    def cross(self, dx):
        return remote(
            self.terms.at[1, dx],
            self.crossed.at[dx],
            self.send_core.at[dx],
            self.recv_core.at[dx],
            self.where.peer(1, 0),
        )

    def hop(self, dx):
        return remote(
            self.crossed.at[dx],
            self.landed.at[dx],
            self.send.at[dx],
            self.recv.at[dx],
            self.where.peer(0, dx),
        )

    def fold(self, dx):
        self.cross(dx).wait_recv()
        total = self.terms[0, dx].astype(F32) + self.crossed[dx].astype(F32)
        self.crossed[dx] = total.astype(BF16)
        self.hop(dx).start()

    def finish(self):
        self.cross(0).wait_recv()
        total = self.terms[0, 0].astype(F32) + self.crossed[0].astype(F32)
        for dx in range(1, self.where.span):
            self.hop(dx).wait_recv()
            total = total + self.landed[dx].astype(F32)
        self.out[...] = total.astype(self.out.dtype)
        for dx in range(self.where.span):
            self.cross(dx).wait_send()
            if dx:
                self.hop(dx).wait_send()

    def run(self, step):
        later = list(reversed(range(self.where.span)))
        if step == 0:
            for dx in later:
                self.cross(dx).start()
        elif step == 1:
            for dx in later[:-1]:
                self.fold(dx)
        else:
            self.finish()


class CoreSum:
    @staticmethod
    def scratch(span, rows, columns):
        dma = pltpu.SemaphoreType.DMA
        return [pltpu.VMEM((span, rows, columns), BF16), dma((span,)), dma((span,))]

    def __init__(self, where, terms, out, scratch):
        self.where, self.terms, self.out = where, terms, out
        self.crossed, self.send_core, self.recv_core = scratch

    cross = GroupSum.cross

    def fold(self, dx):
        self.cross(dx).wait_recv()
        total = self.terms[0, dx].astype(F32) + self.crossed[dx].astype(F32)
        self.out[dx] = total.astype(BF16)

    def finish(self):
        for dx in range(self.where.span):
            self.cross(dx).wait_send()


class PatchSum:
    @staticmethod
    def scratch(span, rows, columns):
        dma = pltpu.SemaphoreType.DMA
        return [pltpu.VMEM((span, rows, columns), BF16), dma((span,)), dma((span,))]

    def __init__(self, where, terms, out, scratch):
        self.where, self.crossed, self.out = where, terms, out
        self.landed, self.send, self.recv = scratch

    hop = GroupSum.hop

    def run(self, step):
        span = self.where.span
        if step == 0:
            for dx in range(1, span):
                self.hop(dx).start()
        else:
            total = self.crossed[0].astype(F32)
            for dx in range(1, span):
                self.hop(dx).wait_recv()
                total = total + self.landed[dx].astype(F32)
            self.out[...] = total
            for dx in range(1, span):
                self.hop(dx).wait_send()


class AllSum:
    @staticmethod
    def bits(sizes, axes=(2, 0, 1)):
        found = []
        for axis in axes:
            bit = 1
            while bit < sizes[axis]:
                found.append((axis, bit))
                bit *= 2
        return found

    @staticmethod
    def scratch(sizes, shape):
        count = len(AllSum.bits(sizes))
        dma = pltpu.SemaphoreType.DMA
        slots = pltpu.VMEM((count,) + tuple(shape), F32)
        return [slots, slots, dma((count,)), dma((count,))]

    def __init__(self, where, sizes, block, out, scratch, axes=(2, 0, 1)):
        self.block, self.out = block, out
        self.held, self.landed, self.send, self.recv = scratch
        here = (where.ring, where.core, where.patch)
        self.peers = []
        for axis, bit in AllSum.bits(sizes, axes):
            peer = list(here)
            peer[axis] = here[axis] + (1 - 2 * ((here[axis] // bit) % 2)) * bit
            self.peers.append(tuple(peer))
        self.events = len(self.peers) + 1

    def copy(self, step):
        return remote(
            self.held.at[step],
            self.landed.at[step],
            self.send.at[step],
            self.recv.at[step],
            self.peers[step],
        )

    def run(self, step):
        if step == 0:
            total = self.block[...]
        else:
            self.copy(step - 1).wait()
            total = self.held[step - 1] + self.landed[step - 1]
        if step < len(self.peers):
            self.held[step] = total
            self.copy(step).start()
        else:
            self.out[...] = total


HBM = pl.BlockSpec(memory_space=pl.ANY)
CORE = pl.BlockSpec(memory_space=pltpu.VMEM)


def take(refs, counts):
    found, at = [], 0
    for count in counts:
        found.append(list(refs[at : at + count]))
        at += count
    return found


def flat_block(vector):
    rows = -(-vector.shape[0] // 1024) * 8
    return jnp.pad(vector, (0, rows * 128 - vector.shape[0])).reshape(rows, 128)


def join(pieces, wide, block):
    group, share, _ = pieces.shape
    for at in range(group):
        wide[at * share : (at + 1) * share, :] = pieces[at].astype(F32)
    block[...] = wide[...].astype(BF16)


def entry_kernel(sizes, clips, chunk, *refs):
    where = Where(sizes)
    ins, outs, scratch = take(refs, (8, 8, len(refs) - 16))
    tokens, qkv_weight, up_weight, out_rows, silu_part, ada_weight, small, frame_clip = ins
    tokens_all, w_qkv, w_out, up_block, summed, hidden, projected, own_rows = outs
    cols, lands, wide, blocks, (w_qkv_t, vector, spread), *sems = take(
        scratch, (2, 3, 3, 2, 3, 3, 3, 3, 3, 3, 5, 4)
    )
    sums = AllSum(where, sizes, vector, summed, sems[6])
    member, span, group = where.member, where.span, 2 * where.span
    rows, width = tokens.shape
    share = out_rows.shape[0]
    device = where.ring * group + member

    def swap(source, land, job_sems):
        return GroupSwap(where, source, lambda dc, dx: land.at[member], job_sems)

    swap_qkv = swap(lambda dc, dx: cols[0].at[where.peer_member(dc, dx)], lands[0], sems[0])
    swap_up = swap(lambda dc, dx: cols[1].at[where.peer_member(dc, dx)], lands[1], sems[1])
    swap_out = swap(lambda dc, dx: out_rows, lands[2], sems[2])
    gather = GroupGather(where, tokens, tokens_all, sems[3], max(1, rows // 128))
    ring = RingGather(where, blocks[0], w_qkv, sems[4])
    ring_out = RingGatherSplit(where, blocks[1], w_out, sems[5])

    features = qkv_weight.shape[1] // (3 * group)
    wide_rows = qkv_weight[...].astype(F32)
    for at in range(group):
        for part in range(3):
            low = (part * group + at) * features
            cols[0][at, :, part * features : (part + 1) * features] = wide_rows[
                :, low : low + features
            ].astype(BF16)

    units = up_weight.shape[1] // (group * where.size)
    spread[...] = jnp.zeros_like(spread)
    lengths = [share] * 4 + [units, 6 * share]
    low = 0
    for at, length in enumerate(lengths):
        spread[at : at + 1, :length] = small[0:1, low : low + length]
        low += length
    lanes = lax.broadcasted_iota(jnp.int32, (1, width), 1)
    vector[...] = jnp.zeros_like(vector)
    vector[0:4, :] = pltpu.roll(spread[...], device * share, 1)[0:4]
    start = device * units
    moved = pltpu.roll(spread[...], start % width, 1)[4:5]
    for at in range(4):
        vector[4 + at : 5 + at, :] = jnp.where(start // width == at, moved, 0.0)
    start = device * 6 * share
    moved = pltpu.roll(spread[...], start % width, 1)[5:6]
    lies = start // width + jnp.where(lanes < start % width, 1, 0)
    terms = jnp.dot(silu_part[...], ada_weight[...], preferred_element_type=F32)
    for part in range(6):
        bias = jnp.where(lies == part, moved, 0.0)
        for clip in range(clips):
            at = 8 + 6 * clip + part
            vector[at : at + 1, :] = (
                terms[clip : clip + 1, part * width : (part + 1) * width] + bias
            )
    own_clip = frame_clip[0].astype(F32)
    own_frame = 2 * where.ring + where.core
    at = 8 + 6 * clips
    vector[at : at + 1, :] = jnp.where((lanes == own_frame) & (where.patch == 0), own_clip, 0.0)

    greet(where.ring_peers() + where.group_peers() + sums.peers)
    swap_qkv.run(0)
    sums.run(0)
    swap_qkv.run(1)
    join(lands[0], wide[0], blocks[0])
    ring.run(0)
    ring.run(1)
    swap_out.run(0)
    gather.run(0)
    wide_rows = up_weight[...].astype(F32)
    for at in range(group):
        for ring_at in range(where.size):
            low = (ring_at * group + at) * units
            cols[1][at, :, ring_at * units : (ring_at + 1) * units] = wide_rows[
                :, low : low + units
            ].astype(BF16)
    swap_up.run(0)
    ring.run(2)
    sums.run(1)
    ring.run(3)
    swap_out.run(1)
    join(lands[2], wide[2], blocks[1])
    ring_out.run(0)
    ring.run(4)
    turns(ring, 5, [(sums, 2), (ring_out, 1)], 2)
    swap_up.run(1)
    join(lands[1], wide[1], up_block)

    at = 8 + 6 * clips
    other_frame = 2 * where.ring + 1 - where.core
    other_clip = jnp.sum(
        jnp.where(lanes == other_frame, summed[at : at + 1, :], 0.0), axis=1, keepdims=True
    )
    own, other = [0.0] * 6, [0.0] * 2
    for clip in range(clips):
        is_own = jnp.maximum(1.0 - jnp.abs(own_clip - clip), 0.0)
        is_other = jnp.maximum(1.0 - jnp.abs(other_clip - clip), 0.0)
        for part in range(6):
            row = summed[8 + 6 * clip + part : 9 + 6 * clip + part, :]
            own[part] = own[part] + is_own * row
            if part < 2:
                other[part] = other[part] + is_other * row
        own_rows[8 + clip : 9 + clip, :] = jnp.zeros((1, width), F32) + is_own
        own_rows[8 + clips + clip : 9 + clips + clip, :] = jnp.zeros((1, width), F32) + is_other
    for part in range(6):
        own_rows[part : part + 1, :] = own[part]
    own_rows[6:8, :] = summed[2:4, :]

    features = blocks[0].shape[1] // 3
    lead = pltpu.roll(summed[0:8, :], (width - member * features) % width, 1).T
    bias_q, bias_v = lead[:features, 0:1], lead[:features, 1:2]
    w_qkv_t[...] = w_qkv[...].reshape(width, 3 * features).T

    def project(dc, dx, at):
        here = slice(at, at + chunk)
        normed, _ = layer_norm(tokens_all[dc, dx, here, :].astype(F32))
        shift, scale = (other if dc else own)[:2]
        low = (normed * (1.0 + scale) + shift).astype(BF16)
        first = (dc * span + dx) * rows + at
        hidden[first : first + chunk, :] = low
        found = lax.dot_general(
            w_qkv_t[...], low, (((1,), (1,)), ((), ())), preferred_element_type=F32
        )
        there = slice(first, first + chunk)
        projected[:features, there] = (found[:features] + bias_q).astype(BF16)
        projected[features : 2 * features, there] = found[features : 2 * features].astype(BF16)
        projected[2 * features :, there] = (found[2 * features :] + bias_v).astype(BF16)

    gather.keep().wait()
    for dx in range(span):
        if dx == 1:
            gather.run(1)
        for dc in range(2):
            if dc:
                gather.arrived(dx)
            for at in range(0, rows, chunk):
                project(dc, dx, at)
    gather.sent()


def turns(ring, event, others, every):
    count = 0
    others = [list(item) for item in others]
    while event < ring.events or any(at < job.events for job, at in others):
        if event < ring.events:
            ring.run(event)
            event += 1
        count += 1
        if count % every == 0 or event >= ring.events:
            for item in others:
                if item[1] < item[0].events:
                    item[0].run(item[1])
                    item[1] += 1


def entry(
    tokens, qkv_weight, up_weight, out_rows, silu_part, ada_weight, small, clip, sizes, call_id
):
    size, _, span = sizes
    group, share = 2 * span, out_rows.shape[0]
    rows, width = tokens.shape
    clips = silu_part.shape[0]
    block_rows = group * share
    columns = [qkv_weight.shape[1] // group, up_weight.shape[1] // group, width]
    count = 9 + 6 * clips
    vector = (count + -count % 8, width)
    shape = jax.ShapeDtypeStruct
    scratch = [pltpu.VMEM((group, share, n), BF16) for n in columns[:2]]
    scratch += [pltpu.VMEM((group, share, n), BF16) for n in columns]
    scratch += [pltpu.VMEM((block_rows, n), F32) for n in columns]
    scratch += [pltpu.VMEM((block_rows, n), BF16) for n in (columns[0], width)]
    scratch += [pltpu.VMEM((columns[0], width), BF16)]
    scratch += [pltpu.VMEM(vector, F32), pltpu.VMEM((8, width), F32)]
    scratch += GroupSwap.scratch(span) * 3
    scratch += GroupGather.scratch(span, max(1, rows // 128))
    scratch += RingGather.scratch(size)
    scratch += RingGatherSplit.scratch(size)
    scratch += AllSum.scratch(sizes, vector)
    return pl.pallas_call(
        functools.partial(entry_kernel, sizes, clips, min(256, rows)),
        out_shape=[
            shape((2, span, rows, width), BF16),
            shape((size, block_rows, columns[0]), BF16),
            shape((size, block_rows, width), BF16),
            shape((block_rows, columns[1]), BF16),
            shape(vector, F32),
            shape((group * rows, width), BF16),
            shape((columns[0], group * rows), BF16),
            shape((8 + 2 * clips + -2 * clips % 8, width), F32),
        ],
        in_specs=[HBM, CORE, CORE, HBM, CORE, CORE, CORE, pl.BlockSpec(memory_space=pltpu.SMEM)],
        out_specs=[CORE, CORE, HBM, CORE, CORE, CORE, CORE, CORE],
        scratch_shapes=scratch,
        compiler_params=pltpu.CompilerParams(
            collective_id=call_id, has_side_effects=True, vmem_limit_bytes=48 * MIB
        ),
        name="entry",
    )(tokens, qkv_weight, up_weight, out_rows, silu_part, ada_weight, small, clip)


def beside(job, total, places, count, first=0, stride=1):
    at = pl.program_id(0) * pl.num_programs(1) + pl.program_id(1)
    slots, event = {}, 0
    for place in range(first, total * places, stride):
        todo = list(range(event, min(event + count, job.events - 1)))
        if todo:
            slots[place] = todo
            event += len(todo)

    def ahead(place):
        for grid in range(total):
            todo = slots.get(grid * places + place)
            if todo:

                @pl.when(at == grid)
                def _():
                    for event in todo:
                        job.run(event)

    def finish():
        for late in range(event, job.events):
            job.run(late)

    return ahead, finish


def attention_kernel(sizes, factor, chunk, total, *refs):
    where = Where(sizes)
    ins, outs, scratch = take(refs, (5, 4, len(refs) - 9))
    q_ref, k_ref, v_ref, up_block, grad_block = ins
    out_ref, lse_ref, w_up, grad_all = outs
    sems = take(scratch, (3, 3))
    chunks = q_ref.shape[2] // chunk
    places = max(chunks // 2, 1)
    ahead, finish = beside(RingGather(where, up_block, w_up, sems[0]), total, places, 1)
    gather = GroupGather(where, grad_block, grad_all, sems[1], 2)
    at = pl.program_id(0) * pl.num_programs(1) + pl.program_id(1)

    @pl.when(at == 0)
    def _():
        greet(where.ring_peers() + where.group_peers())
        gather.run(0)

    keys = k_ref[0].T
    values_t = v_ref[0]
    for number in range(chunks):
        if number % 2 == 0:
            ahead(number // 2)
        span = slice(number * chunk, (number + 1) * chunk)
        scores = jnp.dot(keys, q_ref[0, :, span], preferred_element_type=F32) * factor
        top = jnp.max(scores, axis=0, keepdims=True)
        probs = jnp.exp2(scores - top)
        row_sum = jnp.sum(probs, axis=0, keepdims=True)
        mixed = jnp.dot(values_t, probs.astype(BF16), preferred_element_type=F32)
        out_ref[0, :, span] = (mixed / row_sum).astype(BF16)
        lse_ref[0, :, span] = top + jnp.log2(row_sum)

    @pl.when(at == total - 1)
    def _():
        gather.run(1)
        finish()
        gather.run(2)


def attention(qkv, up_block, grad_block, patches, sizes, call_id):
    size, _, span = sizes
    triple, dim, tokens = qkv.shape
    heads = triple // 3
    frames = tokens // patches
    block = (1, dim, patches)
    factor = LOG2E / math.sqrt(HEAD_DIM)
    shape = jax.ShapeDtypeStruct
    return pl.pallas_call(
        functools.partial(attention_kernel, sizes, factor, min(256, patches), frames * heads),
        out_shape=[
            shape((heads, dim, tokens), BF16),
            shape((heads, 1, tokens), F32),
            shape((size,) + up_block.shape, BF16),
            shape((2, span) + grad_block.shape, BF16),
        ],
        grid=(frames, heads),
        in_specs=[
            pl.BlockSpec(block, lambda f, h: (h, 0, f)),
            pl.BlockSpec(block, lambda f, h: (heads + h, 0, f)),
            pl.BlockSpec(block, lambda f, h: (2 * heads + h, 0, f)),
            HBM,
            HBM,
        ],
        out_specs=[
            pl.BlockSpec(block, lambda f, h: (h, 0, f)),
            pl.BlockSpec((1, 1, patches), lambda f, h: (h, 0, f)),
            HBM,
            HBM,
        ],
        scratch_shapes=RingGather.scratch(size) + GroupGather.scratch(span, 2),
        compiler_params=pltpu.CompilerParams(
            collective_id=call_id, has_side_effects=True, vmem_limit_bytes=32 * MIB
        ),
        cost_estimate=pl.CostEstimate(
            flops=4 * heads * patches * tokens * 256,
            bytes_accessed=4 * heads * dim * tokens * 2,
            transcendentals=heads * patches * tokens,
        ),
        name="attention",
    )(qkv, qkv, qkv, up_block, grad_block)


def attention_back_kernel(sizes, factor, chunk, total, *refs):
    where = Where(sizes)
    ins, outs, scratch = take(refs, (7, 3, len(refs) - 10))
    q_ref, k_ref, v_ref, g_ref, lse_ref, up_terms, half_terms = ins
    grads_ref, up_sum, half_sum = outs
    dk_sum, dv_sum = scratch[:2]
    own = take(scratch[2:], (4, 3))
    patches = q_ref.shape[2]
    chunks = patches // chunk
    ahead, finish = beside(RingSum(where, up_terms, up_sum, own[0]), total, 1, 2)
    half = PatchSum(where, half_terms, half_sum, own[1])
    at = pl.program_id(0) * pl.num_programs(1) + pl.program_id(1)

    @pl.when(at == 0)
    def _():
        greet(where.ring_peers() + where.group_peers())
        half.run(0)

    keys_t = k_ref[0]
    keys = keys_t.T
    values = v_ref[0].T
    scale = factor / LOG2E
    ahead(0)
    for number in range(chunks):
        span = slice(number * chunk, (number + 1) * chunk)
        queries_t = q_ref[0, :, span]
        grad_t = g_ref[0, :, span]
        scores = jnp.dot(keys, queries_t, preferred_element_type=F32) * factor
        probs = jnp.exp2(scores - lse_ref[0, :, span])
        grad_probs = jnp.dot(values, grad_t, preferred_element_type=F32)
        row_dot = jnp.sum(probs * grad_probs, axis=0, keepdims=True)
        grad_scores = (probs * (grad_probs - row_dot)).astype(BF16)
        probs_low = probs.astype(BF16)
        dq = jnp.dot(keys_t, grad_scores, preferred_element_type=F32)
        grads_ref[0, 0, :, span] = (dq * scale).astype(BF16)
        dims = (((1,), (1,)), ((), ()))
        dk = lax.dot_general(queries_t, grad_scores, dims, preferred_element_type=F32)
        dv = lax.dot_general(grad_t, probs_low, dims, preferred_element_type=F32)
        if number == 0:
            dk_sum[...] = dk
            dv_sum[...] = dv
        else:
            dk_sum[...] += dk
            dv_sum[...] += dv
    grads_ref[1, 0] = (dk_sum[...] * scale).astype(BF16)
    grads_ref[2, 0] = dv_sum[...].astype(BF16)

    @pl.when(at == total - 1)
    def _():
        finish()
        half.run(1)


def attention_back(qkv, grad, lse, up_terms, half_terms, patches, sizes, call_id):
    size, _, span = sizes
    triple, dim, tokens = qkv.shape
    heads = triple // 3
    frames = tokens // patches
    block = (1, dim, patches)
    factor = LOG2E / math.sqrt(HEAD_DIM)
    spec = pl.BlockSpec(block, lambda f, h: (h, 0, f))
    shape = jax.ShapeDtypeStruct
    return pl.pallas_call(
        functools.partial(attention_back_kernel, sizes, factor, min(256, patches), frames * heads),
        out_shape=[
            shape((3, heads, dim, tokens), BF16),
            shape(up_terms.shape[1:], BF16),
            shape(half_terms.shape[1:], F32),
        ],
        grid=(frames, heads),
        in_specs=[
            spec,
            pl.BlockSpec(block, lambda f, h: (heads + h, 0, f)),
            pl.BlockSpec(block, lambda f, h: (2 * heads + h, 0, f)),
            spec,
            pl.BlockSpec((1, 1, patches), lambda f, h: (h, 0, f)),
            CORE,
            CORE,
        ],
        out_specs=[pl.BlockSpec((3,) + block, lambda f, h: (0, h, 0, f)), CORE, CORE],
        scratch_shapes=[pltpu.VMEM((dim, patches), F32)] * 2
        + RingSum.scratch(size, *up_terms.shape[1:])
        + PatchSum.scratch(span, *half_terms.shape[1:]),
        compiler_params=pltpu.CompilerParams(
            collective_id=call_id, has_side_effects=True, vmem_limit_bytes=48 * MIB
        ),
        cost_estimate=pl.CostEstimate(
            flops=10 * heads * patches * tokens * 256,
            bytes_accessed=8 * heads * dim * tokens * 2,
            transcendentals=heads * patches * tokens,
        ),
        name="attention_back",
    )(qkv, qkv, qkv, grad, lse, up_terms, half_terms)


def joined(array):
    group, features, count = array.shape
    if features % 16:
        return array.astype(F32).reshape(group * features, count).astype(BF16)
    return array.reshape(group * features, count)


def middle_kernel(sizes, parts, *refs):
    where = Where(sizes)
    ins, outs, scratch = take(refs, (5, 5, len(refs) - 10))
    heads_t, w_out, tokens, vectors, down_block = ins
    attended, branch, midway, hidden_all, w_down = outs
    (hidden,), *sems = take(scratch, (1, 3, 3, 3))
    greet(where.ring_peers() + where.group_peers())
    rows, width = tokens.shape
    span = where.span

    swap = GroupSwap(
        where,
        lambda dc, dx: heads_t.at[:, pl.ds((dc * span + dx) * rows, rows)],
        lambda dc, dx: attended.at[where.member],
        sems[0],
    )
    ring = RingGather(where, down_block, w_down, sems[1])
    gather = GroupGather(where, hidden, hidden_all, sems[2], parts)
    swap.run(0)
    event = min(7, ring.events - 1)
    for early in range(event):
        ring.run(early)
    swap.run(1)
    size = rows // parts
    full = w_out[...]
    for part in range(parts):
        span_rows = slice(part * size, (part + 1) * size)
        mixed = joined(attended[:, :, span_rows])
        one = lax.dot_general(mixed, full, (((0,), (0,)), ((), ())), preferred_element_type=F32)
        one = one + vectors[6:7, :]
        branch[span_rows, :] = one
        mid = tokens[span_rows, :].astype(F32) + vectors[2:3, :] * one
        midway[span_rows, :] = mid
        normed, _ = layer_norm(mid)
        hidden[span_rows, :] = (normed * (1.0 + vectors[4:5, :]) + vectors[3:4, :]).astype(BF16)
        gather.start(part)
        if event < ring.events:
            ring.run(event)
            event += 1
    gather.keep().start()
    for event in range(event, ring.events):
        ring.run(event)
    for part in range(parts):
        gather.pass_on(part)
    gather.finish()
    gather.keep().wait()


def middle(heads_t, w_out, tokens, vectors, down_block, sizes, call_id):
    size, _, span = sizes
    rows, width = tokens.shape
    parts = rows // 128
    shape = jax.ShapeDtypeStruct
    return pl.pallas_call(
        functools.partial(middle_kernel, sizes, parts),
        out_shape=[
            shape((2 * span, heads_t.shape[0], rows), BF16),
            shape((rows, width), F32),
            shape((rows, width), F32),
            shape((2, span, rows, width), BF16),
            shape((size,) + down_block.shape, BF16),
        ],
        in_specs=[CORE, CORE, CORE, CORE, HBM],
        out_specs=[CORE, CORE, CORE, HBM, HBM],
        scratch_shapes=[pltpu.VMEM((rows, width), BF16)]
        + GroupSwap.scratch(span)
        + RingGather.scratch(size)
        + GroupGather.scratch(span, parts),
        compiler_params=pltpu.CompilerParams(
            collective_id=call_id, has_side_effects=True, vmem_limit_bytes=40 * MIB
        ),
        name="middle",
    )(heads_t, w_out, tokens, vectors, down_block)


def gelu_both(values_in):
    square = values_in * values_in
    inner = 0.7978845608028654 * values_in * (1.0 + 0.044715 * square)
    bent = jnp.tanh(inner)
    outer = 0.5 * (1.0 + bent)
    slope = 0.7978845608028654 * (1.0 + 3.0 * 0.044715 * square)
    return values_in * outer, outer + 0.5 * values_in * (1.0 - bent * bent) * slope


def feed_kernel(sizes, chunk, tile, *refs):
    where = Where(sizes)
    ins, outs, scratch = take(refs, (5, 5, len(refs) - 10))
    hidden, grad, w_up, w_down, bias = ins
    half, grad_hidden, g_up, g_down, g_bias = outs
    act, grad_pre, branch, back = scratch[:4]
    own = take(scratch[4:], (3, 6))
    span = where.span
    rows, width = grad_hidden.shape
    units = bias.shape[1]
    sum_half = CoreSum(where, branch, half, own[0])
    sum_back = GroupSum(where, back, grad_hidden, own[1])
    greet(where.group_peers())
    each = rows // chunk
    across = (((1,), (1,)), ((), ()))

    def body(step, total):
        at = step // each
        dx, dc = span - 1 - at // 2, 1 - at % 2
        inside = pl.ds(pl.multiple_of(step % each * chunk, chunk), chunk)
        first = pl.multiple_of((dc * span + dx) * rows + step % each * chunk, chunk)
        here = pl.ds(first, chunk)
        pre = jnp.dot(hidden[here, :], w_up[...], preferred_element_type=F32) + bias[...]
        value, slope = gelu_both(pre)
        value = value.astype(BF16)
        act[here, :] = value
        grad_act = lax.dot_general(grad[here, :], w_down[...], across, preferred_element_type=F32)
        low = (grad_act * slope).astype(BF16)
        grad_pre[here, :] = low
        back[dc, dx, inside, :] = lax.dot_general(
            low, w_up[...], across, preferred_element_type=F32
        ).astype(BF16)
        branch[dc, dx, inside, :] = jnp.dot(
            value, w_down[...], preferred_element_type=F32
        ).astype(BF16)
        for place in range(2 * span):
            done_dx, done_dc = span - 1 - place // 2, 1 - place % 2

            @pl.when(step == (place + 1) * each - 1)
            def _():
                if done_dc:
                    sum_back.cross(done_dx).start()
                    sum_half.cross(done_dx).start()
                elif done_dx:
                    sum_back.fold(done_dx)
                    sum_half.fold(done_dx)

        return total + jnp.sum(low.astype(F32), axis=0, keepdims=True)

    zero = jnp.zeros((1, units), F32)
    g_bias[...] = lax.fori_loop(0, 2 * span * each, body, zero)
    sum_half.fold(0)
    over = (((0,), (0,)), ((), ()))
    for low in range(0, units, tile):
        cut = slice(low, low + tile)
        g_down[cut, :] = lax.dot_general(
            act[:, cut], grad[...], over, preferred_element_type=F32
        ).astype(BF16)
        g_up[:, cut] = lax.dot_general(
            hidden[...], grad_pre[:, cut], over, preferred_element_type=F32
        ).astype(BF16)
    sum_half.finish()
    sum_back.finish()


def feed(hidden, grad, w_up, w_down, bias, sizes, call_id):
    _, _, span = sizes
    tokens, width = hidden.shape
    units = w_up.shape[1]
    rows = tokens // (2 * span)
    shape = jax.ShapeDtypeStruct
    terms = pltpu.VMEM((2, span, rows, width), BF16)
    return pl.pallas_call(
        functools.partial(feed_kernel, sizes, min(256, rows), 384 if units % 384 == 0 else units),
        out_shape=[
            shape((span, rows, width), BF16),
            shape((rows, width), F32),
            shape((width, units), BF16),
            shape((units, width), BF16),
            shape((1, units), F32),
        ],
        in_specs=[CORE] * 5,
        out_specs=[CORE] * 5,
        scratch_shapes=[pltpu.VMEM((tokens, units), BF16)] * 2
        + [terms] * 2
        + CoreSum.scratch(span, rows, width)
        + GroupSum.scratch(span, rows, width),
        compiler_params=pltpu.CompilerParams(
            collective_id=call_id, has_side_effects=True, vmem_limit_bytes=60 * MIB
        ),
        name="feed",
    )(hidden, grad, w_up, w_down, bias)


def return_kernel(sizes, parts, tile, *refs):
    where = Where(sizes)
    ins, outs, scratch = take(refs, (8, 5, len(refs) - 13))
    grad_hidden, midway, branch, grad_out, w_out, attended, vectors, down_terms = ins
    grad_mid, grad_mix, down_sum, g_out, sums = outs
    (grad_heads, grad_one), *own = take(scratch, (2, 4, 3 * parts))
    greet(where.ring_peers() + where.group_peers())
    rows, width = midway.shape
    span = where.span
    size = rows // parts
    features = grad_heads.shape[1]
    ring = RingSum(where, down_terms, down_sum, own[0])
    swaps = []
    for part in range(parts):
        cut = pl.ds(part * size, size)

        def source(dc, dx, cut=cut):
            return grad_heads.at[where.peer_member(dc, dx), :, cut]

        def target(dc, dx, part=part):
            block = dc * span + (span - dx) % span
            return grad_mix.at[:, pl.ds(block * rows + part * size, size)]

        swaps.append(GroupSwap(where, source, target, own[1][3 * part : 3 * part + 3]))
    ring.run(0)
    ring.run(1)
    full = w_out[...]
    totals = [jnp.zeros((1, width), F32)] * 4
    event = 2
    for part in range(parts):
        here = slice(part * size, (part + 1) * size)
        normed, inv_std = layer_norm(midway[here, :])
        grad = grad_hidden[here, :]
        mid = grad_out[here, :].astype(F32) + norm_back(
            grad * (1.0 + vectors[4:5, :]), normed, inv_std
        )
        grad_mid[here, :] = mid
        low = (vectors[2:3, :] * mid).astype(BF16)
        grad_one[here, :] = low
        heads_t = lax.dot_general(full, low, (((1,), (1,)), ((), ())), preferred_element_type=F32)
        grad_heads[:, :, here] = heads_t.reshape(2 * span, features, size).astype(BF16)
        swaps[part].run(0)
        found = [grad, grad * normed, mid * branch[here, :], low.astype(F32)]
        totals = [
            total + jnp.sum(item, axis=0, keepdims=True) for total, item in zip(totals, found)
        ]
        ring.run(event)
        event += 1
    for at, total in enumerate(totals):
        sums[at : at + 1, :] = total
    sums[4:8, :] = jnp.zeros((4, width), F32)
    for low in range(0, width, tile):
        cut = slice(low, low + tile)
        g_out[cut, :] = jnp.dot(
            attended[cut, :], grad_one[...], preferred_element_type=F32
        ).astype(BF16)
        if event < ring.events:
            ring.run(event)
            event += 1
    for event in range(event, ring.events):
        ring.run(event)
    for swap in swaps:
        swap.run(1)


def back_to_heads(
    grad_hidden, midway, branch, grad_out, w_out, attended, vectors, down_terms, sizes, call_id
):
    size, _, span = sizes
    rows, width = midway.shape
    group = 2 * span
    parts = rows // 128
    features = width // group
    shape = jax.ShapeDtypeStruct
    return pl.pallas_call(
        functools.partial(return_kernel, sizes, parts, 384),
        out_shape=[
            shape((rows, width), F32),
            shape((features, group * rows), BF16),
            shape(down_terms.shape[1:], F32),
            shape((width, width), BF16),
            shape((8, width), F32),
        ],
        in_specs=[CORE] * 8,
        out_specs=[CORE] * 5,
        scratch_shapes=[
            pltpu.VMEM((group, features, rows), BF16),
            pltpu.VMEM((rows, width), BF16),
        ]
        + RingSum.scratch(size, *down_terms.shape[1:])
        + GroupSwap.scratch(span) * parts,
        compiler_params=pltpu.CompilerParams(
            collective_id=call_id, has_side_effects=True, vmem_limit_bytes=48 * MIB
        ),
        name="back_to_heads",
    )(grad_hidden, midway, branch, grad_out, w_out, attended, vectors, down_terms)


def last_kernel(sizes, chunk, tile, clips, *refs):
    where = Where(sizes)
    ins, outs, scratch = take(refs, (7, 5, len(refs) - 12))
    grad_qkv, hidden, tokens, w_qkv, out_terms, early, chosen = ins
    grad_hidden, qkv_sum, out_sum, early_sum, late_sum = outs
    (back, g_qkv, late), *own = take(scratch, (3, 6, 4, 7, 4, 4))
    span = where.span
    rows, width = grad_hidden.shape
    sum_back = GroupSum(where, back, grad_hidden, own[0])
    ring = RingSum(where, g_qkv, qkv_sum, own[1])
    ring_out = RingSumSplit(where, out_terms, out_sum, own[2])
    first_sums = AllSum(where, sizes, early, early_sum, own[3])
    sums = AllSum(where, sizes, late, late_sum, own[4], (0, 1, 2))
    greet(where.ring_peers() + where.group_peers() + sums.peers)
    ring_out.run(0)
    first_sums.run(0)
    each = rows // chunk
    blocks = 2 * span
    far = 2 * (span - 1) * each
    planned = dict(zip(range(far, blocks * each), [(ring, at) for at in (2, 3, 4, 5)]))

    def body(step, totals):
        at = step // each
        dx, dc = span - 1 - at // 2, 1 - at % 2
        inside = pl.ds(pl.multiple_of(step % each * chunk, chunk), chunk)
        first = pl.multiple_of((dc * span + dx) * rows + step % each * chunk, chunk)
        here = pl.ds(first, chunk)
        term = lax.dot_general(
            grad_qkv[:, here], w_qkv[...], (((0,), (1,)), ((), ())), preferred_element_type=F32
        )
        back[dc, dx, inside, :] = term.astype(BF16)
        normed, _ = layer_norm(tokens[here, :].astype(F32))
        shift = jnp.sum(term, axis=0, keepdims=True)
        scale = jnp.sum(term * normed, axis=0, keepdims=True)
        other = dc.astype(F32)
        for place in range(blocks):
            done_dx, done_dc = span - 1 - place // 2, 1 - place % 2

            @pl.when(step == (place + 1) * each - 1)
            def _():
                if done_dc:
                    sum_back.cross(done_dx).start()
                elif done_dx:
                    sum_back.fold(done_dx)

        for when, (job, event) in planned.items():
            pl.when(step == when)(functools.partial(job.run, event))
        own_part, other_part = 1.0 - other, other
        return (
            totals[0] + own_part * shift,
            totals[1] + own_part * scale,
            totals[2] + other_part * shift,
            totals[3] + other_part * scale,
        )

    zero = jnp.zeros((1, width), F32)
    totals = lax.fori_loop(0, far, body, (zero,) * 4)
    event = 1
    for low in range(0, width, tile):
        ring_out.run(event)
        first_sums.run(event)
        event += 1
        cut = slice(low, low + tile)
        g_qkv[cut, :] = lax.dot_general(
            hidden[:, cut], grad_qkv[...], (((0,), (1,)), ((), ())), preferred_element_type=F32
        ).astype(BF16)
    ring.run(0)
    ring.run(1)
    totals = lax.fori_loop(far, blocks * each, body, totals)
    late[...] = jnp.zeros_like(late)
    for clip in range(clips):
        for part in range(2):
            at = 2 * clip + part
            late[at : at + 1, :] = (
                chosen[clip : clip + 1, :] * totals[part]
                + chosen[clips + clip : clips + clip + 1, :] * totals[2 + part]
            )
    sums.run(0)
    todo = [(ring_out, at) for at in range(event, ring_out.events)]
    todo += [(first_sums, at) for at in range(event, first_sums.events)]
    late_todo = list(range(1, sums.events - 1))
    for event in range(2 + len(planned), ring.events):
        ring.run(event)
        if todo:
            job, at = todo.pop(0)
            job.run(at)
        if event % 2 and late_todo:
            sums.run(late_todo.pop(0))
    for job, at in todo:
        job.run(at)
    for at in late_todo:
        sums.run(at)
    sum_back.finish()
    sums.run(sums.events - 1)


def back_to_tokens(
    grad_qkv, hidden, tokens, w_qkv, out_terms, early, chosen, clips, sizes, call_id
):
    size, _, span = sizes
    count, width = tokens.shape
    rows = count // (2 * span)
    features = grad_qkv.shape[0]
    block_rows = width // size
    late = (2 * clips + -2 * clips % 8, width)
    shape = jax.ShapeDtypeStruct
    return pl.pallas_call(
        functools.partial(last_kernel, sizes, min(256, rows), 384, clips),
        out_shape=[
            shape((rows, width), F32),
            shape((block_rows, features), BF16),
            shape((block_rows, width), BF16),
            shape(early.shape, F32),
            shape(late, F32),
        ],
        in_specs=[CORE] * 7,
        out_specs=[CORE] * 5,
        scratch_shapes=[
            pltpu.VMEM((2, span, rows, width), BF16),
            pltpu.VMEM((width, features), BF16),
            pltpu.VMEM(late, F32),
        ]
        + GroupSum.scratch(span, rows, width)
        + RingSum.scratch(size, block_rows, features)
        + RingSumSplit.scratch(size, block_rows, width)
        + AllSum.scratch(sizes, early.shape)
        + AllSum.scratch(sizes, late),
        compiler_params=pltpu.CompilerParams(
            collective_id=call_id, has_side_effects=True, vmem_limit_bytes=60 * MIB
        ),
        name="back_to_tokens",
    )(grad_qkv, hidden, tokens, w_qkv, out_terms, early, chosen)


def final_kernel(sizes, *refs):
    where = Where(sizes)
    ins, outs, scratch = take(refs, (4, 4, len(refs) - 8))
    summed, share_qkv, share_up, share_out = outs
    got, own = scratch[:3], take(scratch[3:], (4, 3, 3, 3))
    sums = AllSum(where, sizes, ins[0], summed, own[0])
    greet(where.group_peers() + sums.peers)
    swaps = [
        GroupSwap(
            where,
            lambda dc, dx, source=ins[at + 1]: source.at[where.peer_member(dc, dx)],
            lambda dc, dx, target=got[at]: target.at[where.member],
            own[at + 1],
        )
        for at in range(3)
    ]
    sums.run(0)
    for swap in swaps:
        swap.run(0)
    for event in range(1, sums.events):
        sums.run(event)
    group, _, three = got[0].shape
    features = three // 3
    swaps[0].run(1)
    for member in range(group):
        piece = got[0][member].astype(F32)
        for part in range(3):
            low = (part * group + member) * features
            share_qkv[:, low : low + features] = piece[:, part * features : (part + 1) * features]
    swaps[1].run(1)
    units = got[1].shape[2] // where.size
    for member in range(group):
        piece = got[1][member].astype(F32)
        for ring in range(where.size):
            low = (ring * group + member) * units
            share_up[:, low : low + units] = piece[:, ring * units : (ring + 1) * units]
    swaps[2].run(1)
    total = got[2][0].astype(F32)
    for member in range(1, group):
        total = total + got[2][member].astype(F32)
    share_out[...] = total


def final(block, pieces, sizes, call_id):
    group, share, _ = pieces[0].shape
    shape = jax.ShapeDtypeStruct
    return pl.pallas_call(
        functools.partial(final_kernel, sizes),
        out_shape=[
            shape(block.shape, F32),
            shape((share, group * pieces[0].shape[2]), F32),
            shape((share, group * pieces[1].shape[2]), F32),
            shape((share, pieces[2].shape[2]), F32),
        ],
        in_specs=[CORE] * 4,
        out_specs=[CORE] * 4,
        scratch_shapes=[pltpu.VMEM(item.shape, BF16) for item in pieces]
        + AllSum.scratch(sizes, block.shape)
        + GroupSwap.scratch(sizes[2]) * 3,
        compiler_params=pltpu.CompilerParams(
            collective_id=call_id, has_side_effects=True, vmem_limit_bytes=32 * MIB
        ),
        name="final",
    )(block, *pieces)


def per_device(
    tokens,
    cotangent,
    clip_embed,
    timesteps,
    frame_clip,
    ada_weight,
    ada_bias,
    qkv_weight,
    query_bias,
    value_bias,
    out_weight,
    out_bias,
    up_weight,
    up_bias,
    down_weight,
    down_bias,
):
    ring_size, patch_size = lax.axis_size("ring"), lax.axis_size("patch")
    sizes = (ring_size, 2, patch_size)
    group = 2 * patch_size
    device_count = ring_size * group
    ring, core, patch = (lax.axis_index(name) for name in ("ring", "core", "patch"))
    member = core * patch_size + patch
    device = ring * group + member
    rows, width = tokens.shape[1:]
    tokens, cotangent = tokens[0], cotangent[0]
    patches = patch_size * rows
    clips = clip_embed.shape[0]
    hidden = up_weight.shape[1]
    share = width // device_count
    heads = HEADS // group
    head_width = heads * HEAD_DIM
    units = hidden // group
    mine = jnp.arange(group) == member
    mine_of_all = jnp.arange(device_count) == device

    condition = clip_embed + sinusoid(timesteps, width)
    silu_cond, silu_back = jax.vjp(jax.nn.silu, condition)
    silu_low = silu_cond.astype(BF16)
    silu_part = lax.dynamic_slice_in_dim(silu_low, device * share, share, 1)
    small = jnp.concatenate(
        [query_bias, value_bias, out_bias, down_bias, up_bias, ada_bias]
    ).astype(F32)[None, :]

    tokens_all, w_qkv, w_out, up_block, summed, hidden_one, projected, own_rows = entry(
        tokens,
        qkv_weight,
        up_weight,
        out_weight,
        silu_part,
        ada_weight,
        small,
        frame_clip,
        sizes,
        1,
    )
    w_qkv = w_qkv.reshape(width, 3 * head_width)
    w_out = w_out.reshape(width, width)
    scale_one, gate_one, scale_two, gate_two, b_down = (own_rows[at] for at in (1, 2, 4, 5, 7))
    b_up = lax.dynamic_index_in_dim(
        summed[4 : 4 + hidden // width].reshape(ring_size, group, hidden // device_count),
        member,
        1,
        False,
    ).reshape(units)

    qkv = projected.reshape(3 * heads, HEAD_DIM, 2 * patches)
    grad_out = cotangent.astype(F32)
    grad_branch_two = (gate_two * grad_out).astype(BF16)
    attended_t, lse, w_up, gb_two_all = attention(
        qkv, up_block, grad_branch_two, patches, sizes, 2
    )
    w_up = w_up.reshape(width, units)

    attended, branch_one, midway, hidden_two_all, w_down = middle(
        attended_t.reshape(head_width, 2 * patches),
        w_out,
        tokens,
        own_rows,
        down_weight,
        sizes,
        3,
    )
    attended = attended.reshape(width, rows)
    w_down = w_down.reshape(units, width)

    branch_half, grad_hidden_two, g_up, g_down, g_up_b = feed(
        hidden_two_all.reshape(2 * patches, width),
        gb_two_all.reshape(2 * patches, width),
        w_up,
        w_down,
        b_up[None, :],
        sizes,
        4,
    )
    g_up_b = g_up_b[0]
    g_down_b = jnp.sum(grad_branch_two.astype(F32), axis=0)
    block_rows = width // ring_size
    grad_midway, grad_mix, share_down, g_out, own_sums = back_to_heads(
        grad_hidden_two,
        midway,
        branch_one,
        cotangent,
        w_out,
        attended,
        own_rows,
        g_down.reshape(ring_size, units // ring_size, width),
        sizes,
        5,
    )
    grad_shift_two, grad_scale_two, grad_gate_one, g_out_b = (own_sums[at] for at in range(4))

    grad_projected, sum_up, branch_two = attention_back(
        qkv,
        grad_mix.reshape(heads, HEAD_DIM, 2 * patches),
        lse,
        g_up.reshape(ring_size, block_rows, units),
        branch_half,
        patches,
        sizes,
        6,
    )
    grad_projected = grad_projected.reshape(3 * head_width, 2 * patches)
    branch_two = branch_two + b_down
    output = (midway + gate_two * branch_two).astype(BF16)
    grad_gate_two = jnp.sum(grad_out * branch_two, axis=0)
    g_query_b = jnp.sum(grad_projected[:head_width].astype(F32), axis=1)
    g_value_b = jnp.sum(grad_projected[2 * head_width :].astype(F32), axis=1)

    frame_grads = jnp.stack([grad_gate_one, grad_shift_two, grad_scale_two, grad_gate_two])
    early = jnp.concatenate(
        [
            (own_rows[8 : 8 + clips, None] * frame_grads[None]).reshape(4 * clips, width),
            jnp.where(mine[:, None], g_query_b[None, :], 0.0).reshape(1, width),
            jnp.where(mine[:, None], g_value_b[None, :], 0.0).reshape(1, width),
            jnp.stack([g_out_b, g_down_b]),
            jnp.where(mine[None, :, None], g_up_b.reshape(ring_size, 1, -1), 0.0).reshape(
                -1, width
            ),
        ]
    )
    early = jnp.pad(early, ((0, -early.shape[0] % 8), (0, 0)))
    grad_hidden_one, sum_qkv, sum_out, early_sum, late_sum = back_to_tokens(
        grad_projected,
        hidden_one,
        tokens_all.reshape(2 * patches, width),
        w_qkv,
        g_out.reshape(ring_size, block_rows, width),
        early,
        own_rows[8:],
        clips,
        sizes,
        7,
    )
    first = late_sum[: 2 * clips].reshape(clips, 2 * width)
    second = early_sum[: 4 * clips].reshape(clips, 4 * width)
    mod_low = jnp.concatenate([first, second], axis=1).astype(BF16)
    query_b_all, value_b_all, out_b_all, down_b_all = (early_sum[4 * clips + at] for at in range(4))
    up_b_all = early_sum[4 * clips + 4 :].reshape(-1)[:hidden]

    def own(vector):
        length = vector.shape[0] // device_count
        return lax.dynamic_slice_in_dim(vector, device * length, length, 0)

    ada_bias_grad = own(jnp.sum(mod_low.astype(F32), axis=0))
    ada_weight_grad = lax.dot_general(
        silu_part, mod_low, (((0,), (0,)), ((), ())), preferred_element_type=F32
    )
    grad_silu_part = lax.dot_general(
        mod_low, ada_weight, (((1,), (1,)), ((), ())), preferred_element_type=F32
    )
    spread = jnp.where(mine_of_all[None, :, None], grad_silu_part[:, None, :], 0.0).reshape(-1)
    grad_silu, share_qkv, share_up, share_out = final(
        flat_block(spread),
        [item.reshape(group, share, -1) for item in (sum_qkv, sum_up, sum_out)],
        sizes,
        8,
    )
    grad_silu = grad_silu.reshape(-1)[: clips * width].reshape(clips, width)
    clip_grad = silu_back(grad_silu)[0]

    input_rows = tokens.astype(F32)
    normed_one, inv_one = layer_norm(input_rows)
    tokens_grad = (
        grad_midway + norm_back(grad_hidden_one * (1.0 + scale_one), normed_one, inv_one)
    ).astype(BF16)

    return (
        output[None],
        tokens_grad[None],
        clip_grad,
        ada_weight_grad,
        ada_bias_grad,
        share_qkv,
        own(query_b_all),
        own(value_b_all),
        share_out,
        own(out_b_all),
        share_up,
        own(up_b_all),
        share_down,
        own(down_b_all),
    )


def solution(mesh):
    frames, patch = mesh.shape["frames"], mesh.shape["patch"]
    inner = Mesh(mesh.devices.reshape(frames // 2, 2, patch), ("ring", "core", "patch"))
    every = ("ring", "core", "patch")
    tokens = P(("ring", "core"), "patch", None)
    matrix = P(every, None)
    vector = P(every)
    return jax.shard_map(
        per_device,
        mesh=inner,
        in_specs=(
            tokens,
            tokens,
            P(),
            P(),
            P(("ring", "core")),
            matrix,
            vector,
            matrix,
            vector,
            vector,
            matrix,
            vector,
            matrix,
            vector,
            matrix,
            vector,
        ),
        out_specs=(
            tokens,
            tokens,
            P(),
            matrix,
            vector,
            matrix,
            vector,
            vector,
            matrix,
            vector,
            matrix,
            vector,
            matrix,
            vector,
        ),
        check_vma=False,
    )
```

```python
import functools
import math

import jax
import jax.numpy as jnp
from jax import lax
from jax.experimental import pallas as pl
from jax.experimental.pallas import tpu as pltpu
from jax.sharding import Mesh
from jax.sharding import PartitionSpec as P

HEADS = 16
HEAD_DIM = 72
BF16 = jnp.bfloat16
F32 = jnp.float32
LOG2E = 1.4426950408889634
MESH_ID = pl.DeviceIdType.MESH
MIB = 2**20


def layer_norm(values_in):
    centre = values_in - jnp.mean(values_in, axis=-1, keepdims=True)
    spread = jnp.mean(centre * centre, axis=-1, keepdims=True)
    inv_std = lax.rsqrt(spread + 1e-06)
    return (centre * inv_std, inv_std)


def norm_back(grad_normed, normed, inv_std):
    mean_grad = jnp.mean(grad_normed, axis=-1, keepdims=True)
    mean_prod = jnp.mean(grad_normed * normed, axis=-1, keepdims=True)
    return (grad_normed - mean_grad - normed * mean_prod) * inv_std


def gelu_tanh(values_in):
    inner = 0.7978845608028654 * (values_in + 0.044715 * values_in * values_in * values_in)
    return 0.5 * values_in * (1.0 + jnp.tanh(inner))


def sinusoid(steps_in, width_in):
    half_width = width_in // 2
    freqs = jnp.exp(-math.log(10000.0) * jnp.arange(half_width, dtype=jnp.float32) / half_width)
    angles = steps_in.astype(jnp.float32)[:, None] * freqs[None, :]
    return jnp.concatenate([jnp.cos(angles), jnp.sin(angles)], axis=1)


class Where:
    def __init__(self, sizes):
        self.size, _, self.span = sizes
        self.ring, self.core, self.patch = (
            lax.axis_index(name) for name in ("ring", "core", "patch")
        )
        along, across = self.ring // 2, self.ring % 2
        self.place = (1 - across) * along + across * (self.size - 1 - along)
        self.member = self.core * self.span + self.patch

    def at_place(self, place):
        place = (place + 2 * self.size) % self.size
        back = place // (self.size // 2)
        return (1 - back) * 2 * place + back * (2 * (self.size - 1 - place) + 1)

    def neighbour(self, step):
        return (self.at_place(self.place + step), self.core, self.patch)

    def peer(self, dc, dx):
        core = 1 - self.core if dc else self.core
        return (self.ring, core, (self.patch + dx) % self.span)

    def peer_member(self, dc, dx):
        _, core, patch = self.peer(dc, dx)
        return core * self.span + patch

    def ring_peers(self):
        return [self.neighbour(1), self.neighbour(-1)]

    def group_peers(self):
        return [
            self.peer(dc, dx) for dc in range(2) for dx in range(self.span) if dc or dx
        ]


def greet(peers):
    barrier = pltpu.get_barrier_semaphore()
    for peer in peers:
        pl.semaphore_signal(barrier, inc=1, device_id=peer, device_id_type=MESH_ID)
    pl.semaphore_wait(barrier, len(peers))


def remote(source, target, send_sem, recv_sem, peer):
    return pltpu.make_async_remote_copy(
        src_ref=source,
        dst_ref=target,
        send_sem=send_sem,
        recv_sem=recv_sem,
        device_id=peer,
        device_id_type=MESH_ID,
    )


def strands(rows, columns):
    by_rows = rows % 16 == 0
    tile = 16 if by_rows else 128
    tiles = (rows if by_rows else columns) // tile
    sizes = [tiles // 4 + (at < tiles % 4) for at in range(4)]
    found, low = [], 0
    for at, count in enumerate(sizes):
        cut = pl.ds(low * tile, count * tile)
        found.append((at // 2, (cut, slice(None)) if by_rows else (slice(None), cut)))
        low += count
    return found


class RingGather:
    @staticmethod
    def scratch(size):
        dma = pltpu.SemaphoreType.DMA
        return [dma((4, size - 1)), dma((4, size - 1)), dma((1,))]

    def __init__(self, where, block, out, sems):
        self.where, self.block, self.out = where, block, out
        self.send, self.recv, self.own = sems
        self.parts = strands(*block.shape)
        self.events = 2 * (where.size - 1) + 1

    def keep(self):
        return pltpu.make_async_copy(self.block, self.out.at[self.where.ring], self.own.at[0])

    def copy(self, at, step):
        where = self.where
        way, part = self.parts[at]
        sign = (-1, 1)[way]
        slot = where.at_place(where.place + sign * step)
        target = self.out.at[(slot,) + part]
        source = target if step else self.block.at[part]
        return remote(
            source, target, self.send.at[at, step], self.recv.at[at, step], where.neighbour(-sign)
        )

    def run(self, event):
        step, piece = event // 2, event % 2
        if event == 0:
            self.keep().start()
        if event < self.events - 1:
            for at in (piece, piece + 2):
                if step:
                    self.copy(at, step - 1).wait_recv()
                self.copy(at, step).start()
        else:
            for at in range(4):
                self.copy(at, step - 1).wait_recv()
                for past in range(step):
                    self.copy(at, past).wait_send()
            self.keep().wait()


class RingGatherSplit:
    @staticmethod
    def scratch(size):
        dma, half = pltpu.SemaphoreType.DMA, size // 2
        return [dma((2, half))] * 4 + [dma((1,))]

    def __init__(self, where, block, out, sems):
        self.where, self.block, self.out = where, block, out
        self.send, self.recv, self.send_core, self.recv_core, self.own = sems
        self.half = where.size // 2
        self.events = self.half + 2
        cut = -(-block.shape[0] // 32) * 16
        self.parts = (pl.ds(0, cut), pl.ds(cut, block.shape[0] - cut))

    def keep(self):
        return pltpu.make_async_copy(self.block, self.out.at[self.where.ring], self.own.at[0])

    def slot(self, step, at):
        where = self.where
        place = where.at_place(where.place + (2 * where.core - 1) * step)
        return self.out.at[place, self.parts[at]]

    def copy(self, step, at):
        where = self.where
        target = self.slot(step, at)
        source = target if step else self.block.at[self.parts[at]]
        peer = where.neighbour(1 - 2 * where.core)
        return remote(source, target, self.send.at[at, step], self.recv.at[at, step], peer)

    def hand(self, step, at):
        target = self.slot(step + 1, at)
        return remote(
            target,
            target,
            self.send_core.at[at, step],
            self.recv_core.at[at, step],
            self.where.peer(1, 0),
        )

    def run(self, step):
        half = self.half
        if step == 0:
            self.keep().start()
        for at in range(2):
            if 0 < step <= half:
                self.copy(step - 1, at).wait_recv()
            if step < half:
                self.copy(step, at).start()
            if 0 < step < half:
                self.hand(step - 1, at).start()
            if step == half + 1:
                for past in range(half):
                    self.copy(past, at).wait_send()
                for past in range(half - 1):
                    self.hand(past, at).wait()
        if step == half + 1:
            self.keep().wait()


class RingSum:
    @staticmethod
    def scratch(size, rows, columns):
        dma = pltpu.SemaphoreType.DMA
        slots = pltpu.VMEM((size - 1, rows, columns), BF16)
        return [slots, slots, dma((4, size - 1)), dma((4, size - 1))]

    def __init__(self, where, terms, out, scratch):
        self.where, self.terms, self.out = where, terms, out
        self.held, self.landed, self.send, self.recv = scratch
        self.parts = strands(*out.shape)
        self.events = 2 * where.size

    def copy(self, at, step):
        way, part = self.parts[at]
        part = (step,) + part
        return remote(
            self.held.at[part],
            self.landed.at[part],
            self.send.at[at, step],
            self.recv.at[at, step],
            self.where.neighbour((1, -1)[way]),
        )

    def term(self, slot, part):
        if len(self.terms.shape) == 3:
            return self.terms[(slot,) + part]
        rows = self.out.shape[0]
        first = pl.multiple_of(slot * rows + part[0].start, 16)
        return self.terms[(pl.ds(first, part[0].size), part[1])]

    def run(self, event):
        step, piece = event // 2, event % 2
        where, last = self.where, self.where.size - 2
        for at in (piece, piece + 2):
            way, part = self.parts[at]
            slot = where.at_place(where.place + (-1, 1)[way] * (step + 1))
            total = self.term(slot, part)
            if step:
                self.copy(at, step - 1).wait_recv()
                total = total.astype(F32) + self.landed[(step - 1,) + part].astype(F32)
            if step <= last:
                self.held[(step,) + part] = total.astype(BF16)
                self.copy(at, step).start()
            else:
                self.out[part] = total.astype(self.out.dtype)
        if event == self.events - 1:
            for at in range(4):
                for past in range(last + 1):
                    self.copy(at, past).wait_send()


class RingSumSplit:
    @staticmethod
    def scratch(size, rows, columns):
        dma, half = pltpu.SemaphoreType.DMA, size // 2
        slots = pltpu.VMEM((half, rows, columns), BF16)
        return [slots] * 3 + [dma((half,)), dma((half,)), dma((2, half)), dma((2, half))]

    def __init__(self, where, terms, out, scratch):
        self.where, self.terms, self.out = where, terms, out
        self.given, self.held, self.landed, *sems = scratch
        self.send_core, self.recv_core, self.send, self.recv = sems
        self.half = where.size // 2
        self.events = self.half + 1
        rows = out.shape[0]
        cut = -(-rows // 32) * 16
        self.parts = (pl.ds(0, cut), pl.ds(cut, rows - cut))

    def slot(self, step, side):
        return self.where.at_place(self.where.place + side * (self.half - step))

    def give(self, step):
        side = 2 * self.where.core - 1
        return remote(
            self.terms.at[self.slot(step, side)],
            self.given.at[step],
            self.send_core.at[step],
            self.recv_core.at[step],
            self.where.peer(1, 0),
        )

    def copy(self, step, at):
        return remote(
            self.held.at[step, self.parts[at]],
            self.landed.at[step, self.parts[at]],
            self.send.at[at, step],
            self.recv.at[at, step],
            self.where.neighbour(1 - 2 * self.where.core),
        )

    def run(self, step):
        half, core = self.half, self.where.core
        if step == 0:
            for at in range(half):
                self.give(at).start()
        if step < half:
            self.give(step).wait_recv()
            slot = self.slot(step, 1 - 2 * core)
        for at, rows in enumerate(self.parts):
            if step < half:
                total = self.terms[slot, rows].astype(F32) + self.given[step, rows].astype(F32)
                if step == 0:
                    total = total * (1 - core).astype(F32)
            else:
                total = self.terms[self.where.ring, rows].astype(F32)
            if step:
                self.copy(step - 1, at).wait_recv()
                total = total + self.landed[step - 1, rows].astype(F32)
            if step < half:
                self.held[step, rows] = total.astype(BF16)
                self.copy(step, at).start()
            else:
                self.out[rows] = total.astype(self.out.dtype)
        if step == half:
            for past in range(half):
                self.give(past).wait_send()
                for at in range(2):
                    self.copy(past, at).wait_send()


class GroupGather:
    @staticmethod
    def scratch(span, parts=1):
        dma = pltpu.SemaphoreType.DMA
        return [dma((2, span, parts)), dma((2, span, parts)), dma((1,))]

    def __init__(self, where, block, out, sems, parts=1):
        self.where, self.block, self.out, self.parts = where, block, out, parts
        self.send, self.recv, self.own = sems

    def rows(self, part):
        size = self.block.shape[0] // self.parts
        return pl.ds(part * size, size)

    def hop(self, dx, part):
        where, rows = self.where, self.rows(part)
        at = (0, dx, part)
        return remote(
            self.block.at[rows],
            self.out.at[0, dx, rows],
            self.send.at[at],
            self.recv.at[at],
            where.peer(0, where.span - dx),
        )

    def cross(self, dx, part):
        rows = self.rows(part)
        source = self.out.at[0, dx, rows] if dx else self.block.at[rows]
        at = (1, dx, part)
        return remote(
            source,
            self.out.at[1, dx, rows],
            self.send.at[at],
            self.recv.at[at],
            self.where.peer(1, 0),
        )

    def start(self, part):
        for dx in range(1, self.where.span):
            self.hop(dx, part).start()
        self.cross(0, part).start()

    def pass_on(self, part):
        for dx in range(1, self.where.span):
            self.hop(dx, part).wait_recv()
            self.cross(dx, part).start()

    def arrived(self, dx):
        for part in range(self.parts):
            self.cross(dx, part).wait_recv()

    def sent(self):
        for part in range(self.parts):
            for dx in range(self.where.span):
                if dx:
                    self.hop(dx, part).wait_send()
                self.cross(dx, part).wait_send()

    def finish(self):
        for dx in range(self.where.span):
            self.arrived(dx)
        self.sent()

    def keep(self):
        return pltpu.make_async_copy(self.block, self.out.at[0, 0], self.own.at[0])

    def run(self, step):
        if step == 0:
            self.keep().start()
            for part in range(self.parts):
                self.start(part)
        elif step == 1:
            for part in range(self.parts):
                self.pass_on(part)
        else:
            self.finish()
            self.keep().wait()


class GroupSwap:
    @staticmethod
    def scratch(span):
        dma = pltpu.SemaphoreType.DMA
        return [dma((2, span)), dma((2, span)), dma((1,))]

    def __init__(self, where, source, target, sems):
        self.where, self.source, self.target = where, source, target
        self.send, self.recv, self.own = sems

    def run(self, step):
        where = self.where
        keep = pltpu.make_async_copy(self.source(0, 0), self.target(0, 0), self.own.at[0])
        copies = [
            remote(
                self.source(dc, dx),
                self.target(dc, dx),
                self.send.at[dc, dx],
                self.recv.at[dc, dx],
                where.peer(dc, dx),
            )
            for dx in reversed(range(where.span))
            for dc in range(2)
            if dc or dx
        ]
        if step == 0:
            for copy in copies:
                copy.start()
            keep.start()
        else:
            for copy in copies:
                copy.wait()
            keep.wait()


class GroupSum:
    @staticmethod
    def scratch(span, rows, columns):
        dma = pltpu.SemaphoreType.DMA
        slots = pltpu.VMEM((span, rows, columns), BF16)
        fewer = pltpu.VMEM((max(1, span - 1), rows, columns), BF16)
        return [slots, fewer, dma((span,)), dma((span,)), dma((span,)), dma((span,))]

    def __init__(self, where, terms, out, scratch):
        self.where, self.terms, self.out = where, terms, out
        self.crossed, self.landed, *sems = scratch
        self.send_core, self.recv_core, self.send, self.recv = sems

    def cross(self, dx):
        return remote(
            self.terms.at[1, dx],
            self.crossed.at[dx],
            self.send_core.at[dx],
            self.recv_core.at[dx],
            self.where.peer(1, 0),
        )

    def hop(self, dx):
        return remote(
            self.crossed.at[dx],
            self.landed.at[dx - 1],
            self.send.at[dx],
            self.recv.at[dx],
            self.where.peer(0, dx),
        )

    def fold(self, dx):
        self.cross(dx).wait_recv()
        total = self.terms[0, dx].astype(F32) + self.crossed[dx].astype(F32)
        self.crossed[dx] = total.astype(BF16)
        self.hop(dx).start()

    def finish(self):
        self.cross(0).wait_recv()
        total = self.terms[0, 0].astype(F32) + self.crossed[0].astype(F32)
        for dx in range(1, self.where.span):
            self.hop(dx).wait_recv()
            total = total + self.landed[dx - 1].astype(F32)
        self.out[...] = total.astype(self.out.dtype)
        for dx in range(self.where.span):
            self.cross(dx).wait_send()
            if dx:
                self.hop(dx).wait_send()

    def run(self, step):
        later = list(reversed(range(self.where.span)))
        if step == 0:
            for dx in later:
                self.cross(dx).start()
        elif step == 1:
            for dx in later[:-1]:
                self.fold(dx)
        else:
            self.finish()


class CoreSum:
    @staticmethod
    def scratch(span, rows, columns):
        dma = pltpu.SemaphoreType.DMA
        return [pltpu.VMEM((span, rows, columns), BF16), dma((span,)), dma((span,))]

    def __init__(self, where, terms, out, scratch):
        self.where, self.terms, self.out = where, terms, out
        self.crossed, self.send_core, self.recv_core = scratch

    def cross(self, dx):
        return remote(
            self.terms.at[dx],
            self.crossed.at[dx],
            self.send_core.at[dx],
            self.recv_core.at[dx],
            self.where.peer(1, 0),
        )

    def fold(self, dx):
        self.cross(dx).wait_recv()
        total = self.out[dx].astype(F32) + self.crossed[dx].astype(F32)
        self.out[dx] = total.astype(BF16)

    def finish(self):
        for dx in range(self.where.span):
            self.cross(dx).wait_send()


class PatchSum:
    @staticmethod
    def scratch(span, rows, columns):
        dma = pltpu.SemaphoreType.DMA
        return [pltpu.VMEM((max(1, span - 1), rows, columns), BF16), dma((span,)), dma((span,))]

    def __init__(self, where, terms, out, scratch):
        self.where, self.crossed, self.out = where, terms, out
        self.landed, self.send, self.recv = scratch

    hop = GroupSum.hop

    def run(self, step):
        span = self.where.span
        if step == 0:
            for dx in range(1, span):
                self.hop(dx).start()
        else:
            total = self.crossed[0].astype(F32)
            for dx in range(1, span):
                self.hop(dx).wait_recv()
                total = total + self.landed[dx - 1].astype(F32)
            self.out[...] = total
            for dx in range(1, span):
                self.hop(dx).wait_send()


class AllSum:
    @staticmethod
    def bits(sizes, axes=(2, 0, 1)):
        found = []
        for axis in axes:
            bit = 1
            while bit < sizes[axis]:
                found.append((axis, bit))
                bit *= 2
        return found

    @staticmethod
    def scratch(sizes, shape):
        count = len(AllSum.bits(sizes))
        dma = pltpu.SemaphoreType.DMA
        slots = pltpu.VMEM((count,) + tuple(shape), F32)
        return [slots, slots, dma((count,)), dma((count,))]

    def __init__(self, where, sizes, block, out, scratch, axes=(2, 0, 1)):
        self.block, self.out = block, out
        self.held, self.landed, self.send, self.recv = scratch
        here = (where.ring, where.core, where.patch)
        self.peers = []
        for axis, bit in AllSum.bits(sizes, axes):
            peer = list(here)
            peer[axis] = here[axis] + (1 - 2 * ((here[axis] // bit) % 2)) * bit
            self.peers.append(tuple(peer))
        self.events = len(self.peers) + 1

    def copy(self, step):
        return remote(
            self.held.at[step],
            self.landed.at[step],
            self.send.at[step],
            self.recv.at[step],
            self.peers[step],
        )

    def run(self, step):
        if step == 0:
            total = self.block[...]
        else:
            self.copy(step - 1).wait()
            total = self.held[step - 1] + self.landed[step - 1]
        if step < len(self.peers):
            self.held[step] = total
            self.copy(step).start()
        else:
            self.out[...] = total


HBM = pl.BlockSpec(memory_space=pl.ANY)
CORE = pl.BlockSpec(memory_space=pltpu.VMEM)


def take(refs, counts):
    found, at = [], 0
    for count in counts:
        found.append(list(refs[at : at + count]))
        at += count
    return found


def flat_block(vector):
    rows = -(-vector.shape[0] // 1024) * 8
    return jnp.pad(vector, (0, rows * 128 - vector.shape[0])).reshape(rows, 128)


def join(pieces, wide, block):
    group, share, _ = pieces.shape
    for at in range(group):
        wide[at * share : (at + 1) * share, :] = pieces[at].astype(F32)
    block[...] = wide[...].astype(BF16)


def entry_kernel(sizes, clips, chunk, *refs):
    where = Where(sizes)
    ins, outs, scratch = take(refs, (8, 9, len(refs) - 17))
    tokens, qkv_weight, up_weight, out_rows, silu_part, ada_weight, small, frame_clip = ins
    tokens_all, w_qkv, out_block, up_block, summed, hidden, projected, own_rows, bias_up = outs
    cols, lands, wide, (qkv_block, w_qkv_t, vector, spread, normal), *sems = take(
        scratch, (2, 3, 3, 5, 3, 3, 3, 3, 3, 4)
    )
    sums = AllSum(where, sizes, vector, summed, sems[5])
    member, span, group = where.member, where.span, 2 * where.span
    rows, width = tokens.shape
    share = out_rows.shape[0]
    device = where.ring * group + member

    def swap(source, land, job_sems):
        return GroupSwap(where, source, lambda dc, dx: land.at[member], job_sems)

    swap_qkv = swap(lambda dc, dx: cols[0].at[where.peer_member(dc, dx)], lands[0], sems[0])
    swap_up = swap(lambda dc, dx: cols[1].at[where.peer_member(dc, dx)], lands[1], sems[1])
    swap_out = swap(lambda dc, dx: out_rows, lands[2], sems[2])
    gather = GroupGather(where, tokens, tokens_all, sems[3], max(1, rows // 128))
    ring = RingGather(where, qkv_block, w_qkv, sems[4])

    features = qkv_weight.shape[1] // (3 * group)
    wide_rows = qkv_weight[...].astype(F32)
    for at in range(group):
        for part in range(3):
            low = (part * group + at) * features
            cols[0][at, :, part * features : (part + 1) * features] = wide_rows[
                :, low : low + features
            ].astype(BF16)

    units = up_weight.shape[1] // (group * where.size)
    spread[...] = jnp.zeros_like(spread)
    lengths = [share] * 4 + [units, 6 * share]
    low = 0
    for at, length in enumerate(lengths):
        spread[at : at + 1, :length] = small[0:1, low : low + length]
        low += length
    lanes = lax.broadcasted_iota(jnp.int32, (1, width), 1)
    vector[...] = jnp.zeros_like(vector)
    vector[0:4, :] = pltpu.roll(spread[...], device * share, 1)[0:4]
    start = device * units
    moved = pltpu.roll(spread[...], start % width, 1)[4:5]
    for at in range(4):
        vector[4 + at : 5 + at, :] = jnp.where(start // width == at, moved, 0.0)
    start = device * 6 * share
    moved = pltpu.roll(spread[...], start % width, 1)[5:6]
    lies = start // width + jnp.where(lanes < start % width, 1, 0)
    terms = jnp.dot(silu_part[...], ada_weight[...], preferred_element_type=F32)
    for part in range(6):
        bias = jnp.where(lies == part, moved, 0.0)
        for clip in range(clips):
            at = 8 + 6 * clip + part
            vector[at : at + 1, :] = (
                terms[clip : clip + 1, part * width : (part + 1) * width] + bias
            )
    own_clip = frame_clip[0].astype(F32)
    own_frame = 2 * where.ring + where.core
    at = 8 + 6 * clips
    vector[at : at + 1, :] = jnp.where((lanes == own_frame) & (where.patch == 0), own_clip, 0.0)

    greet(where.ring_peers() + where.group_peers() + sums.peers)
    swap_qkv.run(0)
    sums.run(0)
    swap_qkv.run(1)
    join(lands[0], wide[0], qkv_block)
    ring.run(0)
    ring.run(1)
    gather.run(0)
    wide_rows = up_weight[...].astype(F32)
    for at in range(group):
        for ring_at in range(where.size):
            low = (ring_at * group + at) * units
            cols[1][at, :, ring_at * units : (ring_at + 1) * units] = wide_rows[
                :, low : low + units
            ].astype(BF16)
    swap_up.run(0)
    swap_out.run(0)
    ring.run(2)
    sums.run(1)
    ring.run(3)
    ring.run(4)

    def norm(dc, dx, at, count):
        first = (dc * span + dx) * rows + at
        normal[first : first + count, :], _ = layer_norm(
            tokens_all[dc, dx, at : at + count, :].astype(F32)
        )

    gather.keep().wait()
    near = [(dc, at) for dc in range(2) for at in range(0, rows, chunk)]
    for event in range(5, ring.events):
        ring.run(event)
        if event % 2 == 0 and event // 2 - 1 < sums.events - 1:
            sums.run(event // 2 - 1)
        if near and event > 5:
            dc, at = near.pop(0)
            if dc and not at:
                gather.arrived(0)
            norm(dc, 0, at, chunk)
    sums.run(sums.events - 1)

    at = 8 + 6 * clips
    other_frame = 2 * where.ring + 1 - where.core
    other_clip = jnp.sum(
        jnp.where(lanes == other_frame, summed[at : at + 1, :], 0.0), axis=1, keepdims=True
    )
    own, other = [0.0] * 6, [0.0] * 2
    for clip in range(clips):
        is_own = jnp.maximum(1.0 - jnp.abs(own_clip - clip), 0.0)
        is_other = jnp.maximum(1.0 - jnp.abs(other_clip - clip), 0.0)
        for part in range(6):
            row = summed[8 + 6 * clip + part : 9 + 6 * clip + part, :]
            own[part] = own[part] + is_own * row
            if part < 2:
                other[part] = other[part] + is_other * row
        own_rows[8 + clip : 9 + clip, :] = jnp.zeros((1, width), F32) + is_own
        own_rows[8 + clips + clip : 9 + clips + clip, :] = jnp.zeros((1, width), F32) + is_other
    for part in range(6):
        own_rows[part : part + 1, :] = own[part]
    own_rows[6:8, :] = summed[2:4, :]
    for ring_at in range(where.size):
        start = (ring_at * group + member) * units
        moved = pltpu.roll(summed[0:8, :], (width - start % width) % width, 1)
        picked = jnp.zeros((1, width), F32)
        for at in range(4):
            picked = picked + jnp.where(start // width == at, moved[4 + at : 5 + at], 0.0)
        bias_up[:, ring_at * units : (ring_at + 1) * units] = picked[:, :units]

    features = qkv_block.shape[1] // 3
    lead = pltpu.roll(summed[0:8, :], (width - member * features) % width, 1).T
    bias_q, bias_v = lead[:features, 0:1], lead[:features, 1:2]
    w_qkv_t[...] = w_qkv[...].reshape(width, 3 * features).T

    def project(dc, dx, at):
        shift, scale = (other if dc else own)[:2]
        first = (dc * span + dx) * rows + at
        low = (normal[first : first + chunk, :] * (1.0 + scale) + shift).astype(BF16)
        hidden[first : first + chunk, :] = low
        found = lax.dot_general(
            w_qkv_t[...], low, (((1,), (1,)), ((), ())), preferred_element_type=F32
        )
        there = slice(first, first + chunk)
        projected[:features, there] = (found[:features] + bias_q).astype(BF16)
        projected[features : 2 * features, there] = found[features : 2 * features].astype(BF16)
        projected[2 * features :, there] = (found[2 * features :] + bias_v).astype(BF16)

    for dx in range(span):
        if dx == 1:
            swap_up.run(1)
            join(lands[1], wide[1], up_block)
            swap_out.run(1)
            join(lands[2], wide[2], out_block)
            gather.run(1)
        for dc in range(2):
            if dc and dx:
                gather.arrived(dx)
            for at in range(0, rows, chunk):
                if dx:
                    norm(dc, dx, at, chunk)
                project(dc, dx, at)
    gather.sent()


def entry(
    tokens, qkv_weight, up_weight, out_rows, silu_part, ada_weight, small, clip, sizes, call_id
):
    size, _, span = sizes
    group, share = 2 * span, out_rows.shape[0]
    rows, width = tokens.shape
    clips = silu_part.shape[0]
    block_rows = group * share
    columns = [qkv_weight.shape[1] // group, up_weight.shape[1] // group, width]
    count = 9 + 6 * clips
    vector = (count + -count % 8, width)
    shape = jax.ShapeDtypeStruct
    scratch = [pltpu.VMEM((group, share, n), BF16) for n in columns[:2]]
    scratch += [pltpu.VMEM((group, share, n), BF16) for n in columns]
    scratch += [pltpu.VMEM((block_rows, n), F32) for n in columns]
    scratch += [pltpu.VMEM((block_rows, columns[0]), BF16)]
    scratch += [pltpu.VMEM((columns[0], width), BF16)]
    scratch += [pltpu.VMEM(vector, F32), pltpu.VMEM((8, width), F32)]
    scratch += [pltpu.VMEM((group * rows, width), F32)]
    scratch += GroupSwap.scratch(span) * 3
    scratch += GroupGather.scratch(span, max(1, rows // 128))
    scratch += RingGather.scratch(size)
    scratch += AllSum.scratch(sizes, vector)
    return pl.pallas_call(
        functools.partial(entry_kernel, sizes, clips, min(256, rows)),
        out_shape=[
            shape((2, span, rows, width), BF16),
            shape((size, block_rows, columns[0]), BF16),
            shape((block_rows, width), BF16),
            shape((block_rows, columns[1]), BF16),
            shape(vector, F32),
            shape((group * rows, width), BF16),
            shape((columns[0], group * rows), BF16),
            shape((8 + 2 * clips + -2 * clips % 8, width), F32),
            shape((1, columns[1]), F32),
        ],
        in_specs=[HBM, CORE, CORE, HBM, CORE, CORE, CORE, pl.BlockSpec(memory_space=pltpu.SMEM)],
        out_specs=[CORE] * 9,
        scratch_shapes=scratch,
        compiler_params=pltpu.CompilerParams(
            collective_id=call_id, has_side_effects=True, vmem_limit_bytes=48 * MIB
        ),
        name="entry",
    )(tokens, qkv_weight, up_weight, out_rows, silu_part, ada_weight, small, clip)


def beside(job, total, places, count, first=0, stride=1):
    at = pl.program_id(0) * pl.num_programs(1) + pl.program_id(1)
    slots, event = {}, 0
    for place in range(first, total * places, stride):
        todo = list(range(event, min(event + count, job.events - 1)))
        if todo:
            slots[place] = todo
            event += len(todo)

    def ahead(place):
        for grid in range(total):
            todo = slots.get(grid * places + place)
            if todo:

                @pl.when(at == grid)
                def _():
                    for event in todo:
                        job.run(event)

    def finish():
        for late in range(event, job.events):
            job.run(late)

    return ahead, finish


def attention_kernel(sizes, factor, chunk, total, *refs):
    where = Where(sizes)
    ins, outs, scratch = take(refs, (5, 4, len(refs) - 9))
    q_ref, k_ref, v_ref, up_block, grad_block = ins
    out_ref, lse_ref, w_up, grad_all = outs
    sems = take(scratch, (3, 3))
    chunks = q_ref.shape[2] // chunk
    places = max(chunks // 2, 1)
    ahead, finish = beside(RingGather(where, up_block, w_up, sems[0]), total, places, 1)
    gather = GroupGather(where, grad_block, grad_all, sems[1], 2)
    at = pl.program_id(0) * pl.num_programs(1) + pl.program_id(1)

    @pl.when(at == 0)
    def _():
        greet(where.ring_peers() + where.group_peers())
        gather.run(0)

    keys = k_ref[0].T
    values_t = v_ref[0]
    for number in range(chunks):
        if number % 2 == 0:
            ahead(number // 2)
        span = slice(number * chunk, (number + 1) * chunk)
        scores = jnp.dot(keys, q_ref[0, :, span], preferred_element_type=F32) * factor
        top = jnp.max(scores, axis=0, keepdims=True)
        probs = jnp.exp2(scores - top)
        row_sum = jnp.sum(probs, axis=0, keepdims=True)
        mixed = jnp.dot(values_t, probs.astype(BF16), preferred_element_type=F32)
        out_ref[0, :, span] = (mixed / row_sum).astype(BF16)
        lse_ref[0, :, span] = top + jnp.log2(row_sum)

    @pl.when(at == total - 1)
    def _():
        gather.run(1)
        finish()
        gather.run(2)


def attention(qkv, up_block, grad_block, patches, sizes, call_id):
    size, _, span = sizes
    triple, dim, tokens = qkv.shape
    heads = triple // 3
    frames = tokens // patches
    block = (1, dim, patches)
    factor = LOG2E / math.sqrt(HEAD_DIM)
    shape = jax.ShapeDtypeStruct
    return pl.pallas_call(
        functools.partial(attention_kernel, sizes, factor, min(256, patches), frames * heads),
        out_shape=[
            shape((heads, dim, tokens), BF16),
            shape((heads, 1, tokens), F32),
            shape((size,) + up_block.shape, BF16),
            shape((2, span) + grad_block.shape, BF16),
        ],
        grid=(frames, heads),
        in_specs=[
            pl.BlockSpec(block, lambda f, h: (h, 0, f)),
            pl.BlockSpec(block, lambda f, h: (heads + h, 0, f)),
            pl.BlockSpec(block, lambda f, h: (2 * heads + h, 0, f)),
            HBM,
            HBM,
        ],
        out_specs=[
            pl.BlockSpec(block, lambda f, h: (h, 0, f)),
            pl.BlockSpec((1, 1, patches), lambda f, h: (h, 0, f)),
            HBM,
            HBM,
        ],
        scratch_shapes=RingGather.scratch(size) + GroupGather.scratch(span, 2),
        compiler_params=pltpu.CompilerParams(
            collective_id=call_id, has_side_effects=True, vmem_limit_bytes=32 * MIB
        ),
        cost_estimate=pl.CostEstimate(
            flops=4 * heads * patches * tokens * 256,
            bytes_accessed=4 * heads * dim * tokens * 2,
            transcendentals=heads * patches * tokens,
        ),
        name="attention",
    )(qkv, qkv, qkv, up_block, grad_block)


def attention_back_kernel(sizes, factor, chunk, total, *refs):
    where = Where(sizes)
    ins, outs, scratch = take(refs, (7, 3, len(refs) - 10))
    q_ref, k_ref, v_ref, g_ref, lse_ref, up_terms, half_terms = ins
    grads_ref, up_sum, half_sum = outs
    dk_sum, dv_sum = scratch[:2]
    own = take(scratch[2:], (4, 3))
    patches = q_ref.shape[2]
    chunks = patches // chunk
    places = max(chunks // 2, 1)
    ahead, finish = beside(RingSum(where, up_terms, up_sum, own[0]), total, places, 1)
    half = PatchSum(where, half_terms, half_sum, own[1])
    at = pl.program_id(0) * pl.num_programs(1) + pl.program_id(1)

    @pl.when(at == 0)
    def _():
        greet(where.ring_peers() + where.group_peers())
        half.run(0)

    keys_t = k_ref[0]
    keys = keys_t.T
    values = v_ref[0].T
    scale = factor / LOG2E
    for number in range(chunks):
        if number % 2 == 0:
            ahead(number // 2)
        span = slice(number * chunk, (number + 1) * chunk)
        queries_t = q_ref[0, :, span]
        grad_t = g_ref[0, :, span]
        scores = jnp.dot(keys, queries_t, preferred_element_type=F32) * factor
        probs = jnp.exp2(scores - lse_ref[0, :, span])
        grad_probs = jnp.dot(values, grad_t, preferred_element_type=F32)
        row_dot = jnp.sum(probs * grad_probs, axis=0, keepdims=True)
        grad_scores = (probs * (grad_probs - row_dot)).astype(BF16)
        probs_low = probs.astype(BF16)
        dq = jnp.dot(keys_t, grad_scores, preferred_element_type=F32)
        grads_ref[0, 0, :, span] = (dq * scale).astype(BF16)
        dims = (((1,), (1,)), ((), ()))
        dk = lax.dot_general(queries_t, grad_scores, dims, preferred_element_type=F32)
        dv = lax.dot_general(grad_t, probs_low, dims, preferred_element_type=F32)
        if number == 0:
            dk_sum[...] = dk
            dv_sum[...] = dv
        else:
            dk_sum[...] += dk
            dv_sum[...] += dv
    grads_ref[1, 0] = (dk_sum[...] * scale).astype(BF16)
    grads_ref[2, 0] = dv_sum[...].astype(BF16)

    @pl.when(at == total - 1)
    def _():
        finish()
        half.run(1)


def attention_back(qkv, grad, lse, up_terms, half_terms, patches, sizes, call_id):
    size, _, span = sizes
    triple, dim, tokens = qkv.shape
    heads = triple // 3
    frames = tokens // patches
    block = (1, dim, patches)
    factor = LOG2E / math.sqrt(HEAD_DIM)
    spec = pl.BlockSpec(block, lambda f, h: (h, 0, f))
    shape = jax.ShapeDtypeStruct
    return pl.pallas_call(
        functools.partial(attention_back_kernel, sizes, factor, min(256, patches), frames * heads),
        out_shape=[
            shape((3, heads, dim, tokens), BF16),
            shape(up_terms.shape[1:], BF16),
            shape(half_terms.shape[1:], F32),
        ],
        grid=(frames, heads),
        in_specs=[
            spec,
            pl.BlockSpec(block, lambda f, h: (heads + h, 0, f)),
            pl.BlockSpec(block, lambda f, h: (2 * heads + h, 0, f)),
            spec,
            pl.BlockSpec((1, 1, patches), lambda f, h: (h, 0, f)),
            CORE,
            CORE,
        ],
        out_specs=[pl.BlockSpec((3,) + block, lambda f, h: (0, h, 0, f)), CORE, CORE],
        scratch_shapes=[pltpu.VMEM((dim, patches), F32)] * 2
        + RingSum.scratch(size, *up_terms.shape[1:])
        + PatchSum.scratch(span, *half_terms.shape[1:]),
        compiler_params=pltpu.CompilerParams(
            collective_id=call_id, has_side_effects=True, vmem_limit_bytes=48 * MIB
        ),
        cost_estimate=pl.CostEstimate(
            flops=10 * heads * patches * tokens * 256,
            bytes_accessed=8 * heads * dim * tokens * 2,
            transcendentals=heads * patches * tokens,
        ),
        name="attention_back",
    )(qkv, qkv, qkv, grad, lse, up_terms, half_terms)


def joined(array):
    group, features, count = array.shape
    if features % 16:
        return array.astype(F32).reshape(group * features, count).astype(BF16)
    return array.reshape(group * features, count)


def middle_kernel(sizes, parts, *refs):
    where = Where(sizes)
    ins, outs, scratch = take(refs, (5, 6, len(refs) - 11))
    heads_t, out_block, tokens, vectors, down_block = ins
    attended, branch, midway, hidden_all, w_out, w_down = outs
    (hidden,), *sems = take(scratch, (1, 3, 3, 3, 5))
    greet(where.ring_peers() + where.group_peers())
    rows, width = tokens.shape
    span = where.span

    swap = GroupSwap(
        where,
        lambda dc, dx: heads_t.at[:, pl.ds((dc * span + dx) * rows, rows)],
        lambda dc, dx: attended.at[where.member],
        sems[0],
    )
    ring = RingGather(where, down_block, w_down, sems[1])
    gather = GroupGather(where, hidden, hidden_all, sems[2], parts)
    ring_out = RingGatherSplit(where, out_block, w_out, sems[3])
    swap.run(0)
    ring_out.run(0)
    for event in range(ring_out.events - 2):
        ring.run(event)
        ring_out.run(event + 1)
    event += 1
    swap.run(1)
    ring_out.run(ring_out.events - 1)
    size = rows // parts
    full = w_out[...].reshape(width, width)
    for part in range(parts):
        span_rows = slice(part * size, (part + 1) * size)
        mixed = joined(attended[:, :, span_rows])
        one = lax.dot_general(mixed, full, (((0,), (0,)), ((), ())), preferred_element_type=F32)
        one = one + vectors[6:7, :]
        branch[span_rows, :] = one
        mid = tokens[span_rows, :].astype(F32) + vectors[2:3, :] * one
        midway[span_rows, :] = mid
        normed, _ = layer_norm(mid)
        hidden[span_rows, :] = (normed * (1.0 + vectors[4:5, :]) + vectors[3:4, :]).astype(BF16)
        gather.start(part)
        if event < ring.events:
            ring.run(event)
            event += 1
    gather.keep().start()
    for event in range(event, ring.events):
        ring.run(event)
    for part in range(parts):
        gather.pass_on(part)
    gather.finish()
    gather.keep().wait()


def middle(heads_t, out_block, tokens, vectors, down_block, sizes, call_id):
    size, _, span = sizes
    rows, width = tokens.shape
    parts = rows // 128
    shape = jax.ShapeDtypeStruct
    return pl.pallas_call(
        functools.partial(middle_kernel, sizes, parts),
        out_shape=[
            shape((2 * span, heads_t.shape[0], rows), BF16),
            shape((rows, width), F32),
            shape((rows, width), F32),
            shape((2, span, rows, width), BF16),
            shape((size,) + out_block.shape, BF16),
            shape((size,) + down_block.shape, BF16),
        ],
        in_specs=[CORE, CORE, CORE, CORE, HBM],
        out_specs=[CORE] * 6,
        scratch_shapes=[pltpu.VMEM((rows, width), BF16)]
        + GroupSwap.scratch(span)
        + RingGather.scratch(size)
        + GroupGather.scratch(span, parts)
        + RingGatherSplit.scratch(size),
        compiler_params=pltpu.CompilerParams(
            collective_id=call_id, has_side_effects=True, vmem_limit_bytes=40 * MIB
        ),
        name="middle",
    )(heads_t, out_block, tokens, vectors, down_block)


def gelu_both(values_in):
    square = values_in * values_in
    inner = 0.7978845608028654 * values_in * (1.0 + 0.044715 * square)
    bent = jnp.tanh(inner)
    outer = 0.5 * (1.0 + bent)
    slope = 0.7978845608028654 * (1.0 + 3.0 * 0.044715 * square)
    return values_in * outer, outer + 0.5 * values_in * (1.0 - bent * bent) * slope


def feed_kernel(sizes, chunk, tile, *refs):
    where = Where(sizes)
    ins, outs, scratch = take(refs, (5, 5, len(refs) - 10))
    hidden, grad, w_up, w_down, bias = ins
    half, grad_hidden, g_up, down_sum, g_bias = outs
    (act, grad_pre, branch, back, g_down), *own = take(scratch, (5, 3, 6, 4))
    span = where.span
    rows, width = grad_hidden.shape
    units = bias.shape[1]
    sum_half = CoreSum(where, branch, half, own[0])
    sum_back = GroupSum(where, back, grad_hidden, own[1])
    ring = RingSum(where, g_down, down_sum, own[2])
    greet(where.ring_peers() + where.group_peers())
    each = rows // chunk
    steps = 2 * span * each
    across = (((1,), (1,)), ((), ()))
    over = (((0,), (0,)), ((), ()))

    def forward(step, total):
        here = pl.ds(pl.multiple_of(step * chunk, chunk), chunk)
        pre = jnp.dot(hidden[here, :], w_up[...], preferred_element_type=F32) + bias[...]
        value, slope = gelu_both(pre)
        act[here, :] = value.astype(BF16)
        grad_act = lax.dot_general(grad[here, :], w_down[...], across, preferred_element_type=F32)
        low = (grad_act * slope).astype(BF16)
        grad_pre[here, :] = low
        return total + jnp.sum(low.astype(F32), axis=0, keepdims=True)

    g_bias[...] = lax.fori_loop(0, steps, forward, jnp.zeros((1, units), F32))
    for low in range(0, units, tile):
        cut = slice(low, low + tile)
        found = lax.dot_general(act[:, cut], grad[...], over, preferred_element_type=F32)
        if len(g_down.shape) == 2:
            g_down[cut, :] = found.astype(BF16)
        else:
            size = g_down.shape[1]
            for at in range(tile // size):
                g_down[low // size + at] = found[at * size : (at + 1) * size].astype(BF16)
    ring.run(0)
    ring.run(1)

    def beside_ring(step, first, every, count):
        for at in range(count):
            if first + at < ring.events:
                pl.when(step == (at + 1) * every - 1)(functools.partial(ring.run, first + at))

    def backward(step, carry):
        at = step // each
        dx, dc = span - 1 - at // 2, 1 - at % 2
        inside = pl.ds(pl.multiple_of(step % each * chunk, chunk), chunk)
        first = pl.multiple_of((dc * span + dx) * rows + step % each * chunk, chunk)
        here = pl.ds(first, chunk)
        back[dc, dx, inside, :] = lax.dot_general(
            grad_pre[here, :], w_up[...], across, preferred_element_type=F32
        ).astype(BF16)
        for place in range(2 * span):
            done_dx, done_dc = span - 1 - place // 2, 1 - place % 2

            @pl.when(step == (place + 1) * each - 1)
            def _():
                if done_dc:
                    sum_back.cross(done_dx).start()
                elif done_dx:
                    sum_back.fold(done_dx)

        beside_ring(step, 2, 2, steps // 2)
        return carry

    lax.fori_loop(0, steps, backward, 0)
    event = min(2 + steps // 2, ring.events)

    def give(target, dc, first_event):
        def body(step, carry):
            dx = step // each
            inside = pl.ds(pl.multiple_of(step % each * chunk, chunk), chunk)
            first = pl.multiple_of(dc * span * rows + step * chunk, chunk)
            target[dx, inside, :] = jnp.dot(
                act[pl.ds(first, chunk), :], w_down[...], preferred_element_type=F32
            ).astype(BF16)
            beside_ring(step, first_event, 2, steps // 4)
            return carry

        lax.fori_loop(0, steps // 2, body, 0)
        return min(first_event + steps // 4, ring.events)

    event = give(branch, 1, event)
    for dx in range(span):
        sum_half.cross(dx).start()
    event = give(half, 0, event)
    for low in range(0, width, tile):
        if event < ring.events:
            ring.run(event)
            event += 1
        cut = slice(low, low + tile)
        g_up[cut, :] = lax.dot_general(
            hidden[:, cut], grad_pre[...], over, preferred_element_type=F32
        ).astype(BF16)
    for dx in range(span):
        sum_half.fold(dx)
    for event in range(event, ring.events):
        ring.run(event)
    sum_half.finish()
    sum_back.finish()


def feed(hidden, grad, w_up, w_down, bias, sizes, call_id):
    size, _, span = sizes
    tokens, width = hidden.shape
    units = w_up.shape[1]
    rows = tokens // (2 * span)
    block = (units // size, width)
    shape = jax.ShapeDtypeStruct
    return pl.pallas_call(
        functools.partial(feed_kernel, sizes, min(256, rows), 384 if units % 384 == 0 else units),
        out_shape=[
            shape((span, rows, width), BF16),
            shape((rows, width), F32),
            shape((width, units), BF16),
            shape(block, F32),
            shape((1, units), F32),
        ],
        in_specs=[CORE] * 5,
        out_specs=[CORE] * 5,
        scratch_shapes=[pltpu.VMEM((tokens, units), BF16)] * 2
        + [pltpu.VMEM((span, rows, width), BF16), pltpu.VMEM((2, span, rows, width), BF16)]
        + [pltpu.VMEM((size,) + block if block[0] % 16 else (units, width), BF16)]
        + CoreSum.scratch(span, rows, width)
        + GroupSum.scratch(span, rows, width)
        + RingSum.scratch(size, *block),
        compiler_params=pltpu.CompilerParams(
            collective_id=call_id, has_side_effects=True, vmem_limit_bytes=61 * MIB
        ),
        name="feed",
    )(hidden, grad, w_up, w_down, bias)


def return_kernel(sizes, parts, tile, *refs):
    where = Where(sizes)
    ins, outs, scratch = take(refs, (7, 4, len(refs) - 11))
    grad_hidden, midway, branch, grad_out, w_out, attended, vectors = ins
    grad_mid, grad_mix, g_out, sums = outs
    (grad_heads, grad_one), own = take(scratch, (2, 3 * parts))
    greet(where.group_peers())
    rows, width = midway.shape
    span = where.span
    size = rows // parts
    features = grad_heads.shape[1]
    swaps = []
    for part in range(parts):
        cut = pl.ds(part * size, size)

        def source(dc, dx, cut=cut):
            return grad_heads.at[where.peer_member(dc, dx), :, cut]

        def target(dc, dx, part=part):
            block = dc * span + (span - dx) % span
            return grad_mix.at[:, pl.ds(block * rows + part * size, size)]

        swaps.append(GroupSwap(where, source, target, own[3 * part : 3 * part + 3]))
    full = w_out[...]
    totals = [jnp.zeros((1, width), F32)] * 4
    for part in range(parts):
        here = slice(part * size, (part + 1) * size)
        normed, inv_std = layer_norm(midway[here, :])
        grad = grad_hidden[here, :]
        mid = grad_out[here, :].astype(F32) + norm_back(
            grad * (1.0 + vectors[4:5, :]), normed, inv_std
        )
        grad_mid[here, :] = mid
        low = (vectors[2:3, :] * mid).astype(BF16)
        grad_one[here, :] = low
        heads_t = lax.dot_general(full, low, (((1,), (1,)), ((), ())), preferred_element_type=F32)
        grad_heads[:, :, here] = heads_t.reshape(2 * span, features, size).astype(BF16)
        swaps[part].run(0)
        found = [grad, grad * normed, mid * branch[here, :], low.astype(F32)]
        totals = [
            total + jnp.sum(item, axis=0, keepdims=True) for total, item in zip(totals, found)
        ]
    for at, total in enumerate(totals):
        sums[at : at + 1, :] = total
    sums[4:8, :] = jnp.zeros((4, width), F32)
    for low in range(0, width, tile):
        cut = slice(low, low + tile)
        g_out[cut, :] = jnp.dot(
            attended[cut, :], grad_one[...], preferred_element_type=F32
        ).astype(BF16)
    for swap in swaps:
        swap.run(1)


def back_to_heads(
    grad_hidden, midway, branch, grad_out, w_out, attended, vectors, sizes, call_id
):
    span = sizes[2]
    rows, width = midway.shape
    group = 2 * span
    parts = rows // 128
    features = width // group
    shape = jax.ShapeDtypeStruct
    return pl.pallas_call(
        functools.partial(return_kernel, sizes, parts, 384),
        out_shape=[
            shape((rows, width), F32),
            shape((features, group * rows), BF16),
            shape((width, width), BF16),
            shape((8, width), F32),
        ],
        in_specs=[CORE] * 7,
        out_specs=[CORE] * 4,
        scratch_shapes=[
            pltpu.VMEM((group, features, rows), BF16),
            pltpu.VMEM((rows, width), BF16),
        ]
        + GroupSwap.scratch(span) * parts,
        compiler_params=pltpu.CompilerParams(
            collective_id=call_id, has_side_effects=True, vmem_limit_bytes=48 * MIB
        ),
        name="back_to_heads",
    )(grad_hidden, midway, branch, grad_out, w_out, attended, vectors)


def last_kernel(sizes, chunk, tile, clips, *refs):
    where = Where(sizes)
    ins, outs, scratch = take(refs, (11, 6, len(refs) - 17))
    grad_qkv, hidden, tokens, w_qkv, grad_mid, out_terms, early, own_rows = ins[:8]
    midway, branch, grad_out = ins[8:]
    tokens_grad, output, qkv_sum, out_sum, early_sum, late_sum = outs
    (back, g_qkv, late, grad_hidden, spread), *own = take(scratch, (5, 6, 4, 4, 4, 7))
    span = where.span
    rows, width = grad_mid.shape
    sum_back = GroupSum(where, back, grad_hidden, own[0])
    ring = RingSum(where, g_qkv, qkv_sum, own[1])
    first_sums = AllSum(where, sizes, early, early_sum, own[2])
    sums = AllSum(where, sizes, late, late_sum, own[3], (0, 1, 2))
    ring_out = RingSumSplit(where, out_terms, out_sum, own[4])
    greet(where.ring_peers() + where.group_peers() + sums.peers)
    ring_out.run(0)
    first_sums.run(0)
    each = rows // chunk
    blocks = 2 * span
    far = 2 * (span - 1) * each
    planned = {far + at: [(ring, 2 + at)] for at in range(2 * each)}
    planned[far + 1].append((first_sums, 3))
    planned[far + 2 * each - 1] += [(ring_out, 3), (first_sums, 4)] if each > 1 else []

    def body(step, totals):
        at = step // each
        dx, dc = span - 1 - at // 2, 1 - at % 2
        inside = pl.ds(pl.multiple_of(step % each * chunk, chunk), chunk)
        first = pl.multiple_of((dc * span + dx) * rows + step % each * chunk, chunk)
        here = pl.ds(first, chunk)
        term = lax.dot_general(
            grad_qkv[:, here], w_qkv[...], (((0,), (1,)), ((), ())), preferred_element_type=F32
        )
        back[dc, dx, inside, :] = term.astype(BF16)
        normed, _ = layer_norm(tokens[here, :].astype(F32))
        shift = jnp.sum(term, axis=0, keepdims=True)
        scale = jnp.sum(term * normed, axis=0, keepdims=True)
        other = dc.astype(F32)
        for place in range(blocks):
            done_dx, done_dc = span - 1 - place // 2, 1 - place % 2

            @pl.when(step == (place + 1) * each - 1)
            def _():
                if done_dc:
                    sum_back.cross(done_dx).start()
                elif done_dx:
                    sum_back.fold(done_dx)

        for when, todo in planned.items():

            @pl.when(step == when)
            def _():
                for job, event in todo:
                    job.run(event)

        own_part, other_part = 1.0 - other, other
        return (
            totals[0] + own_part * shift,
            totals[1] + own_part * scale,
            totals[2] + other_part * shift,
            totals[3] + other_part * scale,
        )

    zero = jnp.zeros((1, width), F32)
    totals = lax.fori_loop(0, far, body, (zero,) * 4)
    first_sums.run(1)
    ring_out.run(1)
    for low in range(0, width, tile):
        cut = slice(low, low + tile)
        g_qkv[cut, :] = lax.dot_general(
            hidden[:, cut], grad_qkv[...], (((0,), (1,)), ((), ())), preferred_element_type=F32
        ).astype(BF16)
    ring.run(0)
    ring.run(1)
    first_sums.run(2)
    ring_out.run(2)
    totals = lax.fori_loop(far, blocks * each, body, totals)
    late[...] = jnp.zeros_like(late)
    for clip in range(clips):
        for part in range(2):
            at = 2 * clip + part
            late[at : at + 1, :] = (
                own_rows[8 + clip : 9 + clip, :] * totals[part]
                + own_rows[8 + clips + clip : 9 + clips + clip, :] * totals[2 + part]
            )
    gate = jnp.zeros((1, width), F32)
    part = min(128, rows)
    for low in range(0, rows, part):
        here = slice(low, low + part)
        two = branch[here, :] + own_rows[7:8, :]
        output[here, :] = (midway[here, :] + own_rows[5:6, :] * two).astype(BF16)
        gate = gate + jnp.sum(grad_out[here, :].astype(F32) * two, axis=0, keepdims=True)
    for clip in range(clips):
        late[2 * clips + clip : 2 * clips + clip + 1, :] = own_rows[8 + clip : 9 + clip, :] * gate
    features = grad_qkv.shape[0] // 3
    ones = jnp.ones((8, grad_qkv.shape[1]), BF16)
    head_sums = lax.dot_general(
        ones, grad_qkv[...], (((1,), (1,)), ((), ())), preferred_element_type=F32
    )
    spread[...] = jnp.zeros_like(spread)
    spread[0:1, :features] = head_sums[0:1, :features]
    spread[1:2, :features] = head_sums[0:1, 2 * features :]
    late[3 * clips : 3 * clips + 2, :] = pltpu.roll(
        spread[...], where.member * features, 1
    )[0:2]
    sums.run(0)

    def own_tokens():
        sum_back.finish()
        part = min(128, rows)
        for low in range(0, rows, part):
            here = slice(low, low + part)
            normed, inv_std = layer_norm(tokens[here, :].astype(F32))
            grad = grad_hidden[here, :] * (1.0 + own_rows[1:2, :])
            tokens_grad[here, :] = (
                grad_mid[here, :] + norm_back(grad, normed, inv_std)
            ).astype(BF16)

    ran = [item for todo in planned.values() for item in todo]
    todo = [(ring_out, at) for at in range(3, ring_out.events)]
    todo += [(first_sums, at) for at in range(3, first_sums.events)]
    todo = [item for item in todo if item not in ran]
    late_todo = list(range(1, sums.events - 1))
    for event in range(2 + len(planned), ring.events):
        ring.run(event)
        if todo:
            job, at = todo.pop(0)
            job.run(at)
        if event % 2 and late_todo:
            sums.run(late_todo.pop(0))
        if event == ring.events - 3:
            own_tokens()
    for job, at in todo:
        job.run(at)
    for at in late_todo:
        sums.run(at)
    sums.run(sums.events - 1)


def back_to_tokens(
    grad_qkv,
    hidden,
    tokens,
    w_qkv,
    grad_mid,
    out_terms,
    early,
    own_rows,
    midway,
    branch,
    grad_out,
    clips,
    sizes,
    call_id,
):
    size, _, span = sizes
    count, width = tokens.shape
    rows = count // (2 * span)
    features = grad_qkv.shape[0]
    block_rows = width // size
    late = (3 * clips + 2 + (-3 * clips - 2) % 8, width)
    shape = jax.ShapeDtypeStruct
    return pl.pallas_call(
        functools.partial(last_kernel, sizes, min(256, rows), 384, clips),
        out_shape=[
            shape((rows, width), BF16),
            shape((rows, width), BF16),
            shape((block_rows, features), BF16),
            shape((block_rows, width), BF16),
            shape(early.shape, F32),
            shape(late, F32),
        ],
        in_specs=[CORE] * 11,
        out_specs=[CORE] * 6,
        scratch_shapes=[
            pltpu.VMEM((2, span, rows, width), BF16),
            pltpu.VMEM((width, features), BF16),
            pltpu.VMEM(late, F32),
            pltpu.VMEM((rows, width), F32),
            pltpu.VMEM((8, width), F32),
        ]
        + GroupSum.scratch(span, rows, width)
        + RingSum.scratch(size, block_rows, features)
        + AllSum.scratch(sizes, early.shape)
        + AllSum.scratch(sizes, late)
        + RingSumSplit.scratch(size, block_rows, width),
        compiler_params=pltpu.CompilerParams(
            collective_id=call_id, has_side_effects=True, vmem_limit_bytes=60 * MIB
        ),
        name="back_to_tokens",
    )(
        grad_qkv,
        hidden,
        tokens,
        w_qkv,
        grad_mid,
        out_terms,
        early,
        own_rows,
        midway,
        branch,
        grad_out,
    )


def final_kernel(sizes, *refs):
    where = Where(sizes)
    ins, outs, scratch = take(refs, (4, 4, len(refs) - 8))
    summed, share_qkv, share_up, share_out = outs
    got, own = scratch[:3], take(scratch[3:], (4, 3, 3, 3))
    sums = AllSum(where, sizes, ins[0], summed, own[0])
    greet(where.group_peers() + sums.peers)
    swaps = [
        GroupSwap(
            where,
            lambda dc, dx, source=ins[at + 1]: source.at[where.peer_member(dc, dx)],
            lambda dc, dx, target=got[at]: target.at[where.member],
            own[at + 1],
        )
        for at in range(3)
    ]
    sums.run(0)
    for swap in swaps:
        swap.run(0)
    for event in range(1, sums.events):
        sums.run(event)
    group, _, three = got[0].shape
    features = three // 3
    swaps[0].run(1)
    for member in range(group):
        piece = got[0][member].astype(F32)
        for part in range(3):
            low = (part * group + member) * features
            share_qkv[:, low : low + features] = piece[:, part * features : (part + 1) * features]
    swaps[1].run(1)
    units = got[1].shape[2] // where.size
    for member in range(group):
        piece = got[1][member].astype(F32)
        for ring in range(where.size):
            low = (ring * group + member) * units
            share_up[:, low : low + units] = piece[:, ring * units : (ring + 1) * units]
    swaps[2].run(1)
    total = got[2][0].astype(F32)
    for member in range(1, group):
        total = total + got[2][member].astype(F32)
    share_out[...] = total


def final(block, pieces, sizes, call_id):
    group, share, _ = pieces[0].shape
    shape = jax.ShapeDtypeStruct
    return pl.pallas_call(
        functools.partial(final_kernel, sizes),
        out_shape=[
            shape(block.shape, F32),
            shape((share, group * pieces[0].shape[2]), F32),
            shape((share, group * pieces[1].shape[2]), F32),
            shape((share, pieces[2].shape[2]), F32),
        ],
        in_specs=[CORE] * 4,
        out_specs=[CORE] * 4,
        scratch_shapes=[pltpu.VMEM(item.shape, BF16) for item in pieces]
        + AllSum.scratch(sizes, block.shape)
        + GroupSwap.scratch(sizes[2]) * 3,
        compiler_params=pltpu.CompilerParams(
            collective_id=call_id, has_side_effects=True, vmem_limit_bytes=32 * MIB
        ),
        name="final",
    )(block, *pieces)


def per_device(
    tokens,
    cotangent,
    clip_embed,
    timesteps,
    frame_clip,
    ada_weight,
    ada_bias,
    qkv_weight,
    query_bias,
    value_bias,
    out_weight,
    out_bias,
    up_weight,
    up_bias,
    down_weight,
    down_bias,
):
    ring_size, patch_size = lax.axis_size("ring"), lax.axis_size("patch")
    sizes = (ring_size, 2, patch_size)
    group = 2 * patch_size
    device_count = ring_size * group
    ring, core, patch = (lax.axis_index(name) for name in ("ring", "core", "patch"))
    member = core * patch_size + patch
    device = ring * group + member
    rows, width = tokens.shape[1:]
    tokens, cotangent = tokens[0], cotangent[0]
    patches = patch_size * rows
    clips = clip_embed.shape[0]
    hidden = up_weight.shape[1]
    share = width // device_count
    heads = HEADS // group
    head_width = heads * HEAD_DIM
    units = hidden // group
    mine = jnp.arange(group) == member
    mine_of_all = jnp.arange(device_count) == device

    condition = clip_embed + sinusoid(timesteps, width)
    silu_cond, silu_back = jax.vjp(jax.nn.silu, condition)
    silu_low = silu_cond.astype(BF16)
    silu_part = lax.dynamic_slice_in_dim(silu_low, device * share, share, 1)
    small = jnp.concatenate(
        [query_bias, value_bias, out_bias, down_bias, up_bias, ada_bias]
    ).astype(F32)[None, :]

    tokens_all, w_qkv, out_block, up_block, _, hidden_one, projected, own_rows, b_up = entry(
        tokens,
        qkv_weight,
        up_weight,
        out_weight,
        silu_part,
        ada_weight,
        small,
        frame_clip,
        sizes,
        1,
    )
    w_qkv = w_qkv.reshape(width, 3 * head_width)
    gate_two = own_rows[5]
    qkv = projected.reshape(3 * heads, HEAD_DIM, 2 * patches)
    grad_out = cotangent.astype(F32)
    grad_branch_two = (gate_two * grad_out).astype(BF16)
    attended_t, lse, w_up, gb_two_all = attention(
        qkv, up_block, grad_branch_two, patches, sizes, 2
    )
    w_up = w_up.reshape(width, units)

    attended, branch_one, midway, hidden_two_all, w_out, w_down = middle(
        attended_t.reshape(head_width, 2 * patches),
        out_block,
        tokens,
        own_rows,
        down_weight,
        sizes,
        3,
    )
    attended = attended.reshape(width, rows)
    w_out = w_out.reshape(width, width)
    w_down = w_down.reshape(units, width)

    branch_half, grad_hidden_two, g_up, share_down, g_up_b = feed(
        hidden_two_all.reshape(2 * patches, width),
        gb_two_all.reshape(2 * patches, width),
        w_up,
        w_down,
        b_up,
        sizes,
        4,
    )
    g_up_b = g_up_b[0]
    g_down_b = jnp.sum(grad_branch_two.astype(F32), axis=0)
    block_rows = width // ring_size
    grad_midway, grad_mix, g_out, own_sums = back_to_heads(
        grad_hidden_two,
        midway,
        branch_one,
        cotangent,
        w_out,
        attended,
        own_rows,
        sizes,
        5,
    )
    grad_shift_two, grad_scale_two, grad_gate_one, g_out_b = (own_sums[at] for at in range(4))

    grad_projected, sum_up, branch_two = attention_back(
        qkv,
        grad_mix.reshape(heads, HEAD_DIM, 2 * patches),
        lse,
        g_up.reshape(ring_size, block_rows, units),
        branch_half,
        patches,
        sizes,
        6,
    )
    grad_projected = grad_projected.reshape(3 * head_width, 2 * patches)

    frame_grads = jnp.stack([grad_gate_one, grad_shift_two, grad_scale_two])
    early = jnp.concatenate(
        [
            (own_rows[8 : 8 + clips, None] * frame_grads[None]).reshape(3 * clips, width),
            jnp.stack([g_out_b, g_down_b]),
            jnp.where(mine[None, :, None], g_up_b.reshape(ring_size, 1, -1), 0.0).reshape(
                -1, width
            ),
        ]
    )
    early = jnp.pad(early, ((0, -early.shape[0] % 8), (0, 0)))
    tokens_grad, output, sum_qkv, sum_out, early_sum, late_sum = back_to_tokens(
        grad_projected,
        hidden_one,
        tokens_all.reshape(2 * patches, width),
        w_qkv,
        grad_midway,
        g_out.reshape(ring_size, block_rows, width),
        early,
        own_rows,
        midway,
        branch_two,
        cotangent,
        clips,
        sizes,
        7,
    )
    first = late_sum[: 2 * clips].reshape(clips, 2 * width)
    second = early_sum[: 3 * clips].reshape(clips, 3 * width)
    third = late_sum[2 * clips : 3 * clips]
    mod_low = jnp.concatenate([first, second, third], axis=1).astype(BF16)
    query_b_all, value_b_all = (late_sum[3 * clips + at] for at in range(2))
    out_b_all, down_b_all = (early_sum[3 * clips + at] for at in range(2))
    up_b_all = early_sum[3 * clips + 2 :].reshape(-1)[:hidden]

    def own(vector):
        length = vector.shape[0] // device_count
        return lax.dynamic_slice_in_dim(vector, device * length, length, 0)

    ada_bias_grad = own(jnp.sum(mod_low.astype(F32), axis=0))
    ada_weight_grad = lax.dot_general(
        silu_part, mod_low, (((0,), (0,)), ((), ())), preferred_element_type=F32
    )
    grad_silu_part = lax.dot_general(
        mod_low, ada_weight, (((1,), (1,)), ((), ())), preferred_element_type=F32
    )
    spread = jnp.where(mine_of_all[None, :, None], grad_silu_part[:, None, :], 0.0).reshape(-1)
    grad_silu, share_qkv, share_up, share_out = final(
        flat_block(spread),
        [item.reshape(group, share, -1) for item in (sum_qkv, sum_up, sum_out)],
        sizes,
        8,
    )
    grad_silu = grad_silu.reshape(-1)[: clips * width].reshape(clips, width)
    clip_grad = silu_back(grad_silu)[0]

    return (
        output[None],
        tokens_grad[None],
        clip_grad,
        ada_weight_grad,
        ada_bias_grad,
        share_qkv,
        own(query_b_all),
        own(value_b_all),
        share_out,
        own(out_b_all),
        share_up,
        own(up_b_all),
        share_down,
        own(down_b_all),
    )


def solution(mesh):
    frames, patch = mesh.shape["frames"], mesh.shape["patch"]
    inner = Mesh(mesh.devices.reshape(frames // 2, 2, patch), ("ring", "core", "patch"))
    every = ("ring", "core", "patch")
    tokens = P(("ring", "core"), "patch", None)
    matrix = P(every, None)
    vector = P(every)
    return jax.shard_map(
        per_device,
        mesh=inner,
        in_specs=(
            tokens,
            tokens,
            P(),
            P(),
            P(("ring", "core")),
            matrix,
            vector,
            matrix,
            vector,
            vector,
            matrix,
            vector,
            matrix,
            vector,
            matrix,
            vector,
        ),
        out_specs=(
            tokens,
            tokens,
            P(),
            matrix,
            vector,
            matrix,
            vector,
            vector,
            matrix,
            vector,
            matrix,
            vector,
            matrix,
            vector,
        ),
        check_vma=False,
    )
```

```python
import functools
import math

import jax
import jax.numpy as jnp
from jax import lax
from jax.experimental import pallas as pl
from jax.experimental.pallas import tpu as pltpu
from jax.sharding import Mesh
from jax.sharding import PartitionSpec as P

HEADS = 16
HEAD_DIM = 72
BF16 = jnp.bfloat16
F32 = jnp.float32
LOG2E = 1.4426950408889634
MESH_ID = pl.DeviceIdType.MESH
MIB = 2**20


def layer_norm(values_in):
    centre = values_in - jnp.mean(values_in, axis=-1, keepdims=True)
    spread = jnp.mean(centre * centre, axis=-1, keepdims=True)
    inv_std = lax.rsqrt(spread + 1e-06)
    return (centre * inv_std, inv_std)


def norm_back(grad_normed, normed, inv_std):
    mean_grad = jnp.mean(grad_normed, axis=-1, keepdims=True)
    mean_prod = jnp.mean(grad_normed * normed, axis=-1, keepdims=True)
    return (grad_normed - mean_grad - normed * mean_prod) * inv_std


def gelu_tanh(values_in):
    inner = 0.7978845608028654 * (values_in + 0.044715 * values_in * values_in * values_in)
    return 0.5 * values_in * (1.0 + jnp.tanh(inner))


def sinusoid(steps_in, width_in):
    half_width = width_in // 2
    freqs = jnp.exp(-math.log(10000.0) * jnp.arange(half_width, dtype=jnp.float32) / half_width)
    angles = steps_in.astype(jnp.float32)[:, None] * freqs[None, :]
    return jnp.concatenate([jnp.cos(angles), jnp.sin(angles)], axis=1)


class Where:
    def __init__(self, sizes):
        self.size, _, self.span = sizes
        self.ring, self.core, self.patch = (
            lax.axis_index(name) for name in ("ring", "core", "patch")
        )
        along, across = self.ring // 2, self.ring % 2
        self.place = (1 - across) * along + across * (self.size - 1 - along)
        self.member = self.core * self.span + self.patch

    def at_place(self, place):
        place = (place + 2 * self.size) % self.size
        back = place // (self.size // 2)
        return (1 - back) * 2 * place + back * (2 * (self.size - 1 - place) + 1)

    def neighbour(self, step):
        return (self.at_place(self.place + step), self.core, self.patch)

    def peer(self, dc, dx):
        core = 1 - self.core if dc else self.core
        return (self.ring, core, (self.patch + dx) % self.span)

    def peer_member(self, dc, dx):
        _, core, patch = self.peer(dc, dx)
        return core * self.span + patch

    def ring_peers(self):
        return [self.neighbour(1), self.neighbour(-1)]

    def group_peers(self):
        return [
            self.peer(dc, dx) for dc in range(2) for dx in range(self.span) if dc or dx
        ]


def greet(peers):
    barrier = pltpu.get_barrier_semaphore()
    for peer in peers:
        pl.semaphore_signal(barrier, inc=1, device_id=peer, device_id_type=MESH_ID)
    pl.semaphore_wait(barrier, len(peers))


def remote(source, target, send_sem, recv_sem, peer):
    return pltpu.make_async_remote_copy(
        src_ref=source,
        dst_ref=target,
        send_sem=send_sem,
        recv_sem=recv_sem,
        device_id=peer,
        device_id_type=MESH_ID,
    )


def strands(rows, columns):
    by_rows = rows % 16 == 0
    tile = 16 if by_rows else 128
    tiles = (rows if by_rows else columns) // tile
    sizes = [tiles // 4 + (at < tiles % 4) for at in range(4)]
    found, low = [], 0
    for at, count in enumerate(sizes):
        cut = pl.ds(low * tile, count * tile)
        found.append((at // 2, (cut, slice(None)) if by_rows else (slice(None), cut)))
        low += count
    return found


class RingGather:
    @staticmethod
    def scratch(size):
        dma = pltpu.SemaphoreType.DMA
        return [dma((4, size - 1)), dma((4, size - 1)), dma((1,))]

    def __init__(self, where, block, out, sems):
        self.where, self.block, self.out = where, block, out
        self.send, self.recv, self.own = sems
        self.parts = strands(*block.shape)
        self.events = 2 * (where.size - 1) + 1

    def keep(self):
        return pltpu.make_async_copy(self.block, self.out.at[self.where.ring], self.own.at[0])

    def copy(self, at, step):
        where = self.where
        way, part = self.parts[at]
        sign = (-1, 1)[way]
        slot = where.at_place(where.place + sign * step)
        target = self.out.at[(slot,) + part]
        source = target if step else self.block.at[part]
        return remote(
            source, target, self.send.at[at, step], self.recv.at[at, step], where.neighbour(-sign)
        )

    def run(self, event):
        step, piece = event // 2, event % 2
        if event == 0:
            self.keep().start()
        if event < self.events - 1:
            for at in (piece, piece + 2):
                if step:
                    self.copy(at, step - 1).wait_recv()
                self.copy(at, step).start()
        else:
            for at in range(4):
                self.copy(at, step - 1).wait_recv()
                for past in range(step):
                    self.copy(at, past).wait_send()
            self.keep().wait()


class RingGatherSplit:
    @staticmethod
    def scratch(size):
        dma, half = pltpu.SemaphoreType.DMA, size // 2
        return [dma((2, half))] * 4 + [dma((1,))]

    def __init__(self, where, block, out, sems):
        self.where, self.block, self.out = where, block, out
        self.send, self.recv, self.send_core, self.recv_core, self.own = sems
        self.half = where.size // 2
        self.events = self.half + 2
        cut = -(-block.shape[0] // 32) * 16
        self.parts = (pl.ds(0, cut), pl.ds(cut, block.shape[0] - cut))

    def keep(self):
        return pltpu.make_async_copy(self.block, self.out.at[self.where.ring], self.own.at[0])

    def slot(self, step, at):
        where = self.where
        place = where.at_place(where.place + (2 * where.core - 1) * step)
        return self.out.at[place, self.parts[at]]

    def copy(self, step, at):
        where = self.where
        target = self.slot(step, at)
        source = target if step else self.block.at[self.parts[at]]
        peer = where.neighbour(1 - 2 * where.core)
        return remote(source, target, self.send.at[at, step], self.recv.at[at, step], peer)

    def hand(self, step, at):
        target = self.slot(step + 1, at)
        return remote(
            target,
            target,
            self.send_core.at[at, step],
            self.recv_core.at[at, step],
            self.where.peer(1, 0),
        )

    def run(self, step):
        half = self.half
        if step == 0:
            self.keep().start()
        for at in range(2):
            if 0 < step <= half:
                self.copy(step - 1, at).wait_recv()
            if step < half:
                self.copy(step, at).start()
            if 0 < step < half:
                self.hand(step - 1, at).start()
            if step == half + 1:
                for past in range(half):
                    self.copy(past, at).wait_send()
                for past in range(half - 1):
                    self.hand(past, at).wait()
        if step == half + 1:
            self.keep().wait()


class RingSum:
    @staticmethod
    def scratch(size, rows, columns):
        dma = pltpu.SemaphoreType.DMA
        slots = pltpu.VMEM((size - 1, rows, columns), BF16)
        return [slots, slots, dma((4, size - 1)), dma((4, size - 1))]

    def __init__(self, where, terms, out, scratch):
        self.where, self.terms, self.out = where, terms, out
        self.held, self.landed, self.send, self.recv = scratch
        self.parts = strands(*out.shape)
        self.events = 2 * where.size

    def copy(self, at, step):
        way, part = self.parts[at]
        part = (step,) + part
        return remote(
            self.held.at[part],
            self.landed.at[part],
            self.send.at[at, step],
            self.recv.at[at, step],
            self.where.neighbour((1, -1)[way]),
        )

    def term(self, slot, part):
        if len(self.terms.shape) == 3:
            return self.terms[(slot,) + part]
        rows = self.out.shape[0]
        first = pl.multiple_of(slot * rows + part[0].start, 16)
        return self.terms[(pl.ds(first, part[0].size), part[1])]

    def run(self, event):
        step, piece = event // 2, event % 2
        where, last = self.where, self.where.size - 2
        for at in (piece, piece + 2):
            way, part = self.parts[at]
            slot = where.at_place(where.place + (-1, 1)[way] * (step + 1))
            total = self.term(slot, part)
            if step:
                self.copy(at, step - 1).wait_recv()
                total = total.astype(F32) + self.landed[(step - 1,) + part].astype(F32)
            if step <= last:
                self.held[(step,) + part] = total.astype(BF16)
                self.copy(at, step).start()
            else:
                self.out[part] = total.astype(self.out.dtype)
        if event == self.events - 1:
            for at in range(4):
                for past in range(last + 1):
                    self.copy(at, past).wait_send()


class RingSumSplit:
    @staticmethod
    def scratch(size, rows, columns):
        dma, half = pltpu.SemaphoreType.DMA, size // 2
        slots = pltpu.VMEM((half, rows, columns), BF16)
        return [slots] * 3 + [dma((half,)), dma((half,)), dma((2, half)), dma((2, half))]

    def __init__(self, where, terms, out, scratch):
        self.where, self.terms, self.out = where, terms, out
        self.given, self.held, self.landed, *sems = scratch
        self.send_core, self.recv_core, self.send, self.recv = sems
        self.half = where.size // 2
        self.events = self.half + 1
        rows = out.shape[0]
        cut = -(-rows // 32) * 16
        self.parts = (pl.ds(0, cut), pl.ds(cut, rows - cut))

    def slot(self, step, side):
        return self.where.at_place(self.where.place + side * (self.half - step))

    def give(self, step):
        side = 2 * self.where.core - 1
        return remote(
            self.terms.at[self.slot(step, side)],
            self.given.at[step],
            self.send_core.at[step],
            self.recv_core.at[step],
            self.where.peer(1, 0),
        )

    def copy(self, step, at):
        return remote(
            self.held.at[step, self.parts[at]],
            self.landed.at[step, self.parts[at]],
            self.send.at[at, step],
            self.recv.at[at, step],
            self.where.neighbour(1 - 2 * self.where.core),
        )

    def run(self, step):
        half, core = self.half, self.where.core
        if step == 0:
            for at in range(half):
                self.give(at).start()
        if step < half:
            self.give(step).wait_recv()
            slot = self.slot(step, 1 - 2 * core)
        for at, rows in enumerate(self.parts):
            if step < half:
                total = self.terms[slot, rows].astype(F32) + self.given[step, rows].astype(F32)
                if step == 0:
                    total = total * (1 - core).astype(F32)
            else:
                total = self.terms[self.where.ring, rows].astype(F32)
            if step:
                self.copy(step - 1, at).wait_recv()
                total = total + self.landed[step - 1, rows].astype(F32)
            if step < half:
                self.held[step, rows] = total.astype(BF16)
                self.copy(step, at).start()
            else:
                self.out[rows] = total.astype(self.out.dtype)
        if step == half:
            for past in range(half):
                self.give(past).wait_send()
                for at in range(2):
                    self.copy(past, at).wait_send()


class GroupGather:
    @staticmethod
    def scratch(span, parts=1):
        dma = pltpu.SemaphoreType.DMA
        return [dma((2, span, parts)), dma((2, span, parts)), dma((1,))]

    def __init__(self, where, block, out, sems, parts=1):
        self.where, self.block, self.out, self.parts = where, block, out, parts
        self.send, self.recv, self.own = sems

    def rows(self, part):
        size = self.block.shape[0] // self.parts
        return pl.ds(part * size, size)

    def hop(self, dx, part):
        where, rows = self.where, self.rows(part)
        at = (0, dx, part)
        return remote(
            self.block.at[rows],
            self.out.at[0, dx, rows],
            self.send.at[at],
            self.recv.at[at],
            where.peer(0, where.span - dx),
        )

    def cross(self, dx, part):
        rows = self.rows(part)
        source = self.out.at[0, dx, rows] if dx else self.block.at[rows]
        at = (1, dx, part)
        return remote(
            source,
            self.out.at[1, dx, rows],
            self.send.at[at],
            self.recv.at[at],
            self.where.peer(1, 0),
        )

    def start(self, part):
        for dx in range(1, self.where.span):
            self.hop(dx, part).start()
        self.cross(0, part).start()

    def pass_on(self, part):
        for dx in range(1, self.where.span):
            self.hop(dx, part).wait_recv()
            self.cross(dx, part).start()

    def arrived(self, dx):
        for part in range(self.parts):
            self.cross(dx, part).wait_recv()

    def sent(self):
        for part in range(self.parts):
            for dx in range(self.where.span):
                if dx:
                    self.hop(dx, part).wait_send()
                self.cross(dx, part).wait_send()

    def finish(self):
        for dx in range(self.where.span):
            self.arrived(dx)
        self.sent()

    def keep(self):
        return pltpu.make_async_copy(self.block, self.out.at[0, 0], self.own.at[0])

    def run(self, step):
        if step == 0:
            self.keep().start()
            for part in range(self.parts):
                self.start(part)
        elif step == 1:
            for part in range(self.parts):
                self.pass_on(part)
        else:
            self.finish()
            self.keep().wait()


class GroupSwap:
    @staticmethod
    def scratch(span):
        dma = pltpu.SemaphoreType.DMA
        return [dma((2, span)), dma((2, span)), dma((1,))]

    def __init__(self, where, source, target, sems):
        self.where, self.source, self.target = where, source, target
        self.send, self.recv, self.own = sems

    def run(self, step):
        where = self.where
        keep = pltpu.make_async_copy(self.source(0, 0), self.target(0, 0), self.own.at[0])
        copies = [
            remote(
                self.source(dc, dx),
                self.target(dc, dx),
                self.send.at[dc, dx],
                self.recv.at[dc, dx],
                where.peer(dc, dx),
            )
            for dx in reversed(range(where.span))
            for dc in range(2)
            if dc or dx
        ]
        if step == 0:
            for copy in copies:
                copy.start()
            keep.start()
        else:
            for copy in copies:
                copy.wait()
            keep.wait()


class GroupSum:
    @staticmethod
    def scratch(span, rows, columns):
        dma = pltpu.SemaphoreType.DMA
        slots = pltpu.VMEM((span, rows, columns), BF16)
        fewer = pltpu.VMEM((max(1, span - 1), rows, columns), BF16)
        return [slots, fewer, dma((span,)), dma((span,)), dma((span,)), dma((span,))]

    def __init__(self, where, terms, out, scratch):
        self.where, self.terms, self.out = where, terms, out
        self.crossed, self.landed, *sems = scratch
        self.send_core, self.recv_core, self.send, self.recv = sems

    def cross(self, dx):
        return remote(
            self.terms.at[1, dx],
            self.crossed.at[dx],
            self.send_core.at[dx],
            self.recv_core.at[dx],
            self.where.peer(1, 0),
        )

    def hop(self, dx):
        return remote(
            self.crossed.at[dx],
            self.landed.at[dx - 1],
            self.send.at[dx],
            self.recv.at[dx],
            self.where.peer(0, dx),
        )

    def fold(self, dx):
        self.cross(dx).wait_recv()
        total = self.terms[0, dx].astype(F32) + self.crossed[dx].astype(F32)
        self.crossed[dx] = total.astype(BF16)
        self.hop(dx).start()

    def finish(self):
        self.cross(0).wait_recv()
        total = self.terms[0, 0].astype(F32) + self.crossed[0].astype(F32)
        for dx in range(1, self.where.span):
            self.hop(dx).wait_recv()
            total = total + self.landed[dx - 1].astype(F32)
        self.out[...] = total.astype(self.out.dtype)
        for dx in range(self.where.span):
            self.cross(dx).wait_send()
            if dx:
                self.hop(dx).wait_send()

    def run(self, step):
        later = list(reversed(range(self.where.span)))
        if step == 0:
            for dx in later:
                self.cross(dx).start()
        elif step == 1:
            for dx in later[:-1]:
                self.fold(dx)
        else:
            self.finish()


class CoreSum:
    @staticmethod
    def scratch(span, rows, columns):
        dma = pltpu.SemaphoreType.DMA
        return [pltpu.VMEM((span, rows, columns), BF16), dma((span,)), dma((span,))]

    def __init__(self, where, terms, out, scratch):
        self.where, self.terms, self.out = where, terms, out
        self.crossed, self.send_core, self.recv_core = scratch

    def cross(self, dx):
        return remote(
            self.terms.at[dx],
            self.crossed.at[dx],
            self.send_core.at[dx],
            self.recv_core.at[dx],
            self.where.peer(1, 0),
        )

    def fold(self, dx):
        self.cross(dx).wait_recv()
        total = self.out[dx].astype(F32) + self.crossed[dx].astype(F32)
        self.out[dx] = total.astype(BF16)

    def finish(self):
        for dx in range(self.where.span):
            self.cross(dx).wait_send()


class PatchSum:
    @staticmethod
    def scratch(span, rows, columns):
        dma = pltpu.SemaphoreType.DMA
        return [pltpu.VMEM((max(1, span - 1), rows, columns), BF16), dma((span,)), dma((span,))]

    def __init__(self, where, terms, out, scratch):
        self.where, self.crossed, self.out = where, terms, out
        self.landed, self.send, self.recv = scratch

    hop = GroupSum.hop

    def run(self, step):
        span = self.where.span
        if step == 0:
            for dx in range(1, span):
                self.hop(dx).start()
        else:
            total = self.crossed[0].astype(F32)
            for dx in range(1, span):
                self.hop(dx).wait_recv()
                total = total + self.landed[dx - 1].astype(F32)
            self.out[...] = total
            for dx in range(1, span):
                self.hop(dx).wait_send()


class AllSum:
    @staticmethod
    def bits(sizes, axes=(2, 0, 1)):
        found = []
        for axis in axes:
            bit = 1
            while bit < sizes[axis]:
                found.append((axis, bit))
                bit *= 2
        return found

    @staticmethod
    def scratch(sizes, shape):
        count = len(AllSum.bits(sizes))
        dma = pltpu.SemaphoreType.DMA
        slots = pltpu.VMEM((count,) + tuple(shape), F32)
        return [slots, slots, dma((count,)), dma((count,))]

    def __init__(self, where, sizes, block, out, scratch, axes=(2, 0, 1)):
        self.block, self.out = block, out
        self.held, self.landed, self.send, self.recv = scratch
        here = (where.ring, where.core, where.patch)
        self.peers = []
        for axis, bit in AllSum.bits(sizes, axes):
            peer = list(here)
            peer[axis] = here[axis] + (1 - 2 * ((here[axis] // bit) % 2)) * bit
            self.peers.append(tuple(peer))
        self.events = len(self.peers) + 1

    def copy(self, step):
        return remote(
            self.held.at[step],
            self.landed.at[step],
            self.send.at[step],
            self.recv.at[step],
            self.peers[step],
        )

    def run(self, step):
        if step == 0:
            total = self.block[...]
        else:
            self.copy(step - 1).wait()
            total = self.held[step - 1] + self.landed[step - 1]
        if step < len(self.peers):
            self.held[step] = total
            self.copy(step).start()
        else:
            self.out[...] = total


HBM = pl.BlockSpec(memory_space=pl.ANY)
CORE = pl.BlockSpec(memory_space=pltpu.VMEM)


def take(refs, counts):
    found, at = [], 0
    for count in counts:
        found.append(list(refs[at : at + count]))
        at += count
    return found


def loads(pairs, sems):
    copies = [
        pltpu.make_async_copy(source, target, sems.at[at])
        for at, (source, target) in enumerate(pairs)
    ]
    for copy in copies:
        copy.start()
    return copies


def flat_block(vector):
    rows = -(-vector.shape[0] // 1024) * 8
    return jnp.pad(vector, (0, rows * 128 - vector.shape[0])).reshape(rows, 128)


def join(pieces, wide, block):
    group, share, _ = pieces.shape
    for at in range(group):
        wide[at * share : (at + 1) * share, :] = pieces[at].astype(F32)
    block[...] = wide[...].astype(BF16)


def entry_kernel(sizes, clips, chunk, *refs):
    where = Where(sizes)
    ins, outs, scratch = take(refs, (8, 9, len(refs) - 17))
    tokens, qkv_far, up_far, out_rows, silu_part, ada_far, small, frame_clip = ins
    tokens_all, w_qkv, out_block, up_block, summed, hidden, found_far, own_rows, bias_up = outs
    held, cols, lands, wide, (qkv_block, w_qkv_t, vector, spread, normal), *sems = take(
        scratch, (6, 2, 3, 3, 5, 3, 3, 3, 3, 3, 4)
    )
    qkv_weight, up_weight, ada_weight, projected, load_sems, store_sems = held
    have_qkv, have_ada, have_up = loads(
        [(qkv_far, qkv_weight), (ada_far, ada_weight), (up_far, up_weight)], load_sems
    )
    sums = AllSum(where, sizes, vector, summed, sems[5])
    member, span, group = where.member, where.span, 2 * where.span
    rows, width = tokens.shape
    share = out_rows.shape[0]
    device = where.ring * group + member

    def swap(source, land, job_sems):
        return GroupSwap(where, source, lambda dc, dx: land.at[member], job_sems)

    swap_qkv = swap(lambda dc, dx: cols[0].at[where.peer_member(dc, dx)], lands[0], sems[0])
    swap_up = swap(lambda dc, dx: cols[1].at[where.peer_member(dc, dx)], lands[1], sems[1])
    swap_out = swap(lambda dc, dx: out_rows, lands[2], sems[2])
    gather = GroupGather(where, tokens, tokens_all, sems[3], max(1, rows // 128))
    ring = RingGather(where, qkv_block, w_qkv, sems[4])

    features = qkv_weight.shape[1] // (3 * group)
    have_qkv.wait()
    wide_rows = qkv_weight[...].astype(F32)
    for at in range(group):
        for part in range(3):
            low = (part * group + at) * features
            cols[0][at, :, part * features : (part + 1) * features] = wide_rows[
                :, low : low + features
            ].astype(BF16)

    units = up_weight.shape[1] // (group * where.size)
    spread[...] = jnp.zeros_like(spread)
    lengths = [share] * 4 + [units, 6 * share]
    low = 0
    for at, length in enumerate(lengths):
        spread[at : at + 1, :length] = small[0:1, low : low + length]
        low += length
    lanes = lax.broadcasted_iota(jnp.int32, (1, width), 1)
    vector[...] = jnp.zeros_like(vector)
    vector[0:4, :] = pltpu.roll(spread[...], device * share, 1)[0:4]
    start = device * units
    moved = pltpu.roll(spread[...], start % width, 1)[4:5]
    for at in range(4):
        vector[4 + at : 5 + at, :] = jnp.where(start // width == at, moved, 0.0)
    start = device * 6 * share
    moved = pltpu.roll(spread[...], start % width, 1)[5:6]
    lies = start // width + jnp.where(lanes < start % width, 1, 0)
    have_ada.wait()
    terms = jnp.dot(silu_part[...], ada_weight[...], preferred_element_type=F32)
    for part in range(6):
        bias = jnp.where(lies == part, moved, 0.0)
        for clip in range(clips):
            at = 8 + 6 * clip + part
            vector[at : at + 1, :] = (
                terms[clip : clip + 1, part * width : (part + 1) * width] + bias
            )
    own_clip = frame_clip[0].astype(F32)
    own_frame = 2 * where.ring + where.core
    at = 8 + 6 * clips
    vector[at : at + 1, :] = jnp.where((lanes == own_frame) & (where.patch == 0), own_clip, 0.0)

    greet(where.ring_peers() + where.group_peers() + sums.peers)
    swap_qkv.run(0)
    sums.run(0)
    swap_qkv.run(1)
    join(lands[0], wide[0], qkv_block)
    ring.run(0)
    ring.run(1)
    gather.run(0)
    have_up.wait()
    wide_rows = up_weight[...].astype(F32)
    for at in range(group):
        for ring_at in range(where.size):
            low = (ring_at * group + at) * units
            cols[1][at, :, ring_at * units : (ring_at + 1) * units] = wide_rows[
                :, low : low + units
            ].astype(BF16)
    swap_up.run(0)
    swap_out.run(0)
    ring.run(2)
    sums.run(1)
    ring.run(3)
    ring.run(4)

    def norm(dc, dx, at, count):
        first = (dc * span + dx) * rows + at
        normal[first : first + count, :], _ = layer_norm(
            tokens_all[dc, dx, at : at + count, :].astype(F32)
        )

    gather.keep().wait()
    near = [(dc, at) for dc in range(2) for at in range(0, rows, chunk)]
    for event in range(5, ring.events):
        ring.run(event)
        if event % 2 == 0 and event // 2 - 1 < sums.events - 1:
            sums.run(event // 2 - 1)
        if near and event > 5:
            dc, at = near.pop(0)
            if dc and not at:
                gather.arrived(0)
            norm(dc, 0, at, chunk)
    sums.run(sums.events - 1)

    at = 8 + 6 * clips
    other_frame = 2 * where.ring + 1 - where.core
    other_clip = jnp.sum(
        jnp.where(lanes == other_frame, summed[at : at + 1, :], 0.0), axis=1, keepdims=True
    )
    own, other = [0.0] * 6, [0.0] * 2
    for clip in range(clips):
        is_own = jnp.maximum(1.0 - jnp.abs(own_clip - clip), 0.0)
        is_other = jnp.maximum(1.0 - jnp.abs(other_clip - clip), 0.0)
        for part in range(6):
            row = summed[8 + 6 * clip + part : 9 + 6 * clip + part, :]
            own[part] = own[part] + is_own * row
            if part < 2:
                other[part] = other[part] + is_other * row
        own_rows[8 + clip : 9 + clip, :] = jnp.zeros((1, width), F32) + is_own
        own_rows[8 + clips + clip : 9 + clips + clip, :] = jnp.zeros((1, width), F32) + is_other
    for part in range(6):
        own_rows[part : part + 1, :] = own[part]
    own_rows[6:8, :] = summed[2:4, :]
    for ring_at in range(where.size):
        start = (ring_at * group + member) * units
        moved = pltpu.roll(summed[0:8, :], (width - start % width) % width, 1)
        picked = jnp.zeros((1, width), F32)
        for at in range(4):
            picked = picked + jnp.where(start // width == at, moved[4 + at : 5 + at], 0.0)
        bias_up[:, ring_at * units : (ring_at + 1) * units] = picked[:, :units]

    features = qkv_block.shape[1] // 3
    lead = pltpu.roll(summed[0:8, :], (width - member * features) % width, 1).T
    bias_q, bias_v = lead[:features, 0:1], lead[:features, 1:2]
    w_qkv_t[...] = w_qkv[...].reshape(width, 3 * features).T

    stored = []

    def project(dc, dx, at):
        shift, scale = (other if dc else own)[:2]
        first = (dc * span + dx) * rows + at
        low = (normal[first : first + chunk, :] * (1.0 + scale) + shift).astype(BF16)
        hidden[first : first + chunk, :] = low
        found = lax.dot_general(
            w_qkv_t[...], low, (((1,), (1,)), ((), ())), preferred_element_type=F32
        )
        there = slice(first, first + chunk)
        projected[:features, there] = (found[:features] + bias_q).astype(BF16)
        projected[features : 2 * features, there] = found[features : 2 * features].astype(BF16)
        projected[2 * features :, there] = (found[2 * features :] + bias_v).astype(BF16)
        stored.extend(
            loads(
                [(projected.at[:, pl.ds(first, chunk)], found_far.at[:, pl.ds(first, chunk)])],
                store_sems.at[pl.ds(len(stored), 1)],
            )
        )

    for dx in range(span):
        if dx == 1:
            swap_up.run(1)
            join(lands[1], wide[1], up_block)
            swap_out.run(1)
            join(lands[2], wide[2], out_block)
            gather.run(1)
        for dc in range(2):
            if dc and dx:
                gather.arrived(dx)
            for at in range(0, rows, chunk):
                if dx:
                    norm(dc, dx, at, chunk)
                project(dc, dx, at)
    for copy in stored:
        copy.wait()
    gather.sent()


def entry(
    tokens, qkv_weight, up_weight, out_rows, silu_part, ada_weight, small, clip, sizes, call_id
):
    size, _, span = sizes
    group, share = 2 * span, out_rows.shape[0]
    rows, width = tokens.shape
    clips = silu_part.shape[0]
    block_rows = group * share
    columns = [qkv_weight.shape[1] // group, up_weight.shape[1] // group, width]
    count = 9 + 6 * clips
    vector = (count + -count % 8, width)
    shape = jax.ShapeDtypeStruct
    scratch = [
        pltpu.VMEM(item.shape, BF16) for item in (qkv_weight, up_weight, ada_weight)
    ]
    scratch += [pltpu.VMEM((columns[0], group * rows), BF16)]
    scratch += [pltpu.SemaphoreType.DMA((3,))]
    scratch += [pltpu.SemaphoreType.DMA((group * rows // min(256, rows),))]
    scratch += [pltpu.VMEM((group, share, n), BF16) for n in columns[:2]]
    scratch += [pltpu.VMEM((group, share, n), BF16) for n in columns]
    scratch += [pltpu.VMEM((block_rows, n), F32) for n in columns]
    scratch += [pltpu.VMEM((block_rows, columns[0]), BF16)]
    scratch += [pltpu.VMEM((columns[0], width), BF16)]
    scratch += [pltpu.VMEM(vector, F32), pltpu.VMEM((8, width), F32)]
    scratch += [pltpu.VMEM((group * rows, width), F32)]
    scratch += GroupSwap.scratch(span) * 3
    scratch += GroupGather.scratch(span, max(1, rows // 128))
    scratch += RingGather.scratch(size)
    scratch += AllSum.scratch(sizes, vector)
    return pl.pallas_call(
        functools.partial(entry_kernel, sizes, clips, min(256, rows)),
        out_shape=[
            shape((2, span, rows, width), BF16),
            shape((size, block_rows, columns[0]), BF16),
            shape((block_rows, width), BF16),
            shape((block_rows, columns[1]), BF16),
            shape(vector, F32),
            shape((group * rows, width), BF16),
            shape((columns[0], group * rows), BF16),
            shape((8 + 2 * clips + -2 * clips % 8, width), F32),
            shape((1, columns[1]), F32),
        ],
        in_specs=[HBM, HBM, HBM, HBM, CORE, HBM, CORE, pl.BlockSpec(memory_space=pltpu.SMEM)],
        out_specs=[CORE] * 6 + [HBM] + [CORE] * 2,
        scratch_shapes=scratch,
        compiler_params=pltpu.CompilerParams(
            collective_id=call_id, has_side_effects=True, vmem_limit_bytes=61 * MIB
        ),
        name="entry",
    )(tokens, qkv_weight, up_weight, out_rows, silu_part, ada_weight, small, clip)


def beside(job, total, places, count, first=0, stride=1):
    at = pl.program_id(0) * pl.num_programs(1) + pl.program_id(1)
    slots, event = {}, 0
    for place in range(first, total * places, stride):
        todo = list(range(event, min(event + count, job.events - 1)))
        if todo:
            slots[place] = todo
            event += len(todo)

    def ahead(place):
        for grid in range(total):
            todo = slots.get(grid * places + place)
            if todo:

                @pl.when(at == grid)
                def _():
                    for event in todo:
                        job.run(event)

    def finish():
        for late in range(event, job.events):
            job.run(late)

    return ahead, finish


def attention_kernel(sizes, factor, chunk, total, *refs):
    where = Where(sizes)
    ins, outs, scratch = take(refs, (5, 4, len(refs) - 9))
    q_ref, k_ref, v_ref, up_block, grad_block = ins
    out_ref, lse_ref, w_up, grad_all = outs
    sems = take(scratch, (3, 3))
    chunks = q_ref.shape[2] // chunk
    places = max(chunks // 2, 1)
    ahead, finish = beside(RingGather(where, up_block, w_up, sems[0]), total, places, 1)
    gather = GroupGather(where, grad_block, grad_all, sems[1], 2)
    at = pl.program_id(0) * pl.num_programs(1) + pl.program_id(1)

    @pl.when(at == 0)
    def _():
        greet(where.ring_peers() + where.group_peers())
        gather.run(0)

    keys = k_ref[0].T
    values_t = v_ref[0]
    for number in range(chunks):
        if number % 2 == 0:
            ahead(number // 2)
        span = slice(number * chunk, (number + 1) * chunk)
        scores = jnp.dot(keys, q_ref[0, :, span], preferred_element_type=F32) * factor
        top = jnp.max(scores, axis=0, keepdims=True)
        probs = jnp.exp2(scores - top)
        row_sum = jnp.sum(probs, axis=0, keepdims=True)
        mixed = jnp.dot(values_t, probs.astype(BF16), preferred_element_type=F32)
        out_ref[0, :, span] = (mixed / row_sum).astype(BF16)
        lse_ref[0, :, span] = top + jnp.log2(row_sum)

    @pl.when(at == total - 1)
    def _():
        gather.run(1)
        finish()
        gather.run(2)


def attention(qkv, up_block, grad_block, patches, sizes, call_id):
    size, _, span = sizes
    triple, dim, tokens = qkv.shape
    heads = triple // 3
    frames = tokens // patches
    block = (1, dim, patches)
    factor = LOG2E / math.sqrt(HEAD_DIM)
    shape = jax.ShapeDtypeStruct
    return pl.pallas_call(
        functools.partial(attention_kernel, sizes, factor, min(256, patches), frames * heads),
        out_shape=[
            shape((heads, dim, tokens), BF16),
            shape((heads, 1, tokens), F32),
            shape((size,) + up_block.shape, BF16),
            shape((2, span) + grad_block.shape, BF16),
        ],
        grid=(frames, heads),
        in_specs=[
            pl.BlockSpec(block, lambda f, h: (h, 0, f)),
            pl.BlockSpec(block, lambda f, h: (heads + h, 0, f)),
            pl.BlockSpec(block, lambda f, h: (2 * heads + h, 0, f)),
            HBM,
            HBM,
        ],
        out_specs=[
            pl.BlockSpec(block, lambda f, h: (h, 0, f)),
            pl.BlockSpec((1, 1, patches), lambda f, h: (h, 0, f)),
            HBM,
            HBM,
        ],
        scratch_shapes=RingGather.scratch(size) + GroupGather.scratch(span, 2),
        compiler_params=pltpu.CompilerParams(
            collective_id=call_id, has_side_effects=True, vmem_limit_bytes=32 * MIB
        ),
        cost_estimate=pl.CostEstimate(
            flops=4 * heads * patches * tokens * 256,
            bytes_accessed=4 * heads * dim * tokens * 2,
            transcendentals=heads * patches * tokens,
        ),
        name="attention",
    )(qkv, qkv, qkv, up_block, grad_block)


def attention_back_kernel(sizes, factor, chunk, total, *refs):
    where = Where(sizes)
    ins, outs, scratch = take(refs, (7, 3, len(refs) - 10))
    q_ref, k_ref, v_ref, g_ref, lse_ref, up_terms, half_terms = ins
    grads_ref, up_sum, half_sum = outs
    dk_sum, dv_sum = scratch[:2]
    own = take(scratch[2:], (4, 3))
    patches = q_ref.shape[2]
    chunks = patches // chunk
    places = max(chunks // 2, 1)
    ahead, finish = beside(RingSum(where, up_terms, up_sum, own[0]), total, places, 1)
    half = PatchSum(where, half_terms, half_sum, own[1])
    at = pl.program_id(0) * pl.num_programs(1) + pl.program_id(1)

    @pl.when(at == 0)
    def _():
        greet(where.ring_peers() + where.group_peers())
        half.run(0)

    keys_t = k_ref[0]
    keys = keys_t.T
    values = v_ref[0].T
    scale = factor / LOG2E
    for number in range(chunks):
        if number % 2 == 0:
            ahead(number // 2)
        span = slice(number * chunk, (number + 1) * chunk)
        queries_t = q_ref[0, :, span]
        grad_t = g_ref[0, :, span]
        scores = jnp.dot(keys, queries_t, preferred_element_type=F32) * factor
        probs = jnp.exp2(scores - lse_ref[0, :, span])
        grad_probs = jnp.dot(values, grad_t, preferred_element_type=F32)
        row_dot = jnp.sum(probs * grad_probs, axis=0, keepdims=True)
        grad_scores = (probs * (grad_probs - row_dot)).astype(BF16)
        probs_low = probs.astype(BF16)
        dq = jnp.dot(keys_t, grad_scores, preferred_element_type=F32)
        grads_ref[0, 0, :, span] = (dq * scale).astype(BF16)
        dims = (((1,), (1,)), ((), ()))
        dk = lax.dot_general(queries_t, grad_scores, dims, preferred_element_type=F32)
        dv = lax.dot_general(grad_t, probs_low, dims, preferred_element_type=F32)
        if number == 0:
            dk_sum[...] = dk
            dv_sum[...] = dv
        else:
            dk_sum[...] += dk
            dv_sum[...] += dv
    grads_ref[1, 0] = (dk_sum[...] * scale).astype(BF16)
    grads_ref[2, 0] = dv_sum[...].astype(BF16)

    @pl.when(at == total - 1)
    def _():
        finish()
        half.run(1)


def attention_back(qkv, grad, lse, up_terms, half_terms, patches, sizes, call_id):
    size, _, span = sizes
    triple, dim, tokens = qkv.shape
    heads = triple // 3
    frames = tokens // patches
    block = (1, dim, patches)
    factor = LOG2E / math.sqrt(HEAD_DIM)
    spec = pl.BlockSpec(block, lambda f, h: (h, 0, f))
    shape = jax.ShapeDtypeStruct
    return pl.pallas_call(
        functools.partial(attention_back_kernel, sizes, factor, min(256, patches), frames * heads),
        out_shape=[
            shape((3, heads, dim, tokens), BF16),
            shape(up_terms.shape[1:], BF16),
            shape(half_terms.shape[1:], F32),
        ],
        grid=(frames, heads),
        in_specs=[
            spec,
            pl.BlockSpec(block, lambda f, h: (heads + h, 0, f)),
            pl.BlockSpec(block, lambda f, h: (2 * heads + h, 0, f)),
            spec,
            pl.BlockSpec((1, 1, patches), lambda f, h: (h, 0, f)),
            CORE,
            CORE,
        ],
        out_specs=[pl.BlockSpec((3,) + block, lambda f, h: (0, h, 0, f)), CORE, CORE],
        scratch_shapes=[pltpu.VMEM((dim, patches), F32)] * 2
        + RingSum.scratch(size, *up_terms.shape[1:])
        + PatchSum.scratch(span, *half_terms.shape[1:]),
        compiler_params=pltpu.CompilerParams(
            collective_id=call_id, has_side_effects=True, vmem_limit_bytes=61 * MIB
        ),
        cost_estimate=pl.CostEstimate(
            flops=10 * heads * patches * tokens * 256,
            bytes_accessed=8 * heads * dim * tokens * 2,
            transcendentals=heads * patches * tokens,
        ),
        name="attention_back",
    )(qkv, qkv, qkv, grad, lse, up_terms, half_terms)


def joined(array):
    group, features, count = array.shape
    if features % 16:
        return array.astype(F32).reshape(group * features, count).astype(BF16)
    return array.reshape(group * features, count)


def middle_kernel(sizes, parts, *refs):
    where = Where(sizes)
    ins, outs, scratch = take(refs, (5, 6, len(refs) - 11))
    heads_t, out_block, tokens_far, vectors, down_block = ins
    attended, branch, midway, hidden_all, w_out, w_down = outs
    (hidden, tokens, load_sems), *sems = take(scratch, (3, 3, 3, 3, 5))
    (have_tokens,) = loads([(tokens_far, tokens)], load_sems)
    greet(where.ring_peers() + where.group_peers())
    rows, width = tokens.shape
    span = where.span

    swap = GroupSwap(
        where,
        lambda dc, dx: heads_t.at[:, pl.ds((dc * span + dx) * rows, rows)],
        lambda dc, dx: attended.at[where.member],
        sems[0],
    )
    ring = RingGather(where, down_block, w_down, sems[1])
    gather = GroupGather(where, hidden, hidden_all, sems[2], parts)
    ring_out = RingGatherSplit(where, out_block, w_out, sems[3])
    swap.run(0)
    ring_out.run(0)
    for event in range(ring_out.events - 2):
        ring.run(event)
        ring_out.run(event + 1)
    event += 1
    swap.run(1)
    ring_out.run(ring_out.events - 1)
    size = rows // parts
    full = w_out[...].reshape(width, width)
    have_tokens.wait()
    for part in range(parts):
        span_rows = slice(part * size, (part + 1) * size)
        mixed = joined(attended[:, :, span_rows])
        one = lax.dot_general(mixed, full, (((0,), (0,)), ((), ())), preferred_element_type=F32)
        one = one + vectors[6:7, :]
        branch[span_rows, :] = one
        mid = tokens[span_rows, :].astype(F32) + vectors[2:3, :] * one
        midway[span_rows, :] = mid
        normed, _ = layer_norm(mid)
        hidden[span_rows, :] = (normed * (1.0 + vectors[4:5, :]) + vectors[3:4, :]).astype(BF16)
        gather.start(part)
        if event < ring.events:
            ring.run(event)
            event += 1
    gather.keep().start()
    for event in range(event, ring.events):
        ring.run(event)
    for part in range(parts):
        gather.pass_on(part)
    gather.finish()
    gather.keep().wait()


def middle(heads_t, out_block, tokens, vectors, down_block, sizes, call_id):
    size, _, span = sizes
    rows, width = tokens.shape
    parts = rows // 128
    shape = jax.ShapeDtypeStruct
    return pl.pallas_call(
        functools.partial(middle_kernel, sizes, parts),
        out_shape=[
            shape((2 * span, heads_t.shape[0], rows), BF16),
            shape((rows, width), F32),
            shape((rows, width), F32),
            shape((2, span, rows, width), BF16),
            shape((size,) + out_block.shape, BF16),
            shape((size,) + down_block.shape, BF16),
        ],
        in_specs=[HBM, HBM, HBM, CORE, HBM],
        out_specs=[CORE] * 6,
        scratch_shapes=[pltpu.VMEM((rows, width), BF16)] * 2
        + [pltpu.SemaphoreType.DMA((1,))]
        + GroupSwap.scratch(span)
        + RingGather.scratch(size)
        + GroupGather.scratch(span, parts)
        + RingGatherSplit.scratch(size),
        compiler_params=pltpu.CompilerParams(
            collective_id=call_id, has_side_effects=True, vmem_limit_bytes=61 * MIB
        ),
        name="middle",
    )(heads_t, out_block, tokens, vectors, down_block)


def gelu_both(values_in):
    square = values_in * values_in
    inner = 0.7978845608028654 * values_in * (1.0 + 0.044715 * square)
    bent = jnp.tanh(inner)
    outer = 0.5 * (1.0 + bent)
    slope = 0.7978845608028654 * (1.0 + 3.0 * 0.044715 * square)
    return values_in * outer, outer + 0.5 * values_in * (1.0 - bent * bent) * slope


def feed_kernel(sizes, chunk, tile, *refs):
    where = Where(sizes)
    ins, outs, scratch = take(refs, (5, 5, len(refs) - 10))
    *far_away, bias = ins
    half, grad_hidden, g_up, down_sum, g_bias = outs
    here_now, (act, grad_pre, branch, back, g_down), *own = take(scratch, (5, 5, 3, 6, 4))
    hidden, w_up, grad, w_down, load_sems = here_now
    order = (0, 2, 1, 3)
    have = loads(
        [(far_away[at], target) for at, target in zip(order, here_now)], load_sems
    )
    span = where.span
    rows, width = grad_hidden.shape
    units = bias.shape[1]
    sum_half = CoreSum(where, branch, half, own[0])
    sum_back = GroupSum(where, back, grad_hidden, own[1])
    ring = RingSum(where, g_down, down_sum, own[2])
    greet(where.ring_peers() + where.group_peers())
    each = rows // chunk
    steps = 2 * span * each
    across = (((1,), (1,)), ((), ()))
    over = (((0,), (0,)), ((), ()))

    def forward(step, total):
        here = pl.ds(pl.multiple_of(step * chunk, chunk), chunk)
        pre = jnp.dot(hidden[here, :], w_up[...], preferred_element_type=F32) + bias[...]
        value, slope = gelu_both(pre)
        act[here, :] = value.astype(BF16)
        grad_act = lax.dot_general(grad[here, :], w_down[...], across, preferred_element_type=F32)
        low = (grad_act * slope).astype(BF16)
        grad_pre[here, :] = low
        return total + jnp.sum(low.astype(F32), axis=0, keepdims=True)

    for copy in have:
        copy.wait()
    g_bias[...] = lax.fori_loop(0, steps, forward, jnp.zeros((1, units), F32))
    for low in range(0, units, tile):
        cut = slice(low, low + tile)
        found = lax.dot_general(act[:, cut], grad[...], over, preferred_element_type=F32)
        if len(g_down.shape) == 2:
            g_down[cut, :] = found.astype(BF16)
        else:
            size = g_down.shape[1]
            for at in range(tile // size):
                g_down[low // size + at] = found[at * size : (at + 1) * size].astype(BF16)
    ring.run(0)
    ring.run(1)

    def beside_ring(step, first, every, count):
        for at in range(count):
            if first + at < ring.events:
                pl.when(step == (at + 1) * every - 1)(functools.partial(ring.run, first + at))

    def backward(step, carry):
        at = step // each
        dx, dc = span - 1 - at // 2, 1 - at % 2
        inside = pl.ds(pl.multiple_of(step % each * chunk, chunk), chunk)
        first = pl.multiple_of((dc * span + dx) * rows + step % each * chunk, chunk)
        here = pl.ds(first, chunk)
        back[dc, dx, inside, :] = lax.dot_general(
            grad_pre[here, :], w_up[...], across, preferred_element_type=F32
        ).astype(BF16)
        for place in range(2 * span):
            done_dx, done_dc = span - 1 - place // 2, 1 - place % 2

            @pl.when(step == (place + 1) * each - 1)
            def _():
                if done_dc:
                    sum_back.cross(done_dx).start()
                elif done_dx:
                    sum_back.fold(done_dx)

        beside_ring(step, 2, 2, steps // 2)
        return carry

    lax.fori_loop(0, steps, backward, 0)
    event = min(2 + steps // 2, ring.events)

    def give(target, dc, first_event):
        def body(step, carry):
            dx = step // each
            inside = pl.ds(pl.multiple_of(step % each * chunk, chunk), chunk)
            first = pl.multiple_of(dc * span * rows + step * chunk, chunk)
            target[dx, inside, :] = jnp.dot(
                act[pl.ds(first, chunk), :], w_down[...], preferred_element_type=F32
            ).astype(BF16)
            beside_ring(step, first_event, 2, steps // 4)
            return carry

        lax.fori_loop(0, steps // 2, body, 0)
        return min(first_event + steps // 4, ring.events)

    event = give(branch, 1, event)
    for dx in range(span):
        sum_half.cross(dx).start()
    event = give(half, 0, event)
    for low in range(0, width, tile):
        if event < ring.events:
            ring.run(event)
            event += 1
        cut = slice(low, low + tile)
        g_up[cut, :] = lax.dot_general(
            hidden[:, cut], grad_pre[...], over, preferred_element_type=F32
        ).astype(BF16)
    for dx in range(span):
        sum_half.fold(dx)
    for event in range(event, ring.events):
        ring.run(event)
    sum_half.finish()
    sum_back.finish()


def feed(hidden, grad, w_up, w_down, bias, sizes, call_id):
    size, _, span = sizes
    tokens, width = hidden.shape
    units = w_up.shape[1]
    rows = tokens // (2 * span)
    block = (units // size, width)
    shape = jax.ShapeDtypeStruct
    return pl.pallas_call(
        functools.partial(feed_kernel, sizes, min(256, rows), 384 if units % 384 == 0 else units),
        out_shape=[
            shape((span, rows, width), BF16),
            shape((rows, width), F32),
            shape((width, units), BF16),
            shape(block, F32),
            shape((1, units), F32),
        ],
        in_specs=[HBM] * 4 + [CORE],
        out_specs=[CORE] * 5,
        scratch_shapes=[pltpu.VMEM(item.shape, BF16) for item in (hidden, w_up, grad, w_down)]
        + [pltpu.SemaphoreType.DMA((4,))]
        + [pltpu.VMEM((tokens, units), BF16)] * 2
        + [pltpu.VMEM((span, rows, width), BF16), pltpu.VMEM((2, span, rows, width), BF16)]
        + [pltpu.VMEM((size,) + block if block[0] % 16 else (units, width), BF16)]
        + CoreSum.scratch(span, rows, width)
        + GroupSum.scratch(span, rows, width)
        + RingSum.scratch(size, *block),
        compiler_params=pltpu.CompilerParams(
            collective_id=call_id, has_side_effects=True, vmem_limit_bytes=61 * MIB
        ),
        name="feed",
    )(hidden, grad, w_up, w_down, bias)


def return_kernel(sizes, parts, tile, *refs):
    where = Where(sizes)
    ins, outs, scratch = take(refs, (7, 4, len(refs) - 11))
    grad_hidden, midway, branch, grad_out, w_out, attended, vectors = ins
    grad_mid, grad_mix, g_out, sums = outs
    (grad_heads, grad_one), own = take(scratch, (2, 3 * parts))
    greet(where.group_peers())
    rows, width = midway.shape
    span = where.span
    size = rows // parts
    features = grad_heads.shape[1]
    swaps = []
    for part in range(parts):
        cut = pl.ds(part * size, size)

        def source(dc, dx, cut=cut):
            return grad_heads.at[where.peer_member(dc, dx), :, cut]

        def target(dc, dx, part=part):
            block = dc * span + (span - dx) % span
            return grad_mix.at[:, pl.ds(block * rows + part * size, size)]

        swaps.append(GroupSwap(where, source, target, own[3 * part : 3 * part + 3]))
    full = w_out[...]
    totals = [jnp.zeros((1, width), F32)] * 4
    for part in range(parts):
        here = slice(part * size, (part + 1) * size)
        normed, inv_std = layer_norm(midway[here, :])
        grad = grad_hidden[here, :]
        mid = grad_out[here, :].astype(F32) + norm_back(
            grad * (1.0 + vectors[4:5, :]), normed, inv_std
        )
        grad_mid[here, :] = mid
        low = (vectors[2:3, :] * mid).astype(BF16)
        grad_one[here, :] = low
        heads_t = lax.dot_general(full, low, (((1,), (1,)), ((), ())), preferred_element_type=F32)
        grad_heads[:, :, here] = heads_t.reshape(2 * span, features, size).astype(BF16)
        swaps[part].run(0)
        found = [grad, grad * normed, mid * branch[here, :], low.astype(F32)]
        totals = [
            total + jnp.sum(item, axis=0, keepdims=True) for total, item in zip(totals, found)
        ]
    for at, total in enumerate(totals):
        sums[at : at + 1, :] = total
    sums[4:8, :] = jnp.zeros((4, width), F32)
    for low in range(0, width, tile):
        cut = slice(low, low + tile)
        g_out[cut, :] = jnp.dot(
            attended[cut, :], grad_one[...], preferred_element_type=F32
        ).astype(BF16)
    for swap in swaps:
        swap.run(1)


def back_to_heads(
    grad_hidden, midway, branch, grad_out, w_out, attended, vectors, sizes, call_id
):
    span = sizes[2]
    rows, width = midway.shape
    group = 2 * span
    parts = rows // 128
    features = width // group
    shape = jax.ShapeDtypeStruct
    return pl.pallas_call(
        functools.partial(return_kernel, sizes, parts, 384),
        out_shape=[
            shape((rows, width), F32),
            shape((features, group * rows), BF16),
            shape((width, width), BF16),
            shape((8, width), F32),
        ],
        in_specs=[CORE] * 7,
        out_specs=[CORE] * 4,
        scratch_shapes=[
            pltpu.VMEM((group, features, rows), BF16),
            pltpu.VMEM((rows, width), BF16),
        ]
        + GroupSwap.scratch(span) * parts,
        compiler_params=pltpu.CompilerParams(
            collective_id=call_id, has_side_effects=True, vmem_limit_bytes=61 * MIB
        ),
        name="back_to_heads",
    )(grad_hidden, midway, branch, grad_out, w_out, attended, vectors)


def last_kernel(sizes, chunk, tile, clips, *refs):
    where = Where(sizes)
    ins, outs, scratch = take(refs, (11, 6, len(refs) - 17))
    grad_qkv, hidden, tokens, w_qkv, grad_mid, out_terms, early, own_rows = ins[:8]
    midway, branch, grad_out = ins[8:]
    tokens_grad, output, qkv_sum, out_sum, early_sum, late_sum = outs
    (back, g_qkv, late, grad_hidden, spread), *own = take(scratch, (5, 6, 4, 4, 4, 7))
    span = where.span
    rows, width = grad_mid.shape
    sum_back = GroupSum(where, back, grad_hidden, own[0])
    ring = RingSum(where, g_qkv, qkv_sum, own[1])
    first_sums = AllSum(where, sizes, early, early_sum, own[2])
    sums = AllSum(where, sizes, late, late_sum, own[3], (0, 1, 2))
    ring_out = RingSumSplit(where, out_terms, out_sum, own[4])
    greet(where.ring_peers() + where.group_peers() + sums.peers)
    ring_out.run(0)
    first_sums.run(0)
    each = rows // chunk
    blocks = 2 * span
    far = 2 * (span - 1) * each
    planned = {far + at: [(ring, 2 + at)] for at in range(2 * each)}
    planned[far + 1].append((first_sums, 3))
    planned[far + 2 * each - 1] += [(ring_out, 3), (first_sums, 4)] if each > 1 else []

    def body(step, totals):
        at = step // each
        dx, dc = span - 1 - at // 2, 1 - at % 2
        inside = pl.ds(pl.multiple_of(step % each * chunk, chunk), chunk)
        first = pl.multiple_of((dc * span + dx) * rows + step % each * chunk, chunk)
        here = pl.ds(first, chunk)
        term = lax.dot_general(
            grad_qkv[:, here], w_qkv[...], (((0,), (1,)), ((), ())), preferred_element_type=F32
        )
        back[dc, dx, inside, :] = term.astype(BF16)
        normed, _ = layer_norm(tokens[here, :].astype(F32))
        shift = jnp.sum(term, axis=0, keepdims=True)
        scale = jnp.sum(term * normed, axis=0, keepdims=True)
        other = dc.astype(F32)
        for place in range(blocks):
            done_dx, done_dc = span - 1 - place // 2, 1 - place % 2

            @pl.when(step == (place + 1) * each - 1)
            def _():
                if done_dc:
                    sum_back.cross(done_dx).start()
                elif done_dx:
                    sum_back.fold(done_dx)

        for when, todo in planned.items():

            @pl.when(step == when)
            def _():
                for job, event in todo:
                    job.run(event)

        own_part, other_part = 1.0 - other, other
        return (
            totals[0] + own_part * shift,
            totals[1] + own_part * scale,
            totals[2] + other_part * shift,
            totals[3] + other_part * scale,
        )

    zero = jnp.zeros((1, width), F32)
    totals = lax.fori_loop(0, far, body, (zero,) * 4)
    first_sums.run(1)
    ring_out.run(1)
    for low in range(0, width, tile):
        cut = slice(low, low + tile)
        g_qkv[cut, :] = lax.dot_general(
            hidden[:, cut], grad_qkv[...], (((0,), (1,)), ((), ())), preferred_element_type=F32
        ).astype(BF16)
    ring.run(0)
    ring.run(1)
    first_sums.run(2)
    ring_out.run(2)
    totals = lax.fori_loop(far, blocks * each, body, totals)
    late[...] = jnp.zeros_like(late)
    for clip in range(clips):
        for part in range(2):
            at = 2 * clip + part
            late[at : at + 1, :] = (
                own_rows[8 + clip : 9 + clip, :] * totals[part]
                + own_rows[8 + clips + clip : 9 + clips + clip, :] * totals[2 + part]
            )
    gate = jnp.zeros((1, width), F32)
    part = min(128, rows)
    for low in range(0, rows, part):
        here = slice(low, low + part)
        two = branch[here, :] + own_rows[7:8, :]
        output[here, :] = (midway[here, :] + own_rows[5:6, :] * two).astype(BF16)
        gate = gate + jnp.sum(grad_out[here, :].astype(F32) * two, axis=0, keepdims=True)
    for clip in range(clips):
        late[2 * clips + clip : 2 * clips + clip + 1, :] = own_rows[8 + clip : 9 + clip, :] * gate
    features = grad_qkv.shape[0] // 3
    ones = jnp.ones((8, grad_qkv.shape[1]), BF16)
    head_sums = lax.dot_general(
        ones, grad_qkv[...], (((1,), (1,)), ((), ())), preferred_element_type=F32
    )
    spread[...] = jnp.zeros_like(spread)
    spread[0:1, :features] = head_sums[0:1, :features]
    spread[1:2, :features] = head_sums[0:1, 2 * features :]
    late[3 * clips : 3 * clips + 2, :] = pltpu.roll(
        spread[...], where.member * features, 1
    )[0:2]
    sums.run(0)

    def own_tokens():
        sum_back.finish()
        part = min(128, rows)
        for low in range(0, rows, part):
            here = slice(low, low + part)
            normed, inv_std = layer_norm(tokens[here, :].astype(F32))
            grad = grad_hidden[here, :] * (1.0 + own_rows[1:2, :])
            tokens_grad[here, :] = (
                grad_mid[here, :] + norm_back(grad, normed, inv_std)
            ).astype(BF16)

    ran = [item for todo in planned.values() for item in todo]
    todo = [(ring_out, at) for at in range(3, ring_out.events)]
    todo += [(first_sums, at) for at in range(3, first_sums.events)]
    todo = [item for item in todo if item not in ran]
    late_todo = list(range(1, sums.events - 1))
    for event in range(2 + len(planned), ring.events):
        ring.run(event)
        if todo:
            job, at = todo.pop(0)
            job.run(at)
        if event % 2 and late_todo:
            sums.run(late_todo.pop(0))
        if event == ring.events - 3:
            own_tokens()
    for job, at in todo:
        job.run(at)
    for at in late_todo:
        sums.run(at)
    sums.run(sums.events - 1)


def back_to_tokens(
    grad_qkv,
    hidden,
    tokens,
    w_qkv,
    grad_mid,
    out_terms,
    early,
    own_rows,
    midway,
    branch,
    grad_out,
    clips,
    sizes,
    call_id,
):
    size, _, span = sizes
    count, width = tokens.shape
    rows = count // (2 * span)
    features = grad_qkv.shape[0]
    block_rows = width // size
    late = (3 * clips + 2 + (-3 * clips - 2) % 8, width)
    shape = jax.ShapeDtypeStruct
    return pl.pallas_call(
        functools.partial(last_kernel, sizes, min(256, rows), 384, clips),
        out_shape=[
            shape((rows, width), BF16),
            shape((rows, width), BF16),
            shape((block_rows, features), BF16),
            shape((block_rows, width), BF16),
            shape(early.shape, F32),
            shape(late, F32),
        ],
        in_specs=[CORE] * 11,
        out_specs=[CORE] * 6,
        scratch_shapes=[
            pltpu.VMEM((2, span, rows, width), BF16),
            pltpu.VMEM((width, features), BF16),
            pltpu.VMEM(late, F32),
            pltpu.VMEM((rows, width), F32),
            pltpu.VMEM((8, width), F32),
        ]
        + GroupSum.scratch(span, rows, width)
        + RingSum.scratch(size, block_rows, features)
        + AllSum.scratch(sizes, early.shape)
        + AllSum.scratch(sizes, late)
        + RingSumSplit.scratch(size, block_rows, width),
        compiler_params=pltpu.CompilerParams(
            collective_id=call_id, has_side_effects=True, vmem_limit_bytes=61 * MIB
        ),
        name="back_to_tokens",
    )(
        grad_qkv,
        hidden,
        tokens,
        w_qkv,
        grad_mid,
        out_terms,
        early,
        own_rows,
        midway,
        branch,
        grad_out,
    )


def final_kernel(sizes, *refs):
    where = Where(sizes)
    ins, outs, scratch = take(refs, (4, 4, len(refs) - 8))
    summed, share_qkv, share_up, share_out = outs
    got, own = scratch[:3], take(scratch[3:], (4, 3, 3, 3))
    sums = AllSum(where, sizes, ins[0], summed, own[0])
    greet(where.group_peers() + sums.peers)
    swaps = [
        GroupSwap(
            where,
            lambda dc, dx, source=ins[at + 1]: source.at[where.peer_member(dc, dx)],
            lambda dc, dx, target=got[at]: target.at[where.member],
            own[at + 1],
        )
        for at in range(3)
    ]
    sums.run(0)
    for swap in swaps:
        swap.run(0)
    for event in range(1, sums.events):
        sums.run(event)
    group, _, three = got[0].shape
    features = three // 3
    swaps[0].run(1)
    for member in range(group):
        piece = got[0][member].astype(F32)
        for part in range(3):
            low = (part * group + member) * features
            share_qkv[:, low : low + features] = piece[:, part * features : (part + 1) * features]
    swaps[1].run(1)
    units = got[1].shape[2] // where.size
    for member in range(group):
        piece = got[1][member].astype(F32)
        for ring in range(where.size):
            low = (ring * group + member) * units
            share_up[:, low : low + units] = piece[:, ring * units : (ring + 1) * units]
    swaps[2].run(1)
    total = got[2][0].astype(F32)
    for member in range(1, group):
        total = total + got[2][member].astype(F32)
    share_out[...] = total


def final(block, pieces, sizes, call_id):
    group, share, _ = pieces[0].shape
    shape = jax.ShapeDtypeStruct
    return pl.pallas_call(
        functools.partial(final_kernel, sizes),
        out_shape=[
            shape(block.shape, F32),
            shape((share, group * pieces[0].shape[2]), F32),
            shape((share, group * pieces[1].shape[2]), F32),
            shape((share, pieces[2].shape[2]), F32),
        ],
        in_specs=[CORE] * 4,
        out_specs=[CORE] * 4,
        scratch_shapes=[pltpu.VMEM(item.shape, BF16) for item in pieces]
        + AllSum.scratch(sizes, block.shape)
        + GroupSwap.scratch(sizes[2]) * 3,
        compiler_params=pltpu.CompilerParams(
            collective_id=call_id, has_side_effects=True, vmem_limit_bytes=32 * MIB
        ),
        name="final",
    )(block, *pieces)


def per_device(
    tokens,
    cotangent,
    clip_embed,
    timesteps,
    frame_clip,
    ada_weight,
    ada_bias,
    qkv_weight,
    query_bias,
    value_bias,
    out_weight,
    out_bias,
    up_weight,
    up_bias,
    down_weight,
    down_bias,
):
    ring_size, patch_size = lax.axis_size("ring"), lax.axis_size("patch")
    sizes = (ring_size, 2, patch_size)
    group = 2 * patch_size
    device_count = ring_size * group
    ring, core, patch = (lax.axis_index(name) for name in ("ring", "core", "patch"))
    member = core * patch_size + patch
    device = ring * group + member
    rows, width = tokens.shape[1:]
    tokens, cotangent = tokens[0], cotangent[0]
    patches = patch_size * rows
    clips = clip_embed.shape[0]
    hidden = up_weight.shape[1]
    share = width // device_count
    heads = HEADS // group
    head_width = heads * HEAD_DIM
    units = hidden // group
    mine = jnp.arange(group) == member
    mine_of_all = jnp.arange(device_count) == device

    condition = clip_embed + sinusoid(timesteps, width)
    silu_cond, silu_back = jax.vjp(jax.nn.silu, condition)
    silu_low = silu_cond.astype(BF16)
    silu_part = lax.dynamic_slice_in_dim(silu_low, device * share, share, 1)
    small = jnp.concatenate(
        [query_bias, value_bias, out_bias, down_bias, up_bias, ada_bias]
    ).astype(F32)[None, :]

    tokens_all, w_qkv, out_block, up_block, _, hidden_one, projected, own_rows, b_up = entry(
        tokens,
        qkv_weight,
        up_weight,
        out_weight,
        silu_part,
        ada_weight,
        small,
        frame_clip,
        sizes,
        1,
    )
    w_qkv = w_qkv.reshape(width, 3 * head_width)
    gate_two = own_rows[5]
    qkv = projected.reshape(3 * heads, HEAD_DIM, 2 * patches)
    grad_out = cotangent.astype(F32)
    grad_branch_two = (gate_two * grad_out).astype(BF16)
    attended_t, lse, w_up, gb_two_all = attention(
        qkv, up_block, grad_branch_two, patches, sizes, 2
    )
    w_up = w_up.reshape(width, units)

    attended, branch_one, midway, hidden_two_all, w_out, w_down = middle(
        attended_t.reshape(head_width, 2 * patches),
        out_block,
        tokens,
        own_rows,
        down_weight,
        sizes,
        3,
    )
    attended = attended.reshape(width, rows)
    w_out = w_out.reshape(width, width)
    w_down = w_down.reshape(units, width)

    branch_half, grad_hidden_two, g_up, share_down, g_up_b = feed(
        hidden_two_all.reshape(2 * patches, width),
        gb_two_all.reshape(2 * patches, width),
        w_up,
        w_down,
        b_up,
        sizes,
        4,
    )
    g_up_b = g_up_b[0]
    g_down_b = jnp.sum(grad_branch_two.astype(F32), axis=0)
    block_rows = width // ring_size
    grad_midway, grad_mix, g_out, own_sums = back_to_heads(
        grad_hidden_two,
        midway,
        branch_one,
        cotangent,
        w_out,
        attended,
        own_rows,
        sizes,
        5,
    )
    grad_shift_two, grad_scale_two, grad_gate_one, g_out_b = (own_sums[at] for at in range(4))

    grad_projected, sum_up, branch_two = attention_back(
        qkv,
        grad_mix.reshape(heads, HEAD_DIM, 2 * patches),
        lse,
        g_up.reshape(ring_size, block_rows, units),
        branch_half,
        patches,
        sizes,
        6,
    )
    grad_projected = grad_projected.reshape(3 * head_width, 2 * patches)

    frame_grads = jnp.stack([grad_gate_one, grad_shift_two, grad_scale_two])
    early = jnp.concatenate(
        [
            (own_rows[8 : 8 + clips, None] * frame_grads[None]).reshape(3 * clips, width),
            jnp.stack([g_out_b, g_down_b]),
            jnp.where(mine[None, :, None], g_up_b.reshape(ring_size, 1, -1), 0.0).reshape(
                -1, width
            ),
        ]
    )
    early = jnp.pad(early, ((0, -early.shape[0] % 8), (0, 0)))
    tokens_grad, output, sum_qkv, sum_out, early_sum, late_sum = back_to_tokens(
        grad_projected,
        hidden_one,
        tokens_all.reshape(2 * patches, width),
        w_qkv,
        grad_midway,
        g_out.reshape(ring_size, block_rows, width),
        early,
        own_rows,
        midway,
        branch_two,
        cotangent,
        clips,
        sizes,
        7,
    )
    first = late_sum[: 2 * clips].reshape(clips, 2 * width)
    second = early_sum[: 3 * clips].reshape(clips, 3 * width)
    third = late_sum[2 * clips : 3 * clips]
    mod_low = jnp.concatenate([first, second, third], axis=1).astype(BF16)
    query_b_all, value_b_all = (late_sum[3 * clips + at] for at in range(2))
    out_b_all, down_b_all = (early_sum[3 * clips + at] for at in range(2))
    up_b_all = early_sum[3 * clips + 2 :].reshape(-1)[:hidden]

    def own(vector):
        length = vector.shape[0] // device_count
        return lax.dynamic_slice_in_dim(vector, device * length, length, 0)

    ada_bias_grad = own(jnp.sum(mod_low.astype(F32), axis=0))
    ada_weight_grad = lax.dot_general(
        silu_part, mod_low, (((0,), (0,)), ((), ())), preferred_element_type=F32
    )
    grad_silu_part = lax.dot_general(
        mod_low, ada_weight, (((1,), (1,)), ((), ())), preferred_element_type=F32
    )
    spread = jnp.where(mine_of_all[None, :, None], grad_silu_part[:, None, :], 0.0).reshape(-1)
    grad_silu, share_qkv, share_up, share_out = final(
        flat_block(spread),
        [item.reshape(group, share, -1) for item in (sum_qkv, sum_up, sum_out)],
        sizes,
        8,
    )
    grad_silu = grad_silu.reshape(-1)[: clips * width].reshape(clips, width)
    clip_grad = silu_back(grad_silu)[0]

    return (
        output[None],
        tokens_grad[None],
        clip_grad,
        ada_weight_grad,
        ada_bias_grad,
        share_qkv,
        own(query_b_all),
        own(value_b_all),
        share_out,
        own(out_b_all),
        share_up,
        own(up_b_all),
        share_down,
        own(down_b_all),
    )


def solution(mesh):
    frames, patch = mesh.shape["frames"], mesh.shape["patch"]
    inner = Mesh(mesh.devices.reshape(frames // 2, 2, patch), ("ring", "core", "patch"))
    every = ("ring", "core", "patch")
    tokens = P(("ring", "core"), "patch", None)
    matrix = P(every, None)
    vector = P(every)
    return jax.shard_map(
        per_device,
        mesh=inner,
        in_specs=(
            tokens,
            tokens,
            P(),
            P(),
            P(("ring", "core")),
            matrix,
            vector,
            matrix,
            vector,
            vector,
            matrix,
            vector,
            matrix,
            vector,
            matrix,
            vector,
        ),
        out_specs=(
            tokens,
            tokens,
            P(),
            matrix,
            vector,
            matrix,
            vector,
            vector,
            matrix,
            vector,
            matrix,
            vector,
            matrix,
            vector,
        ),
        check_vma=False,
    )
```

```python
import functools
import math

import jax
import jax.numpy as jnp
from jax import lax
from jax.experimental import pallas as pl
from jax.experimental.pallas import tpu as pltpu
from jax.sharding import Mesh
from jax.sharding import PartitionSpec as P

HEADS = 16
HEAD_DIM = 72
BF16 = jnp.bfloat16
F32 = jnp.float32
LOG2E = 1.4426950408889634
MESH_ID = pl.DeviceIdType.MESH
MIB = 2**20


def layer_norm(values_in):
    centre = values_in - jnp.mean(values_in, axis=-1, keepdims=True)
    spread = jnp.mean(centre * centre, axis=-1, keepdims=True)
    inv_std = lax.rsqrt(spread + 1e-06)
    return (centre * inv_std, inv_std)


def norm_back(grad_normed, normed, inv_std):
    mean_grad = jnp.mean(grad_normed, axis=-1, keepdims=True)
    mean_prod = jnp.mean(grad_normed * normed, axis=-1, keepdims=True)
    return (grad_normed - mean_grad - normed * mean_prod) * inv_std


def gelu_tanh(values_in):
    inner = 0.7978845608028654 * (values_in + 0.044715 * values_in * values_in * values_in)
    return 0.5 * values_in * (1.0 + jnp.tanh(inner))


def sinusoid(steps_in, width_in):
    half_width = width_in // 2
    freqs = jnp.exp(-math.log(10000.0) * jnp.arange(half_width, dtype=jnp.float32) / half_width)
    angles = steps_in.astype(jnp.float32)[:, None] * freqs[None, :]
    return jnp.concatenate([jnp.cos(angles), jnp.sin(angles)], axis=1)


class Where:
    def __init__(self, sizes):
        self.size, _, self.span = sizes
        self.ring, self.core, self.patch = (
            lax.axis_index(name) for name in ("ring", "core", "patch")
        )
        along, across = self.ring // 2, self.ring % 2
        self.place = (1 - across) * along + across * (self.size - 1 - along)
        self.member = self.core * self.span + self.patch

    def at_place(self, place):
        place = (place + 2 * self.size) % self.size
        back = place // (self.size // 2)
        return (1 - back) * 2 * place + back * (2 * (self.size - 1 - place) + 1)

    def neighbour(self, step):
        return (self.at_place(self.place + step), self.core, self.patch)

    def peer(self, dc, dx):
        core = 1 - self.core if dc else self.core
        return (self.ring, core, (self.patch + dx) % self.span)

    def peer_member(self, dc, dx):
        _, core, patch = self.peer(dc, dx)
        return core * self.span + patch

    def ring_peers(self):
        return [self.neighbour(1), self.neighbour(-1)]

    def group_peers(self):
        return [
            self.peer(dc, dx) for dc in range(2) for dx in range(self.span) if dc or dx
        ]


def greet(peers):
    barrier = pltpu.get_barrier_semaphore()
    for peer in peers:
        pl.semaphore_signal(barrier, inc=1, device_id=peer, device_id_type=MESH_ID)
    pl.semaphore_wait(barrier, len(peers))


def remote(source, target, send_sem, recv_sem, peer):
    return pltpu.make_async_remote_copy(
        src_ref=source,
        dst_ref=target,
        send_sem=send_sem,
        recv_sem=recv_sem,
        device_id=peer,
        device_id_type=MESH_ID,
    )


def strands(rows, columns):
    by_rows = rows % 16 == 0
    tile = 16 if by_rows else 128
    tiles = (rows if by_rows else columns) // tile
    sizes = [tiles // 4 + (at < tiles % 4) for at in range(4)]
    found, low = [], 0
    for at, count in enumerate(sizes):
        cut = pl.ds(low * tile, count * tile)
        found.append((at // 2, (cut, slice(None)) if by_rows else (slice(None), cut)))
        low += count
    return found


class RingGather:
    @staticmethod
    def scratch(size):
        dma = pltpu.SemaphoreType.DMA
        return [dma((4, size - 1)), dma((4, size - 1)), dma((1,))]

    def __init__(self, where, block, out, sems):
        self.where, self.block, self.out = where, block, out
        self.send, self.recv, self.own = sems
        self.parts = strands(*block.shape)
        self.events = 2 * (where.size - 1) + 1

    def keep(self):
        return pltpu.make_async_copy(self.block, self.out.at[self.where.ring], self.own.at[0])

    def copy(self, at, step):
        where = self.where
        way, part = self.parts[at]
        sign = (-1, 1)[way]
        slot = where.at_place(where.place + sign * step)
        target = self.out.at[(slot,) + part]
        source = target if step else self.block.at[part]
        return remote(
            source, target, self.send.at[at, step], self.recv.at[at, step], where.neighbour(-sign)
        )

    def run(self, event):
        step, piece = event // 2, event % 2
        if event == 0:
            self.keep().start()
        if event < self.events - 1:
            for at in (piece, piece + 2):
                if step:
                    self.copy(at, step - 1).wait_recv()
                self.copy(at, step).start()
        else:
            for at in range(4):
                self.copy(at, step - 1).wait_recv()
                for past in range(step):
                    self.copy(at, past).wait_send()
            self.keep().wait()


class RingGatherSplit:
    @staticmethod
    def scratch(size):
        dma, half = pltpu.SemaphoreType.DMA, size // 2
        return [dma((2, half))] * 4 + [dma((1,))]

    def __init__(self, where, block, out, sems):
        self.where, self.block, self.out = where, block, out
        self.send, self.recv, self.send_core, self.recv_core, self.own = sems
        self.half = where.size // 2
        self.events = self.half + 2
        cut = -(-block.shape[0] // 32) * 16
        self.parts = (pl.ds(0, cut), pl.ds(cut, block.shape[0] - cut))

    def keep(self):
        return pltpu.make_async_copy(self.block, self.out.at[self.where.ring], self.own.at[0])

    def slot(self, step, at):
        where = self.where
        place = where.at_place(where.place + (2 * where.core - 1) * step)
        return self.out.at[place, self.parts[at]]

    def copy(self, step, at):
        where = self.where
        target = self.slot(step, at)
        source = target if step else self.block.at[self.parts[at]]
        peer = where.neighbour(1 - 2 * where.core)
        return remote(source, target, self.send.at[at, step], self.recv.at[at, step], peer)

    def hand(self, step, at):
        target = self.slot(step + 1, at)
        return remote(
            target,
            target,
            self.send_core.at[at, step],
            self.recv_core.at[at, step],
            self.where.peer(1, 0),
        )

    def run(self, step):
        half = self.half
        if step == 0:
            self.keep().start()
        for at in range(2):
            if 0 < step <= half:
                self.copy(step - 1, at).wait_recv()
            if step < half:
                self.copy(step, at).start()
            if 0 < step < half:
                self.hand(step - 1, at).start()
            if step == half + 1:
                for past in range(half):
                    self.copy(past, at).wait_send()
                for past in range(half - 1):
                    self.hand(past, at).wait()
        if step == half + 1:
            self.keep().wait()


class RingSum:
    @staticmethod
    def scratch(size, rows, columns):
        dma = pltpu.SemaphoreType.DMA
        slots = pltpu.VMEM((size - 1, rows, columns), BF16)
        return [slots, slots, dma((4, size - 1)), dma((4, size - 1))]

    def __init__(self, where, terms, out, scratch):
        self.where, self.terms, self.out = where, terms, out
        self.held, self.landed, self.send, self.recv = scratch
        self.parts = strands(*out.shape)
        self.events = 2 * where.size

    def copy(self, at, step):
        way, part = self.parts[at]
        part = (step,) + part
        return remote(
            self.held.at[part],
            self.landed.at[part],
            self.send.at[at, step],
            self.recv.at[at, step],
            self.where.neighbour((1, -1)[way]),
        )

    def term(self, slot, part):
        if len(self.terms.shape) == 3:
            return self.terms[(slot,) + part]
        rows = self.out.shape[0]
        first = pl.multiple_of(slot * rows + part[0].start, 16)
        return self.terms[(pl.ds(first, part[0].size), part[1])]

    def run(self, event):
        step, piece = event // 2, event % 2
        where, last = self.where, self.where.size - 2
        for at in (piece, piece + 2):
            way, part = self.parts[at]
            slot = where.at_place(where.place + (-1, 1)[way] * (step + 1))
            total = self.term(slot, part)
            if step:
                self.copy(at, step - 1).wait_recv()
                total = total.astype(F32) + self.landed[(step - 1,) + part].astype(F32)
            if step <= last:
                self.held[(step,) + part] = total.astype(BF16)
                self.copy(at, step).start()
            else:
                self.out[part] = total.astype(self.out.dtype)
        if event == self.events - 1:
            for at in range(4):
                for past in range(last + 1):
                    self.copy(at, past).wait_send()


class RingSumSplit:
    @staticmethod
    def scratch(size, rows, columns):
        dma, half = pltpu.SemaphoreType.DMA, size // 2
        slots = pltpu.VMEM((half, rows, columns), BF16)
        return [slots] * 3 + [dma((half,)), dma((half,)), dma((2, half)), dma((2, half))]

    def __init__(self, where, terms, out, scratch):
        self.where, self.terms, self.out = where, terms, out
        self.given, self.held, self.landed, *sems = scratch
        self.send_core, self.recv_core, self.send, self.recv = sems
        self.half = where.size // 2
        self.events = self.half + 1
        rows = out.shape[0]
        cut = -(-rows // 32) * 16
        self.parts = (pl.ds(0, cut), pl.ds(cut, rows - cut))

    def slot(self, step, side):
        return self.where.at_place(self.where.place + side * (self.half - step))

    def give(self, step):
        side = 2 * self.where.core - 1
        return remote(
            self.terms.at[self.slot(step, side)],
            self.given.at[step],
            self.send_core.at[step],
            self.recv_core.at[step],
            self.where.peer(1, 0),
        )

    def copy(self, step, at):
        return remote(
            self.held.at[step, self.parts[at]],
            self.landed.at[step, self.parts[at]],
            self.send.at[at, step],
            self.recv.at[at, step],
            self.where.neighbour(1 - 2 * self.where.core),
        )

    def run(self, step):
        half, core = self.half, self.where.core
        if step == 0:
            for at in range(half):
                self.give(at).start()
        if step < half:
            self.give(step).wait_recv()
            slot = self.slot(step, 1 - 2 * core)
        for at, rows in enumerate(self.parts):
            if step < half:
                total = self.terms[slot, rows].astype(F32) + self.given[step, rows].astype(F32)
                if step == 0:
                    total = total * (1 - core).astype(F32)
            else:
                total = self.terms[self.where.ring, rows].astype(F32)
            if step:
                self.copy(step - 1, at).wait_recv()
                total = total + self.landed[step - 1, rows].astype(F32)
            if step < half:
                self.held[step, rows] = total.astype(BF16)
                self.copy(step, at).start()
            else:
                self.out[rows] = total.astype(self.out.dtype)
        if step == half:
            for past in range(half):
                self.give(past).wait_send()
                for at in range(2):
                    self.copy(past, at).wait_send()


class GroupGather:
    @staticmethod
    def scratch(span, parts=1):
        dma = pltpu.SemaphoreType.DMA
        return [dma((2, span, parts)), dma((2, span, parts)), dma((1,))]

    def __init__(self, where, block, out, sems, parts=1):
        self.where, self.block, self.out, self.parts = where, block, out, parts
        self.send, self.recv, self.own = sems

    def rows(self, part):
        size = self.block.shape[0] // self.parts
        return pl.ds(part * size, size)

    def hop(self, dx, part):
        where, rows = self.where, self.rows(part)
        at = (0, dx, part)
        return remote(
            self.block.at[rows],
            self.out.at[0, dx, rows],
            self.send.at[at],
            self.recv.at[at],
            where.peer(0, where.span - dx),
        )

    def cross(self, dx, part):
        rows = self.rows(part)
        source = self.out.at[0, dx, rows] if dx else self.block.at[rows]
        at = (1, dx, part)
        return remote(
            source,
            self.out.at[1, dx, rows],
            self.send.at[at],
            self.recv.at[at],
            self.where.peer(1, 0),
        )

    def start(self, part):
        for dx in range(1, self.where.span):
            self.hop(dx, part).start()
        self.cross(0, part).start()

    def pass_on(self, part):
        for dx in range(1, self.where.span):
            self.hop(dx, part).wait_recv()
            self.cross(dx, part).start()

    def arrived(self, dx):
        for part in range(self.parts):
            self.cross(dx, part).wait_recv()

    def sent(self):
        for part in range(self.parts):
            for dx in range(self.where.span):
                if dx:
                    self.hop(dx, part).wait_send()
                self.cross(dx, part).wait_send()

    def finish(self):
        for dx in range(self.where.span):
            self.arrived(dx)
        self.sent()

    def keep(self):
        return pltpu.make_async_copy(self.block, self.out.at[0, 0], self.own.at[0])

    def run(self, step):
        if step == 0:
            self.keep().start()
            for part in range(self.parts):
                self.start(part)
        elif step == 1:
            for part in range(self.parts):
                self.pass_on(part)
        else:
            self.finish()
            self.keep().wait()


class GroupSwap:
    @staticmethod
    def scratch(span):
        dma = pltpu.SemaphoreType.DMA
        return [dma((2, span)), dma((2, span)), dma((1,))]

    def __init__(self, where, source, target, sems):
        self.where, self.source, self.target = where, source, target
        self.send, self.recv, self.own = sems

    def run(self, step):
        where = self.where
        keep = pltpu.make_async_copy(self.source(0, 0), self.target(0, 0), self.own.at[0])
        copies = [
            remote(
                self.source(dc, dx),
                self.target(dc, dx),
                self.send.at[dc, dx],
                self.recv.at[dc, dx],
                where.peer(dc, dx),
            )
            for dx in reversed(range(where.span))
            for dc in range(2)
            if dc or dx
        ]
        if step == 0:
            for copy in copies:
                copy.start()
            keep.start()
        else:
            for copy in copies:
                copy.wait()
            keep.wait()


class GroupSum:
    @staticmethod
    def scratch(span, rows, columns):
        dma = pltpu.SemaphoreType.DMA
        slots = pltpu.VMEM((span, rows, columns), BF16)
        fewer = pltpu.VMEM((max(1, span - 1), rows, columns), BF16)
        return [slots, fewer, dma((span,)), dma((span,)), dma((span,)), dma((span,))]

    def __init__(self, where, terms, out, scratch):
        self.where, self.terms, self.out = where, terms, out
        self.crossed, self.landed, *sems = scratch
        self.send_core, self.recv_core, self.send, self.recv = sems

    def cross(self, dx):
        return remote(
            self.terms.at[1, dx],
            self.crossed.at[dx],
            self.send_core.at[dx],
            self.recv_core.at[dx],
            self.where.peer(1, 0),
        )

    def hop(self, dx):
        return remote(
            self.crossed.at[dx],
            self.landed.at[dx - 1],
            self.send.at[dx],
            self.recv.at[dx],
            self.where.peer(0, dx),
        )

    def fold(self, dx):
        self.cross(dx).wait_recv()
        total = self.terms[0, dx].astype(F32) + self.crossed[dx].astype(F32)
        self.crossed[dx] = total.astype(BF16)
        self.hop(dx).start()

    def finish(self):
        self.cross(0).wait_recv()
        total = self.terms[0, 0].astype(F32) + self.crossed[0].astype(F32)
        for dx in range(1, self.where.span):
            self.hop(dx).wait_recv()
            total = total + self.landed[dx - 1].astype(F32)
        self.out[...] = total.astype(self.out.dtype)
        for dx in range(self.where.span):
            self.cross(dx).wait_send()
            if dx:
                self.hop(dx).wait_send()

    def run(self, step):
        later = list(reversed(range(self.where.span)))
        if step == 0:
            for dx in later:
                self.cross(dx).start()
        elif step == 1:
            for dx in later[:-1]:
                self.fold(dx)
        else:
            self.finish()


class CoreSum:
    @staticmethod
    def scratch(span, rows, columns):
        dma = pltpu.SemaphoreType.DMA
        return [pltpu.VMEM((span, rows, columns), BF16), dma((span,)), dma((span,))]

    def __init__(self, where, terms, out, scratch):
        self.where, self.terms, self.out = where, terms, out
        self.crossed, self.send_core, self.recv_core = scratch

    def cross(self, dx):
        return remote(
            self.terms.at[dx],
            self.crossed.at[dx],
            self.send_core.at[dx],
            self.recv_core.at[dx],
            self.where.peer(1, 0),
        )

    def fold(self, dx):
        self.cross(dx).wait_recv()
        total = self.out[dx].astype(F32) + self.crossed[dx].astype(F32)
        self.out[dx] = total.astype(BF16)

    def finish(self):
        for dx in range(self.where.span):
            self.cross(dx).wait_send()


class PatchSum:
    @staticmethod
    def scratch(span, rows, columns):
        dma = pltpu.SemaphoreType.DMA
        return [pltpu.VMEM((max(1, span - 1), rows, columns), BF16), dma((span,)), dma((span,))]

    def __init__(self, where, terms, out, scratch):
        self.where, self.crossed, self.out = where, terms, out
        self.landed, self.send, self.recv = scratch

    hop = GroupSum.hop

    def run(self, step):
        span = self.where.span
        if step == 0:
            for dx in range(1, span):
                self.hop(dx).start()
        else:
            total = self.crossed[0].astype(F32)
            for dx in range(1, span):
                self.hop(dx).wait_recv()
                total = total + self.landed[dx - 1].astype(F32)
            self.out[...] = total
            for dx in range(1, span):
                self.hop(dx).wait_send()


class AllSum:
    @staticmethod
    def bits(sizes, axes=(2, 0, 1)):
        found = []
        for axis in axes:
            bit = 1
            while bit < sizes[axis]:
                found.append((axis, bit))
                bit *= 2
        return found

    @staticmethod
    def scratch(sizes, shape):
        count = len(AllSum.bits(sizes))
        dma = pltpu.SemaphoreType.DMA
        slots = pltpu.VMEM((count,) + tuple(shape), F32)
        return [slots, slots, dma((count,)), dma((count,))]

    def __init__(self, where, sizes, block, out, scratch, axes=(2, 0, 1)):
        self.block, self.out = block, out
        self.held, self.landed, self.send, self.recv = scratch
        here = (where.ring, where.core, where.patch)
        self.peers = []
        for axis, bit in AllSum.bits(sizes, axes):
            peer = list(here)
            peer[axis] = here[axis] + (1 - 2 * ((here[axis] // bit) % 2)) * bit
            self.peers.append(tuple(peer))
        self.events = len(self.peers) + 1

    def copy(self, step):
        return remote(
            self.held.at[step],
            self.landed.at[step],
            self.send.at[step],
            self.recv.at[step],
            self.peers[step],
        )

    def run(self, step):
        if step == 0:
            total = self.block[...]
        else:
            self.copy(step - 1).wait()
            total = self.held[step - 1] + self.landed[step - 1]
        if step < len(self.peers):
            self.held[step] = total
            self.copy(step).start()
        else:
            self.out[...] = total


HBM = pl.BlockSpec(memory_space=pl.ANY)
CORE = pl.BlockSpec(memory_space=pltpu.VMEM)


def take(refs, counts):
    found, at = [], 0
    for count in counts:
        found.append(list(refs[at : at + count]))
        at += count
    return found


def loads(pairs, sems):
    copies = [
        pltpu.make_async_copy(source, target, sems.at[at])
        for at, (source, target) in enumerate(pairs)
    ]
    for copy in copies:
        copy.start()
    return copies


def flat_block(vector):
    rows = -(-vector.shape[0] // 1024) * 8
    return jnp.pad(vector, (0, rows * 128 - vector.shape[0])).reshape(rows, 128)


def join(pieces, wide, block):
    group, share, _ = pieces.shape
    for at in range(group):
        wide[at * share : (at + 1) * share, :] = pieces[at].astype(F32)
    block[...] = wide[...].astype(BF16)


def entry_kernel(sizes, clips, chunk, *refs):
    where = Where(sizes)
    ins, outs, scratch = take(refs, (8, 9, len(refs) - 17))
    tokens, qkv_far, up_far, out_rows, silu_part, ada_far, small, frame_clip = ins
    tokens_all, w_qkv, out_block, up_block, summed, hidden, found_far, own_rows, bias_up = outs
    held, cols, lands, wide, (qkv_block, w_qkv_t, vector, spread, normal), *sems = take(
        scratch, (6, 2, 3, 3, 5, 3, 3, 3, 3, 3, 4)
    )
    qkv_weight, up_weight, ada_weight, projected, load_sems, store_sems = held
    have_qkv, have_ada, have_up = loads(
        [(qkv_far, qkv_weight), (ada_far, ada_weight), (up_far, up_weight)], load_sems
    )
    sums = AllSum(where, sizes, vector, summed, sems[5])
    member, span, group = where.member, where.span, 2 * where.span
    rows, width = tokens.shape
    share = out_rows.shape[0]
    device = where.ring * group + member

    def swap(source, land, job_sems):
        return GroupSwap(where, source, lambda dc, dx: land.at[member], job_sems)

    swap_qkv = swap(lambda dc, dx: cols[0].at[where.peer_member(dc, dx)], lands[0], sems[0])
    swap_up = swap(lambda dc, dx: cols[1].at[where.peer_member(dc, dx)], lands[1], sems[1])
    swap_out = swap(lambda dc, dx: out_rows, lands[2], sems[2])
    gather = GroupGather(where, tokens, tokens_all, sems[3], max(1, rows // 128))
    ring = RingGather(where, qkv_block, w_qkv, sems[4])

    features = qkv_weight.shape[1] // (3 * group)
    have_qkv.wait()
    wide_rows = qkv_weight[...].astype(F32)
    for at in range(group):
        for part in range(3):
            low = (part * group + at) * features
            cols[0][at, :, part * features : (part + 1) * features] = wide_rows[
                :, low : low + features
            ].astype(BF16)

    units = up_weight.shape[1] // (group * where.size)
    spread[...] = jnp.zeros_like(spread)
    lengths = [share] * 4 + [units, 6 * share]
    low = 0
    for at, length in enumerate(lengths):
        spread[at : at + 1, :length] = small[0:1, low : low + length]
        low += length
    lanes = lax.broadcasted_iota(jnp.int32, (1, width), 1)
    vector[...] = jnp.zeros_like(vector)
    vector[0:4, :] = pltpu.roll(spread[...], device * share, 1)[0:4]
    start = device * units
    moved = pltpu.roll(spread[...], start % width, 1)[4:5]
    for at in range(4):
        vector[4 + at : 5 + at, :] = jnp.where(start // width == at, moved, 0.0)
    start = device * 6 * share
    moved = pltpu.roll(spread[...], start % width, 1)[5:6]
    lies = start // width + jnp.where(lanes < start % width, 1, 0)
    have_ada.wait()
    terms = jnp.dot(silu_part[...], ada_weight[...], preferred_element_type=F32)
    for part in range(6):
        bias = jnp.where(lies == part, moved, 0.0)
        for clip in range(clips):
            at = 8 + 6 * clip + part
            vector[at : at + 1, :] = (
                terms[clip : clip + 1, part * width : (part + 1) * width] + bias
            )
    own_clip = frame_clip[0].astype(F32)
    own_frame = 2 * where.ring + where.core
    at = 8 + 6 * clips
    vector[at : at + 1, :] = jnp.where((lanes == own_frame) & (where.patch == 0), own_clip, 0.0)

    greet(where.ring_peers() + where.group_peers() + sums.peers)
    swap_qkv.run(0)
    sums.run(0)
    swap_qkv.run(1)
    join(lands[0], wide[0], qkv_block)
    ring.run(0)
    ring.run(1)
    gather.run(0)
    have_up.wait()
    wide_rows = up_weight[...].astype(F32)
    for at in range(group):
        for ring_at in range(where.size):
            low = (ring_at * group + at) * units
            cols[1][at, :, ring_at * units : (ring_at + 1) * units] = wide_rows[
                :, low : low + units
            ].astype(BF16)
    swap_up.run(0)
    swap_out.run(0)
    ring.run(2)
    sums.run(1)
    ring.run(3)
    ring.run(4)

    def norm(dc, dx, at, count):
        first = (dc * span + dx) * rows + at
        normal[first : first + count, :], _ = layer_norm(
            tokens_all[dc, dx, at : at + count, :].astype(F32)
        )

    gather.keep().wait()
    near = [(dc, at) for dc in range(2) for at in range(0, rows, chunk)]
    for event in range(5, ring.events):
        ring.run(event)
        if event % 2 == 0 and event // 2 - 1 < sums.events - 1:
            sums.run(event // 2 - 1)
        if near and event > 5:
            dc, at = near.pop(0)
            if dc and not at:
                gather.arrived(0)
            norm(dc, 0, at, chunk)
    sums.run(sums.events - 1)

    at = 8 + 6 * clips
    other_frame = 2 * where.ring + 1 - where.core
    other_clip = jnp.sum(
        jnp.where(lanes == other_frame, summed[at : at + 1, :], 0.0), axis=1, keepdims=True
    )
    own, other = [0.0] * 6, [0.0] * 2
    for clip in range(clips):
        is_own = jnp.maximum(1.0 - jnp.abs(own_clip - clip), 0.0)
        is_other = jnp.maximum(1.0 - jnp.abs(other_clip - clip), 0.0)
        for part in range(6):
            row = summed[8 + 6 * clip + part : 9 + 6 * clip + part, :]
            own[part] = own[part] + is_own * row
            if part < 2:
                other[part] = other[part] + is_other * row
        own_rows[8 + clip : 9 + clip, :] = jnp.zeros((1, width), F32) + is_own
        own_rows[8 + clips + clip : 9 + clips + clip, :] = jnp.zeros((1, width), F32) + is_other
    for part in range(6):
        own_rows[part : part + 1, :] = own[part]
    own_rows[6:8, :] = summed[2:4, :]
    for ring_at in range(where.size):
        start = (ring_at * group + member) * units
        moved = pltpu.roll(summed[0:8, :], (width - start % width) % width, 1)
        picked = jnp.zeros((1, width), F32)
        for at in range(4):
            picked = picked + jnp.where(start // width == at, moved[4 + at : 5 + at], 0.0)
        bias_up[:, ring_at * units : (ring_at + 1) * units] = picked[:, :units]

    features = qkv_block.shape[1] // 3
    lead = pltpu.roll(summed[0:8, :], (width - member * features) % width, 1).T
    bias_q, bias_v = lead[:features, 0:1], lead[:features, 1:2]
    w_qkv_t[...] = w_qkv[...].reshape(width, 3 * features).T

    stored = []

    def project(dc, dx, at):
        shift, scale = (other if dc else own)[:2]
        first = (dc * span + dx) * rows + at
        low = (normal[first : first + chunk, :] * (1.0 + scale) + shift).astype(BF16)
        hidden[first : first + chunk, :] = low
        found = lax.dot_general(
            w_qkv_t[...], low, (((1,), (1,)), ((), ())), preferred_element_type=F32
        )
        there = slice(first, first + chunk)
        projected[:features, there] = (found[:features] + bias_q).astype(BF16)
        projected[features : 2 * features, there] = found[features : 2 * features].astype(BF16)
        projected[2 * features :, there] = (found[2 * features :] + bias_v).astype(BF16)
        stored.extend(
            loads(
                [(projected.at[:, pl.ds(first, chunk)], found_far.at[:, pl.ds(first, chunk)])],
                store_sems.at[pl.ds(len(stored), 1)],
            )
        )

    for dx in range(span):
        if dx == 1:
            swap_up.run(1)
            join(lands[1], wide[1], up_block)
            swap_out.run(1)
            join(lands[2], wide[2], out_block)
            gather.run(1)
        for dc in range(2):
            if dc and dx:
                gather.arrived(dx)
            for at in range(0, rows, chunk):
                if dx:
                    norm(dc, dx, at, chunk)
                project(dc, dx, at)
    for copy in stored:
        copy.wait()
    gather.sent()


def entry(
    tokens, qkv_weight, up_weight, out_rows, silu_part, ada_weight, small, clip, sizes, call_id
):
    size, _, span = sizes
    group, share = 2 * span, out_rows.shape[0]
    rows, width = tokens.shape
    clips = silu_part.shape[0]
    block_rows = group * share
    columns = [qkv_weight.shape[1] // group, up_weight.shape[1] // group, width]
    count = 9 + 6 * clips
    vector = (count + -count % 8, width)
    shape = jax.ShapeDtypeStruct
    scratch = [
        pltpu.VMEM(item.shape, BF16) for item in (qkv_weight, up_weight, ada_weight)
    ]
    scratch += [pltpu.VMEM((columns[0], group * rows), BF16)]
    scratch += [pltpu.SemaphoreType.DMA((3,))]
    scratch += [pltpu.SemaphoreType.DMA((group * rows // min(256, rows),))]
    scratch += [pltpu.VMEM((group, share, n), BF16) for n in columns[:2]]
    scratch += [pltpu.VMEM((group, share, n), BF16) for n in columns]
    scratch += [pltpu.VMEM((block_rows, n), F32) for n in columns]
    scratch += [pltpu.VMEM((block_rows, columns[0]), BF16)]
    scratch += [pltpu.VMEM((columns[0], width), BF16)]
    scratch += [pltpu.VMEM(vector, F32), pltpu.VMEM((8, width), F32)]
    scratch += [pltpu.VMEM((group * rows, width), F32)]
    scratch += GroupSwap.scratch(span) * 3
    scratch += GroupGather.scratch(span, max(1, rows // 128))
    scratch += RingGather.scratch(size)
    scratch += AllSum.scratch(sizes, vector)
    return pl.pallas_call(
        functools.partial(entry_kernel, sizes, clips, min(256, rows)),
        out_shape=[
            shape((2, span, rows, width), BF16),
            shape((size, block_rows, columns[0]), BF16),
            shape((block_rows, width), BF16),
            shape((block_rows, columns[1]), BF16),
            shape(vector, F32),
            shape((group * rows, width), BF16),
            shape((columns[0], group * rows), BF16),
            shape((8 + 2 * clips + -2 * clips % 8, width), F32),
            shape((1, columns[1]), F32),
        ],
        in_specs=[HBM, HBM, HBM, HBM, CORE, HBM, CORE, pl.BlockSpec(memory_space=pltpu.SMEM)],
        out_specs=[CORE] * 6 + [HBM] + [CORE] * 2,
        scratch_shapes=scratch,
        compiler_params=pltpu.CompilerParams(
            collective_id=call_id, has_side_effects=True, vmem_limit_bytes=61 * MIB
        ),
        name="entry",
    )(tokens, qkv_weight, up_weight, out_rows, silu_part, ada_weight, small, clip)


def beside(job, total, places, count, first=0, stride=1):
    at = pl.program_id(0) * pl.num_programs(1) + pl.program_id(1)
    slots, event = {}, 0
    for place in range(first, total * places, stride):
        todo = list(range(event, min(event + count, job.events - 1)))
        if todo:
            slots[place] = todo
            event += len(todo)

    def ahead(place):
        for grid in range(total):
            todo = slots.get(grid * places + place)
            if todo:

                @pl.when(at == grid)
                def _():
                    for event in todo:
                        job.run(event)

    def finish():
        for late in range(event, job.events):
            job.run(late)

    return ahead, finish


def attention_kernel(sizes, factor, chunk, total, *refs):
    where = Where(sizes)
    ins, outs, scratch = take(refs, (5, 4, len(refs) - 9))
    q_ref, k_ref, v_ref, up_block, grad_block = ins
    out_ref, lse_ref, w_up, grad_all = outs
    sems = take(scratch, (3, 3))
    chunks = q_ref.shape[2] // chunk
    places = max(chunks // 2, 1)
    ahead, finish = beside(RingGather(where, up_block, w_up, sems[0]), total, places, 1)
    gather = GroupGather(where, grad_block, grad_all, sems[1], 2)
    at = pl.program_id(0) * pl.num_programs(1) + pl.program_id(1)

    @pl.when(at == 0)
    def _():
        greet(where.ring_peers() + where.group_peers())
        gather.run(0)

    keys = k_ref[0].T
    values_t = v_ref[0]
    for number in range(chunks):
        if number % 2 == 0:
            ahead(number // 2)
        span = slice(number * chunk, (number + 1) * chunk)
        scores = jnp.dot(keys, q_ref[0, :, span], preferred_element_type=F32) * factor
        top = jnp.max(scores, axis=0, keepdims=True)
        probs = jnp.exp2(scores - top)
        row_sum = jnp.sum(probs, axis=0, keepdims=True)
        mixed = jnp.dot(values_t, probs.astype(BF16), preferred_element_type=F32)
        out_ref[0, :, span] = (mixed / row_sum).astype(BF16)
        lse_ref[0, :, span] = top + jnp.log2(row_sum)

    @pl.when(at == total - 1)
    def _():
        gather.run(1)
        finish()
        gather.run(2)


def attention(qkv, up_block, grad_block, patches, sizes, call_id):
    size, _, span = sizes
    triple, dim, tokens = qkv.shape
    heads = triple // 3
    frames = tokens // patches
    block = (1, dim, patches)
    factor = LOG2E / math.sqrt(HEAD_DIM)
    shape = jax.ShapeDtypeStruct
    return pl.pallas_call(
        functools.partial(attention_kernel, sizes, factor, min(256, patches), frames * heads),
        out_shape=[
            shape((heads, dim, tokens), BF16),
            shape((heads, 1, tokens), F32),
            shape((size,) + up_block.shape, BF16),
            shape((2, span) + grad_block.shape, BF16),
        ],
        grid=(frames, heads),
        in_specs=[
            pl.BlockSpec(block, lambda f, h: (h, 0, f)),
            pl.BlockSpec(block, lambda f, h: (heads + h, 0, f)),
            pl.BlockSpec(block, lambda f, h: (2 * heads + h, 0, f)),
            HBM,
            HBM,
        ],
        out_specs=[
            pl.BlockSpec(block, lambda f, h: (h, 0, f)),
            pl.BlockSpec((1, 1, patches), lambda f, h: (h, 0, f)),
            HBM,
            HBM,
        ],
        scratch_shapes=RingGather.scratch(size) + GroupGather.scratch(span, 2),
        compiler_params=pltpu.CompilerParams(
            collective_id=call_id, has_side_effects=True, vmem_limit_bytes=32 * MIB
        ),
        cost_estimate=pl.CostEstimate(
            flops=4 * heads * patches * tokens * 256,
            bytes_accessed=4 * heads * dim * tokens * 2,
            transcendentals=heads * patches * tokens,
        ),
        name="attention",
    )(qkv, qkv, qkv, up_block, grad_block)


def attention_back_kernel(sizes, factor, chunk, total, *refs):
    where = Where(sizes)
    ins, outs, scratch = take(refs, (7, 3, len(refs) - 10))
    q_ref, k_ref, v_ref, g_ref, lse_ref, up_terms, half_terms = ins
    grads_ref, up_sum, half_sum = outs
    dk_sum, dv_sum = scratch[:2]
    own = take(scratch[2:], (4, 3))
    patches = q_ref.shape[2]
    chunks = patches // chunk
    places = max(chunks // 2, 1)
    ahead, finish = beside(RingSum(where, up_terms, up_sum, own[0]), total, places, 1)
    half = PatchSum(where, half_terms, half_sum, own[1])
    at = pl.program_id(0) * pl.num_programs(1) + pl.program_id(1)

    @pl.when(at == 0)
    def _():
        greet(where.ring_peers() + where.group_peers())
        half.run(0)

    keys_t = k_ref[0]
    keys = keys_t.T
    values = v_ref[0].T
    scale = factor / LOG2E
    for number in range(chunks):
        if number % 2 == 0:
            ahead(number // 2)
        span = slice(number * chunk, (number + 1) * chunk)
        queries_t = q_ref[0, :, span]
        grad_t = g_ref[0, :, span]
        scores = jnp.dot(keys, queries_t, preferred_element_type=F32) * factor
        probs = jnp.exp2(scores - lse_ref[0, :, span])
        grad_probs = jnp.dot(values, grad_t, preferred_element_type=F32)
        row_dot = jnp.sum(probs * grad_probs, axis=0, keepdims=True)
        grad_scores = (probs * (grad_probs - row_dot)).astype(BF16)
        probs_low = probs.astype(BF16)
        dq = jnp.dot(keys_t, grad_scores, preferred_element_type=F32)
        grads_ref[0, 0, :, span] = (dq * scale).astype(BF16)
        dims = (((1,), (1,)), ((), ()))
        dk = lax.dot_general(queries_t, grad_scores, dims, preferred_element_type=F32)
        dv = lax.dot_general(grad_t, probs_low, dims, preferred_element_type=F32)
        if number == 0:
            dk_sum[...] = dk
            dv_sum[...] = dv
        else:
            dk_sum[...] += dk
            dv_sum[...] += dv
    grads_ref[1, 0] = (dk_sum[...] * scale).astype(BF16)
    grads_ref[2, 0] = dv_sum[...].astype(BF16)

    @pl.when(at == total - 1)
    def _():
        finish()
        half.run(1)


def attention_back(qkv, grad, lse, up_terms, half_terms, patches, sizes, call_id):
    size, _, span = sizes
    triple, dim, tokens = qkv.shape
    heads = triple // 3
    frames = tokens // patches
    block = (1, dim, patches)
    factor = LOG2E / math.sqrt(HEAD_DIM)
    spec = pl.BlockSpec(block, lambda f, h: (h, 0, f))
    shape = jax.ShapeDtypeStruct
    return pl.pallas_call(
        functools.partial(attention_back_kernel, sizes, factor, min(256, patches), frames * heads),
        out_shape=[
            shape((3, heads, dim, tokens), BF16),
            shape(up_terms.shape[1:], BF16),
            shape(half_terms.shape[1:], F32),
        ],
        grid=(frames, heads),
        in_specs=[
            spec,
            pl.BlockSpec(block, lambda f, h: (heads + h, 0, f)),
            pl.BlockSpec(block, lambda f, h: (2 * heads + h, 0, f)),
            spec,
            pl.BlockSpec((1, 1, patches), lambda f, h: (h, 0, f)),
            CORE,
            CORE,
        ],
        out_specs=[pl.BlockSpec((3,) + block, lambda f, h: (0, h, 0, f)), CORE, CORE],
        scratch_shapes=[pltpu.VMEM((dim, patches), F32)] * 2
        + RingSum.scratch(size, *up_terms.shape[1:])
        + PatchSum.scratch(span, *half_terms.shape[1:]),
        compiler_params=pltpu.CompilerParams(
            collective_id=call_id, has_side_effects=True, vmem_limit_bytes=61 * MIB
        ),
        cost_estimate=pl.CostEstimate(
            flops=10 * heads * patches * tokens * 256,
            bytes_accessed=8 * heads * dim * tokens * 2,
            transcendentals=heads * patches * tokens,
        ),
        name="attention_back",
    )(qkv, qkv, qkv, grad, lse, up_terms, half_terms)


def joined(array):
    group, features, count = array.shape
    if features % 16:
        return array.astype(F32).reshape(group * features, count).astype(BF16)
    return array.reshape(group * features, count)


def middle_kernel(sizes, parts, *refs):
    where = Where(sizes)
    ins, outs, scratch = take(refs, (5, 6, len(refs) - 11))
    heads_t, out_block, tokens_far, vectors, down_block = ins
    attended, branch, midway, hidden_all, w_out, w_down = outs
    (hidden, tokens, load_sems), *sems = take(scratch, (3, 3, 3, 3, 5))
    (have_tokens,) = loads([(tokens_far, tokens)], load_sems)
    greet(where.ring_peers() + where.group_peers())
    rows, width = tokens.shape
    span = where.span

    swap = GroupSwap(
        where,
        lambda dc, dx: heads_t.at[:, pl.ds((dc * span + dx) * rows, rows)],
        lambda dc, dx: attended.at[where.member],
        sems[0],
    )
    ring = RingGather(where, down_block, w_down, sems[1])
    gather = GroupGather(where, hidden, hidden_all, sems[2], parts)
    ring_out = RingGatherSplit(where, out_block, w_out, sems[3])
    swap.run(0)
    ring_out.run(0)
    for event in range(ring_out.events - 2):
        ring.run(event)
        ring_out.run(event + 1)
    event += 1
    swap.run(1)
    ring_out.run(ring_out.events - 1)
    size = rows // parts
    full = w_out[...].reshape(width, width)
    have_tokens.wait()
    for part in range(parts):
        span_rows = slice(part * size, (part + 1) * size)
        mixed = joined(attended[:, :, span_rows])
        one = lax.dot_general(mixed, full, (((0,), (0,)), ((), ())), preferred_element_type=F32)
        one = one + vectors[6:7, :]
        branch[span_rows, :] = one
        mid = tokens[span_rows, :].astype(F32) + vectors[2:3, :] * one
        midway[span_rows, :] = mid
        normed, _ = layer_norm(mid)
        hidden[span_rows, :] = (normed * (1.0 + vectors[4:5, :]) + vectors[3:4, :]).astype(BF16)
        gather.start(part)
        if event < ring.events:
            ring.run(event)
            event += 1
    gather.keep().start()
    for event in range(event, ring.events):
        ring.run(event)
    for part in range(parts):
        gather.pass_on(part)
    gather.finish()
    gather.keep().wait()


def middle(heads_t, out_block, tokens, vectors, down_block, sizes, call_id):
    size, _, span = sizes
    rows, width = tokens.shape
    parts = rows // 128
    shape = jax.ShapeDtypeStruct
    return pl.pallas_call(
        functools.partial(middle_kernel, sizes, parts),
        out_shape=[
            shape((2 * span, heads_t.shape[0], rows), BF16),
            shape((rows, width), F32),
            shape((rows, width), F32),
            shape((2, span, rows, width), BF16),
            shape((size,) + out_block.shape, BF16),
            shape((size,) + down_block.shape, BF16),
        ],
        in_specs=[HBM, HBM, HBM, CORE, HBM],
        out_specs=[CORE] * 6,
        scratch_shapes=[pltpu.VMEM((rows, width), BF16)] * 2
        + [pltpu.SemaphoreType.DMA((1,))]
        + GroupSwap.scratch(span)
        + RingGather.scratch(size)
        + GroupGather.scratch(span, parts)
        + RingGatherSplit.scratch(size),
        compiler_params=pltpu.CompilerParams(
            collective_id=call_id, has_side_effects=True, vmem_limit_bytes=61 * MIB
        ),
        name="middle",
    )(heads_t, out_block, tokens, vectors, down_block)


def gelu_both(values_in):
    square = values_in * values_in
    inner = 0.7978845608028654 * values_in * (1.0 + 0.044715 * square)
    bent = jnp.tanh(inner)
    outer = 0.5 * (1.0 + bent)
    slope = 0.7978845608028654 * (1.0 + 3.0 * 0.044715 * square)
    return values_in * outer, outer + 0.5 * values_in * (1.0 - bent * bent) * slope


def feed_kernel(sizes, chunk, tile, *refs):
    where = Where(sizes)
    ins, outs, scratch = take(refs, (5, 5, len(refs) - 10))
    *far_away, bias = ins
    half, grad_hidden, g_up, down_sum, g_bias = outs
    here_now, (act, grad_pre, branch, back, g_down), *own = take(scratch, (5, 5, 3, 6, 4))
    hidden, w_up, grad, w_down, load_sems = here_now
    order = (0, 2, 1, 3)
    have = loads(
        [(far_away[at], target) for at, target in zip(order, here_now)], load_sems
    )
    span = where.span
    rows, width = grad_hidden.shape
    units = bias.shape[1]
    sum_half = CoreSum(where, branch, half, own[0])
    sum_back = GroupSum(where, back, grad_hidden, own[1])
    ring = RingSum(where, g_down, down_sum, own[2])
    greet(where.ring_peers() + where.group_peers())
    each = rows // chunk
    steps = 2 * span * each
    across = (((1,), (1,)), ((), ()))
    over = (((0,), (0,)), ((), ()))

    def forward(step, total):
        here = pl.ds(pl.multiple_of(step * chunk, chunk), chunk)
        pre = jnp.dot(hidden[here, :], w_up[...], preferred_element_type=F32) + bias[...]
        value, slope = gelu_both(pre)
        act[here, :] = value.astype(BF16)
        grad_act = lax.dot_general(grad[here, :], w_down[...], across, preferred_element_type=F32)
        low = (grad_act * slope).astype(BF16)
        grad_pre[here, :] = low
        return total + jnp.sum(low.astype(F32), axis=0, keepdims=True)

    for copy in have:
        copy.wait()
    g_bias[...] = lax.fori_loop(0, steps, forward, jnp.zeros((1, units), F32))
    for low in range(0, units, tile):
        cut = slice(low, low + tile)
        found = lax.dot_general(act[:, cut], grad[...], over, preferred_element_type=F32)
        if len(g_down.shape) == 2:
            g_down[cut, :] = found.astype(BF16)
        else:
            size = g_down.shape[1]
            for at in range(tile // size):
                g_down[low // size + at] = found[at * size : (at + 1) * size].astype(BF16)
    ring.run(0)
    ring.run(1)

    def beside_ring(step, first, every, count):
        for at in range(count):
            if first + at < ring.events:
                pl.when(step == (at + 1) * every - 1)(functools.partial(ring.run, first + at))

    def backward(step, carry):
        at = step // each
        dx, dc = span - 1 - at // 2, 1 - at % 2
        inside = pl.ds(pl.multiple_of(step % each * chunk, chunk), chunk)
        first = pl.multiple_of((dc * span + dx) * rows + step % each * chunk, chunk)
        here = pl.ds(first, chunk)
        back[dc, dx, inside, :] = lax.dot_general(
            grad_pre[here, :], w_up[...], across, preferred_element_type=F32
        ).astype(BF16)
        for place in range(2 * span):
            done_dx, done_dc = span - 1 - place // 2, 1 - place % 2

            @pl.when(step == (place + 1) * each - 1)
            def _():
                if done_dc:
                    sum_back.cross(done_dx).start()
                elif done_dx:
                    sum_back.fold(done_dx)

        beside_ring(step, 2, 2, steps // 2)
        return carry

    lax.fori_loop(0, steps, backward, 0)
    event = min(2 + steps // 2, ring.events)

    def give(target, dc, first_event):
        def body(step, carry):
            dx = step // each
            inside = pl.ds(pl.multiple_of(step % each * chunk, chunk), chunk)
            first = pl.multiple_of(dc * span * rows + step * chunk, chunk)
            target[dx, inside, :] = jnp.dot(
                act[pl.ds(first, chunk), :], w_down[...], preferred_element_type=F32
            ).astype(BF16)
            beside_ring(step, first_event, 2, steps // 4)
            return carry

        lax.fori_loop(0, steps // 2, body, 0)
        return min(first_event + steps // 4, ring.events)

    event = give(branch, 1, event)
    for dx in range(span):
        sum_half.cross(dx).start()
    event = give(half, 0, event)
    for low in range(0, width, tile):
        if event < ring.events:
            ring.run(event)
            event += 1
        cut = slice(low, low + tile)
        g_up[cut, :] = lax.dot_general(
            hidden[:, cut], grad_pre[...], over, preferred_element_type=F32
        ).astype(BF16)
    for dx in range(span):
        sum_half.fold(dx)
    for event in range(event, ring.events):
        ring.run(event)
    sum_half.finish()
    sum_back.finish()


def feed(hidden, grad, w_up, w_down, bias, sizes, call_id):
    size, _, span = sizes
    tokens, width = hidden.shape
    units = w_up.shape[1]
    rows = tokens // (2 * span)
    block = (units // size, width)
    shape = jax.ShapeDtypeStruct
    return pl.pallas_call(
        functools.partial(feed_kernel, sizes, min(256, rows), 384 if units % 384 == 0 else units),
        out_shape=[
            shape((span, rows, width), BF16),
            shape((rows, width), F32),
            shape((width, units), BF16),
            shape(block, F32),
            shape((1, units), F32),
        ],
        in_specs=[HBM] * 4 + [CORE],
        out_specs=[CORE] * 5,
        scratch_shapes=[pltpu.VMEM(item.shape, BF16) for item in (hidden, w_up, grad, w_down)]
        + [pltpu.SemaphoreType.DMA((4,))]
        + [pltpu.VMEM((tokens, units), BF16)] * 2
        + [pltpu.VMEM((span, rows, width), BF16), pltpu.VMEM((2, span, rows, width), BF16)]
        + [pltpu.VMEM((size,) + block if block[0] % 16 else (units, width), BF16)]
        + CoreSum.scratch(span, rows, width)
        + GroupSum.scratch(span, rows, width)
        + RingSum.scratch(size, *block),
        compiler_params=pltpu.CompilerParams(
            collective_id=call_id, has_side_effects=True, vmem_limit_bytes=61 * MIB
        ),
        name="feed",
    )(hidden, grad, w_up, w_down, bias)


def return_kernel(sizes, parts, tile, *refs):
    where = Where(sizes)
    ins, outs, scratch = take(refs, (7, 4, len(refs) - 11))
    grad_hidden, midway, branch, grad_out, w_out, attended, vectors = ins
    grad_mid, grad_mix, g_out, sums = outs
    (grad_heads, grad_one), own = take(scratch, (2, 3 * parts))
    greet(where.group_peers())
    rows, width = midway.shape
    span = where.span
    size = rows // parts
    features = grad_heads.shape[1]
    swaps = []
    for part in range(parts):
        cut = pl.ds(part * size, size)

        def source(dc, dx, cut=cut):
            return grad_heads.at[where.peer_member(dc, dx), :, cut]

        def target(dc, dx, part=part):
            block = dc * span + (span - dx) % span
            return grad_mix.at[:, pl.ds(block * rows + part * size, size)]

        swaps.append(GroupSwap(where, source, target, own[3 * part : 3 * part + 3]))
    full = w_out[...]
    totals = [jnp.zeros((1, width), F32)] * 4
    for part in range(parts):
        here = slice(part * size, (part + 1) * size)
        normed, inv_std = layer_norm(midway[here, :])
        grad = grad_hidden[here, :]
        mid = grad_out[here, :].astype(F32) + norm_back(
            grad * (1.0 + vectors[4:5, :]), normed, inv_std
        )
        grad_mid[here, :] = mid
        low = (vectors[2:3, :] * mid).astype(BF16)
        grad_one[here, :] = low
        heads_t = lax.dot_general(full, low, (((1,), (1,)), ((), ())), preferred_element_type=F32)
        grad_heads[:, :, here] = heads_t.reshape(2 * span, features, size).astype(BF16)
        swaps[part].run(0)
        found = [grad, grad * normed, mid * branch[here, :], low.astype(F32)]
        totals = [
            total + jnp.sum(item, axis=0, keepdims=True) for total, item in zip(totals, found)
        ]
    for at, total in enumerate(totals):
        sums[at : at + 1, :] = total
    sums[4:8, :] = jnp.zeros((4, width), F32)
    for low in range(0, width, tile):
        cut = slice(low, low + tile)
        g_out[cut, :] = jnp.dot(
            attended[cut, :], grad_one[...], preferred_element_type=F32
        ).astype(BF16)
    for swap in swaps:
        swap.run(1)


def back_to_heads(
    grad_hidden, midway, branch, grad_out, w_out, attended, vectors, sizes, call_id
):
    span = sizes[2]
    rows, width = midway.shape
    group = 2 * span
    parts = rows // 128
    features = width // group
    shape = jax.ShapeDtypeStruct
    return pl.pallas_call(
        functools.partial(return_kernel, sizes, parts, 384),
        out_shape=[
            shape((rows, width), F32),
            shape((features, group * rows), BF16),
            shape((width, width), BF16),
            shape((8, width), F32),
        ],
        in_specs=[CORE] * 7,
        out_specs=[CORE] * 4,
        scratch_shapes=[
            pltpu.VMEM((group, features, rows), BF16),
            pltpu.VMEM((rows, width), BF16),
        ]
        + GroupSwap.scratch(span) * parts,
        compiler_params=pltpu.CompilerParams(
            collective_id=call_id, has_side_effects=True, vmem_limit_bytes=61 * MIB
        ),
        name="back_to_heads",
    )(grad_hidden, midway, branch, grad_out, w_out, attended, vectors)


def last_kernel(sizes, chunk, tile, clips, *refs):
    where = Where(sizes)
    ins, outs, scratch = take(refs, (11, 6, len(refs) - 17))
    grad_qkv, hidden, tokens, w_qkv, grad_mid, out_terms, early, own_rows = ins[:8]
    midway, branch, grad_out = ins[8:]
    tokens_grad, output, qkv_sum, out_sum, early_sum, late_sum = outs
    (back, g_qkv, late, grad_hidden, spread), *own = take(scratch, (5, 6, 4, 4, 4, 7))
    span = where.span
    rows, width = grad_mid.shape
    sum_back = GroupSum(where, back, grad_hidden, own[0])
    ring = RingSum(where, g_qkv, qkv_sum, own[1])
    first_sums = AllSum(where, sizes, early, early_sum, own[2])
    sums = AllSum(where, sizes, late, late_sum, own[3], (0, 1, 2))
    ring_out = RingSumSplit(where, out_terms, out_sum, own[4])
    greet(where.ring_peers() + where.group_peers() + sums.peers)
    ring_out.run(0)
    first_sums.run(0)
    each = rows // chunk
    blocks = 2 * span
    far = 2 * (span - 1) * each
    planned = {far + at: [(ring, 2 + at)] for at in range(2 * each)}
    planned[far + 1].append((first_sums, 3))
    planned[far + 2 * each - 1] += [(ring_out, 3), (first_sums, 4)] if each > 1 else []

    def body(step, totals):
        at = step // each
        dx, dc = span - 1 - at // 2, 1 - at % 2
        inside = pl.ds(pl.multiple_of(step % each * chunk, chunk), chunk)
        first = pl.multiple_of((dc * span + dx) * rows + step % each * chunk, chunk)
        here = pl.ds(first, chunk)
        term = lax.dot_general(
            grad_qkv[:, here], w_qkv[...], (((0,), (1,)), ((), ())), preferred_element_type=F32
        )
        back[dc, dx, inside, :] = term.astype(BF16)
        normed, _ = layer_norm(tokens[here, :].astype(F32))
        shift = jnp.sum(term, axis=0, keepdims=True)
        scale = jnp.sum(term * normed, axis=0, keepdims=True)
        other = dc.astype(F32)
        for place in range(blocks):
            done_dx, done_dc = span - 1 - place // 2, 1 - place % 2

            @pl.when(step == (place + 1) * each - 1)
            def _():
                if done_dc:
                    sum_back.cross(done_dx).start()
                elif done_dx:
                    sum_back.fold(done_dx)

        for when, todo in planned.items():

            @pl.when(step == when)
            def _():
                for job, event in todo:
                    job.run(event)

        own_part, other_part = 1.0 - other, other
        return (
            totals[0] + own_part * shift,
            totals[1] + own_part * scale,
            totals[2] + other_part * shift,
            totals[3] + other_part * scale,
        )

    zero = jnp.zeros((1, width), F32)
    totals = lax.fori_loop(0, far, body, (zero,) * 4)
    first_sums.run(1)
    ring_out.run(1)
    for low in range(0, width, tile):
        cut = slice(low, low + tile)
        g_qkv[cut, :] = lax.dot_general(
            hidden[:, cut], grad_qkv[...], (((0,), (1,)), ((), ())), preferred_element_type=F32
        ).astype(BF16)
    ring.run(0)
    ring.run(1)
    gate = jnp.zeros((1, width), F32)
    part = min(128, rows)
    for low in range(0, rows, part):
        here = slice(low, low + part)
        two = branch[here, :] + own_rows[7:8, :]
        output[here, :] = (midway[here, :] + own_rows[5:6, :] * two).astype(BF16)
        gate = gate + jnp.sum(grad_out[here, :].astype(F32) * two, axis=0, keepdims=True)
    features = grad_qkv.shape[0] // 3
    ones = jnp.ones((8, grad_qkv.shape[1]), BF16)
    head_sums = lax.dot_general(
        ones, grad_qkv[...], (((1,), (1,)), ((), ())), preferred_element_type=F32
    )
    first_sums.run(2)
    ring_out.run(2)
    totals = lax.fori_loop(far, blocks * each, body, totals)
    late[...] = jnp.zeros_like(late)
    for clip in range(clips):
        for part in range(2):
            at = 2 * clip + part
            late[at : at + 1, :] = (
                own_rows[8 + clip : 9 + clip, :] * totals[part]
                + own_rows[8 + clips + clip : 9 + clips + clip, :] * totals[2 + part]
            )
    for clip in range(clips):
        late[2 * clips + clip : 2 * clips + clip + 1, :] = own_rows[8 + clip : 9 + clip, :] * gate
    spread[...] = jnp.zeros_like(spread)
    spread[0:1, :features] = head_sums[0:1, :features]
    spread[1:2, :features] = head_sums[0:1, 2 * features :]
    late[3 * clips : 3 * clips + 2, :] = pltpu.roll(
        spread[...], where.member * features, 1
    )[0:2]
    sums.run(0)

    def own_tokens():
        sum_back.finish()
        part = min(128, rows)
        for low in range(0, rows, part):
            here = slice(low, low + part)
            normed, inv_std = layer_norm(tokens[here, :].astype(F32))
            grad = grad_hidden[here, :] * (1.0 + own_rows[1:2, :])
            tokens_grad[here, :] = (
                grad_mid[here, :] + norm_back(grad, normed, inv_std)
            ).astype(BF16)

    ran = [item for todo in planned.values() for item in todo]
    todo = [(ring_out, at) for at in range(3, ring_out.events)]
    todo += [(first_sums, at) for at in range(3, first_sums.events)]
    todo = [item for item in todo if item not in ran]
    late_todo = list(range(1, sums.events - 1))
    for event in range(2 + len(planned), ring.events):
        ring.run(event)
        if todo:
            job, at = todo.pop(0)
            job.run(at)
        if event % 2 and late_todo:
            sums.run(late_todo.pop(0))
        if event == ring.events - 3:
            own_tokens()
    for job, at in todo:
        job.run(at)
    for at in late_todo:
        sums.run(at)
    sums.run(sums.events - 1)


def back_to_tokens(
    grad_qkv,
    hidden,
    tokens,
    w_qkv,
    grad_mid,
    out_terms,
    early,
    own_rows,
    midway,
    branch,
    grad_out,
    clips,
    sizes,
    call_id,
):
    size, _, span = sizes
    count, width = tokens.shape
    rows = count // (2 * span)
    features = grad_qkv.shape[0]
    block_rows = width // size
    late = (3 * clips + 2 + (-3 * clips - 2) % 8, width)
    shape = jax.ShapeDtypeStruct
    return pl.pallas_call(
        functools.partial(last_kernel, sizes, min(256, rows), 384, clips),
        out_shape=[
            shape((rows, width), BF16),
            shape((rows, width), BF16),
            shape((block_rows, features), BF16),
            shape((block_rows, width), BF16),
            shape(early.shape, F32),
            shape(late, F32),
        ],
        in_specs=[CORE] * 11,
        out_specs=[CORE] * 6,
        scratch_shapes=[
            pltpu.VMEM((2, span, rows, width), BF16),
            pltpu.VMEM((width, features), BF16),
            pltpu.VMEM(late, F32),
            pltpu.VMEM((rows, width), F32),
            pltpu.VMEM((8, width), F32),
        ]
        + GroupSum.scratch(span, rows, width)
        + RingSum.scratch(size, block_rows, features)
        + AllSum.scratch(sizes, early.shape)
        + AllSum.scratch(sizes, late)
        + RingSumSplit.scratch(size, block_rows, width),
        compiler_params=pltpu.CompilerParams(
            collective_id=call_id, has_side_effects=True, vmem_limit_bytes=61 * MIB
        ),
        name="back_to_tokens",
    )(
        grad_qkv,
        hidden,
        tokens,
        w_qkv,
        grad_mid,
        out_terms,
        early,
        own_rows,
        midway,
        branch,
        grad_out,
    )


def final_kernel(sizes, *refs):
    where = Where(sizes)
    ins, outs, scratch = take(refs, (4, 4, len(refs) - 8))
    summed, share_qkv, share_up, share_out = outs
    got, own = scratch[:3], take(scratch[3:], (4, 3, 3, 3))
    sums = AllSum(where, sizes, ins[0], summed, own[0])
    greet(where.group_peers() + sums.peers)
    swaps = [
        GroupSwap(
            where,
            lambda dc, dx, source=ins[at + 1]: source.at[where.peer_member(dc, dx)],
            lambda dc, dx, target=got[at]: target.at[where.member],
            own[at + 1],
        )
        for at in range(3)
    ]
    sums.run(0)
    for swap in swaps:
        swap.run(0)
    for event in range(1, sums.events):
        sums.run(event)
    group, _, three = got[0].shape
    features = three // 3
    swaps[0].run(1)
    for member in range(group):
        piece = got[0][member].astype(F32)
        for part in range(3):
            low = (part * group + member) * features
            share_qkv[:, low : low + features] = piece[:, part * features : (part + 1) * features]
    swaps[1].run(1)
    units = got[1].shape[2] // where.size
    for member in range(group):
        piece = got[1][member].astype(F32)
        for ring in range(where.size):
            low = (ring * group + member) * units
            share_up[:, low : low + units] = piece[:, ring * units : (ring + 1) * units]
    swaps[2].run(1)
    total = got[2][0].astype(F32)
    for member in range(1, group):
        total = total + got[2][member].astype(F32)
    share_out[...] = total


def final(block, pieces, sizes, call_id):
    group, share, _ = pieces[0].shape
    shape = jax.ShapeDtypeStruct
    return pl.pallas_call(
        functools.partial(final_kernel, sizes),
        out_shape=[
            shape(block.shape, F32),
            shape((share, group * pieces[0].shape[2]), F32),
            shape((share, group * pieces[1].shape[2]), F32),
            shape((share, pieces[2].shape[2]), F32),
        ],
        in_specs=[CORE] * 4,
        out_specs=[CORE] * 4,
        scratch_shapes=[pltpu.VMEM(item.shape, BF16) for item in pieces]
        + AllSum.scratch(sizes, block.shape)
        + GroupSwap.scratch(sizes[2]) * 3,
        compiler_params=pltpu.CompilerParams(
            collective_id=call_id, has_side_effects=True, vmem_limit_bytes=32 * MIB
        ),
        name="final",
    )(block, *pieces)


def per_device(
    tokens,
    cotangent,
    clip_embed,
    timesteps,
    frame_clip,
    ada_weight,
    ada_bias,
    qkv_weight,
    query_bias,
    value_bias,
    out_weight,
    out_bias,
    up_weight,
    up_bias,
    down_weight,
    down_bias,
):
    ring_size, patch_size = lax.axis_size("ring"), lax.axis_size("patch")
    sizes = (ring_size, 2, patch_size)
    group = 2 * patch_size
    device_count = ring_size * group
    ring, core, patch = (lax.axis_index(name) for name in ("ring", "core", "patch"))
    member = core * patch_size + patch
    device = ring * group + member
    rows, width = tokens.shape[1:]
    tokens, cotangent = tokens[0], cotangent[0]
    patches = patch_size * rows
    clips = clip_embed.shape[0]
    hidden = up_weight.shape[1]
    share = width // device_count
    heads = HEADS // group
    head_width = heads * HEAD_DIM
    units = hidden // group
    mine = jnp.arange(group) == member
    mine_of_all = jnp.arange(device_count) == device

    condition = clip_embed + sinusoid(timesteps, width)
    silu_cond, silu_back = jax.vjp(jax.nn.silu, condition)
    silu_low = silu_cond.astype(BF16)
    silu_part = lax.dynamic_slice_in_dim(silu_low, device * share, share, 1)
    small = jnp.concatenate(
        [query_bias, value_bias, out_bias, down_bias, up_bias, ada_bias]
    ).astype(F32)[None, :]

    tokens_all, w_qkv, out_block, up_block, _, hidden_one, projected, own_rows, b_up = entry(
        tokens,
        qkv_weight,
        up_weight,
        out_weight,
        silu_part,
        ada_weight,
        small,
        frame_clip,
        sizes,
        1,
    )
    w_qkv = w_qkv.reshape(width, 3 * head_width)
    gate_two = own_rows[5]
    qkv = projected.reshape(3 * heads, HEAD_DIM, 2 * patches)
    grad_out = cotangent.astype(F32)
    grad_branch_two = (gate_two * grad_out).astype(BF16)
    attended_t, lse, w_up, gb_two_all = attention(
        qkv, up_block, grad_branch_two, patches, sizes, 2
    )
    w_up = w_up.reshape(width, units)

    attended, branch_one, midway, hidden_two_all, w_out, w_down = middle(
        attended_t.reshape(head_width, 2 * patches),
        out_block,
        tokens,
        own_rows,
        down_weight,
        sizes,
        3,
    )
    attended = attended.reshape(width, rows)
    w_out = w_out.reshape(width, width)
    w_down = w_down.reshape(units, width)

    branch_half, grad_hidden_two, g_up, share_down, g_up_b = feed(
        hidden_two_all.reshape(2 * patches, width),
        gb_two_all.reshape(2 * patches, width),
        w_up,
        w_down,
        b_up,
        sizes,
        4,
    )
    g_up_b = g_up_b[0]
    g_down_b = jnp.sum(grad_branch_two.astype(F32), axis=0)
    block_rows = width // ring_size
    grad_midway, grad_mix, g_out, own_sums = back_to_heads(
        grad_hidden_two,
        midway,
        branch_one,
        cotangent,
        w_out,
        attended,
        own_rows,
        sizes,
        5,
    )
    grad_shift_two, grad_scale_two, grad_gate_one, g_out_b = (own_sums[at] for at in range(4))

    grad_projected, sum_up, branch_two = attention_back(
        qkv,
        grad_mix.reshape(heads, HEAD_DIM, 2 * patches),
        lse,
        g_up.reshape(ring_size, block_rows, units),
        branch_half,
        patches,
        sizes,
        6,
    )
    grad_projected = grad_projected.reshape(3 * head_width, 2 * patches)

    frame_grads = jnp.stack([grad_gate_one, grad_shift_two, grad_scale_two])
    early = jnp.concatenate(
        [
            (own_rows[8 : 8 + clips, None] * frame_grads[None]).reshape(3 * clips, width),
            jnp.stack([g_out_b, g_down_b]),
            jnp.where(mine[None, :, None], g_up_b.reshape(ring_size, 1, -1), 0.0).reshape(
                -1, width
            ),
        ]
    )
    early = jnp.pad(early, ((0, -early.shape[0] % 8), (0, 0)))
    tokens_grad, output, sum_qkv, sum_out, early_sum, late_sum = back_to_tokens(
        grad_projected,
        hidden_one,
        tokens_all.reshape(2 * patches, width),
        w_qkv,
        grad_midway,
        g_out.reshape(ring_size, block_rows, width),
        early,
        own_rows,
        midway,
        branch_two,
        cotangent,
        clips,
        sizes,
        7,
    )
    first = late_sum[: 2 * clips].reshape(clips, 2 * width)
    second = early_sum[: 3 * clips].reshape(clips, 3 * width)
    third = late_sum[2 * clips : 3 * clips]
    mod_low = jnp.concatenate([first, second, third], axis=1).astype(BF16)
    query_b_all, value_b_all = (late_sum[3 * clips + at] for at in range(2))
    out_b_all, down_b_all = (early_sum[3 * clips + at] for at in range(2))
    up_b_all = early_sum[3 * clips + 2 :].reshape(-1)[:hidden]

    def own(vector):
        length = vector.shape[0] // device_count
        return lax.dynamic_slice_in_dim(vector, device * length, length, 0)

    ada_bias_grad = own(jnp.sum(mod_low.astype(F32), axis=0))
    ada_weight_grad = lax.dot_general(
        silu_part, mod_low, (((0,), (0,)), ((), ())), preferred_element_type=F32
    )
    grad_silu_part = lax.dot_general(
        mod_low, ada_weight, (((1,), (1,)), ((), ())), preferred_element_type=F32
    )
    spread = jnp.where(mine_of_all[None, :, None], grad_silu_part[:, None, :], 0.0).reshape(-1)
    grad_silu, share_qkv, share_up, share_out = final(
        flat_block(spread),
        [item.reshape(group, share, -1) for item in (sum_qkv, sum_up, sum_out)],
        sizes,
        8,
    )
    grad_silu = grad_silu.reshape(-1)[: clips * width].reshape(clips, width)
    clip_grad = silu_back(grad_silu)[0]

    return (
        output[None],
        tokens_grad[None],
        clip_grad,
        ada_weight_grad,
        ada_bias_grad,
        share_qkv,
        own(query_b_all),
        own(value_b_all),
        share_out,
        own(out_b_all),
        share_up,
        own(up_b_all),
        share_down,
        own(down_b_all),
    )


def solution(mesh):
    frames, patch = mesh.shape["frames"], mesh.shape["patch"]
    inner = Mesh(mesh.devices.reshape(frames // 2, 2, patch), ("ring", "core", "patch"))
    every = ("ring", "core", "patch")
    tokens = P(("ring", "core"), "patch", None)
    matrix = P(every, None)
    vector = P(every)
    return jax.shard_map(
        per_device,
        mesh=inner,
        in_specs=(
            tokens,
            tokens,
            P(),
            P(),
            P(("ring", "core")),
            matrix,
            vector,
            matrix,
            vector,
            vector,
            matrix,
            vector,
            matrix,
            vector,
            matrix,
            vector,
        ),
        out_specs=(
            tokens,
            tokens,
            P(),
            matrix,
            vector,
            matrix,
            vector,
            vector,
            matrix,
            vector,
            matrix,
            vector,
            matrix,
            vector,
        ),
        check_vma=False,
    )
```
